32 devices in a mesh: grp: 2 (over y), tile: 8 (over z, x), gene: 2 (over core).
Axes of the slice: x: 2, y: 2, z: 4, core: 2. Of those that a mesh axis runs over, the one named last changes fastest.
Arguments:
- counts: int32 [4096, 8192], P(('grp', 'tile'), 'gene'), parts along dimension 0, may hold values from 0 to 86, as said below
- cell_factor: float32 [32, 4096], P(None, ('grp', 'tile')), parts along dimension 1, may hold values from 0.05 to 1
- gene_factor: bfloat16 [32, 16384], P(None, ('grp', 'gene')), parts along dimension 1, may hold values from 0.049804688 to 1
- tissue: int32 [4096], P(('grp', 'tile')), parts along dimension 0, may hold values from 0 to 1, as said below
- neighbours: int32 [8, 4096], P(None, ('grp', 'tile')), parts along dimension 1, may hold values from 0 to 2047, as said below
Outputs:
- new_cells: float32 [32, 4096], P(None, ('grp', 'tile')), parts along dimension 1
- new_genes: bfloat16 [32, 16384], P(None, ('grp', 'gene')), parts along dimension 1
The draws below stay inside these ranges and needn't reach their ends.
There are 2 independent parts, one for each index of `grp`. The reference program is written for one: setup_inputs(seed, part) draws one part's arguments, and reference() takes and returns one part's arrays. A program takes and returns all parts, laid end to end along the dimension named above; each array names one. Nothing has to cross between parts.
Inputs may be any that keep to these rules, and one draw needn't show every extreme that they name: `counts`: counts of each cell and gene. Share of tissue differs among tiles. `neighbours`: every neighbour index lies within 32 positions of its cell in cell order, and that distance is reached.
All inputs are finite; a program needn't handle non-finite values.
Results may differ from the reference program's by a relative error of at most 0.00165.
Values may be sent and summed in bfloat16 or wider, within the bound.
No kernel may reach another device: no remote copies, remote signals or barrier semaphores. Data moves between devices by JAX's collectives and lax.ppermute only.
A program may use at most 64 MiB of HBM per device.

```python
import math
import jax
import jax.numpy as jnp
from jax import lax

RANK = 32
GENES = 8192
C_DEV = 256
BORDER = 32
NEIGH = 8
PASSES = 2
CELLS = 2048
N_TILE = 8


def draw_counts(key, part):
    pair_key = jax.random.fold_in(key, 31)
    base_key = jax.random.fold_in(key, 32)
    extra_key = jax.random.fold_in(key, 33)
    tiles = CELLS // C_DEV
    block = GENES // tiles
    paired = jax.random.permutation(pair_key, tiles)
    target = paired[jnp.arange(CELLS, dtype=jnp.int32) // C_DEV]
    gene_block = jnp.arange(GENES, dtype=jnp.int32) // block
    hit = target[:, None] == gene_block[None, :]
    base = jax.random.randint(base_key, (CELLS, GENES), 0, 8)
    extra = jax.random.randint(extra_key, (CELLS, GENES), 48, 80)
    return (base + jnp.where(hit, extra, 0)).astype(jnp.int32)


def draw_tissue(key, part):
    level_key = jax.random.fold_in(key, 11)
    cell_key = jax.random.fold_in(key, 12)
    tiles = CELLS // C_DEV
    levels = jax.random.randint(level_key, (tiles,), 20, 96)
    per_cell = jnp.repeat(levels, C_DEV, total_repeat_length=CELLS)
    rolls = jax.random.randint(cell_key, (CELLS,), 0, 100)
    return (rolls < per_cell).astype(jnp.int32)


def draw_neighbours(key, part):
    step_key = jax.random.fold_in(key, 21)
    sign_key = jax.random.fold_in(key, 22)
    offsets = jax.random.randint(step_key, (NEIGH, CELLS), -BORDER, BORDER + 1)
    signs = 2 * jax.random.randint(sign_key, (1, CELLS), 0, 2) - 1
    first = signs * BORDER
    offsets = jnp.concatenate([first, offsets[1:]], axis=0)
    position = jnp.arange(CELLS, dtype=jnp.int32)[None, :]
    return jnp.clip(position + offsets, 0, CELLS - 1).astype(jnp.int32)


def block_levels(stream_key, dims, cuts, smallest, top_value):
    gain = 1.0
    for axis_at, parts in cuts:
        steps = jax.random.uniform(jax.random.fold_in(jax.random.fold_in(stream_key, 6), axis_at), (parts,), jnp.float32, smallest / len(cuts), top_value / len(cuts))
        gain = gain * jnp.repeat(jnp.exp(steps), dims[axis_at] // parts).reshape((-1,) + (1,) * (len(dims) - 1 - axis_at))
    return gain


def setup_inputs(seed: int = 0, part: int = 0) -> dict:
    key_list = jax.random.split(jax.random.key(seed), 6)
    part_keys = jax.random.split(jax.random.fold_in(key_list[5], part), 6)
    counts = draw_counts(jax.random.fold_in(jax.random.fold_in(key_list[5], part), 71), part)
    cell_factor = jnp.clip(jnp.exp(math.log(1.0) - 2.9957323 * jax.random.uniform(part_keys[1], (RANK, CELLS), jnp.float32) ** block_levels(part_keys[1], (RANK, CELLS), ((1, 8),), -0.2, 0.2)), 0.05, 1.0)
    gene_factor = jnp.clip(jnp.exp(math.log(1.0) - 2.9996462 * jax.random.uniform(part_keys[2], (RANK, GENES), jnp.float32) ** block_levels(part_keys[2], (RANK, GENES), ((1, 2),), -0.2, 0.2)), 0.049804688, 1.0).astype(jnp.bfloat16)
    tissue = draw_tissue(jax.random.fold_in(jax.random.fold_in(key_list[5], part), 71), part)
    neighbours = draw_neighbours(jax.random.fold_in(jax.random.fold_in(key_list[5], part), 71), part)
    return {"counts": counts, "cell_factor": cell_factor, "gene_factor": gene_factor, "tissue": tissue, "neighbours": neighbours}


smooth_weight = 0.5


def smooth(updated, tissue, neighbours):
    maskf = tissue.astype(jnp.float32)
    flat = neighbours.reshape(-1)
    count = neighbours.shape[0]
    near_mask = maskf[flat].reshape(count, CELLS)
    gathered = jnp.take(updated, flat, axis=1).reshape(RANK, count, CELLS)
    near = jnp.sum(gathered * near_mask[None], axis=1) / jnp.maximum(jnp.sum(near_mask, axis=0), 1.0)
    return jnp.where(tissue[None] > 0, (1.0 - smooth_weight) * updated + smooth_weight * near, updated)


def reference(counts, cell_factor, gene_factor, tissue, neighbours):
    hfull = gene_factor.astype(jnp.float32)
    maskf = tissue.astype(jnp.float32)
    gsum = jnp.sum(hfull, axis=1)
    blocks = jnp.arange(N_TILE, dtype=jnp.int32)

    def cell_numer(cells):
        def single(index):
            start = (index * C_DEV).astype(jnp.int32)
            wblock = lax.dynamic_slice_in_dim(cells, start, C_DEV, 1)
            xblock = lax.dynamic_slice_in_dim(counts, start, C_DEV, 0).astype(jnp.float32)
            product = lax.dot_general(wblock, hfull, (((0,), (0,)), ((), ())), precision=lax.Precision.HIGHEST)
            ratio = xblock / product
            return lax.dot_general(hfull, ratio, (((1,), (1,)), ((), ())), precision=lax.Precision.HIGHEST)
        pieces = lax.map(single, blocks)
        return jnp.transpose(pieces, (1, 0, 2)).reshape(RANK, CELLS)

    cells = cell_factor
    for step in range(PASSES):
        numer = cell_numer(cells)
        updated = jnp.where(tissue[None] > 0, cells * numer / gsum[:, None], cells)
        cells = smooth(updated, tissue, neighbours)

    def accumulate(total, index):
        start = (index * C_DEV).astype(jnp.int32)
        wblock = lax.dynamic_slice_in_dim(cells, start, C_DEV, 1)
        xblock = lax.dynamic_slice_in_dim(counts, start, C_DEV, 0).astype(jnp.float32)
        mblock = lax.dynamic_slice_in_dim(maskf, start, C_DEV, 0)
        product = lax.dot_general(wblock, hfull, (((0,), (0,)), ((), ())), precision=lax.Precision.HIGHEST)
        ratio = mblock[:, None] * xblock / product
        return total + jnp.dot(wblock, ratio, precision=lax.Precision.HIGHEST), None

    hnum, unused = lax.scan(accumulate, jnp.zeros((RANK, GENES), jnp.float32), blocks)
    hden = jnp.sum(cells * maskf[None], axis=1)
    new_genes = (hfull * hnum / hden[:, None]).astype(jnp.bfloat16)
    return cells, new_genes
```

```python
import functools

import jax
import jax.numpy as jnp
from jax import lax
from jax.experimental import pallas as pl
from jax.experimental.pallas import tpu as pltpu
from jax.sharding import PartitionSpec as P

BORDER = 32
LANES = 128
FLAG_ROWS = 8
smooth_weight = 0.5
VMEM_BYTES = 24 * 1024 * 1024


def split(values):
    high = values.astype(jnp.bfloat16)
    low = (values - high.astype(jnp.float32)).astype(jnp.bfloat16)
    return high, low


def chunk_of(genes):
    for size in (512, 256, 128):
        if genes % size == 0:
            return size
    return genes


def factor_columns(cells):
    return jnp.concatenate(split(cells.T), axis=1)


def numerator(columns, gene_ref, counts_at, part_ref):
    rank, genes = gene_ref.shape
    size = chunk_of(genes)
    total = jnp.zeros((rank, columns.shape[0]), jnp.float32)
    for start in range(0, genes, size):
        hf = gene_ref[:, start : start + size]
        product = jnp.dot(
            columns, jnp.concatenate([hf, hf], axis=0), preferred_element_type=jnp.float32
        )
        ratio = counts_at(start, size) * pl.reciprocal(product, approx=True)
        total += lax.dot_general(
            hf,
            ratio.astype(jnp.bfloat16),
            (((1,), (1,)), ((), ())),
            preferred_element_type=jnp.float32,
        )
    part_ref[:, : columns.shape[0]] = total


def first_kernel(
    tiles, place_ref, counts_ref, cells_ref, gene_ref, neigh_ref,
    part_ref, kept_ref, pick_ref, landed, sems,
):
    rank, genes = gene_ref.shape
    width = cells_ref.shape[1]
    size = chunk_of(genes)
    copies = [
        pltpu.make_async_copy(
            counts_ref.at[:, pl.ds(at, size)], landed.at[:, pl.ds(at, size)], sems.at[i]
        )
        for i, at in enumerate(range(0, genes, size))
    ]
    for copy in copies:
        copy.start()
    here = place_ref[0]
    neigh = neigh_ref[...] - here * width
    for at in range(0, width, LANES):
        where = at + lax.broadcasted_iota(jnp.int32, (LANES, width), 0)
        found = jnp.zeros((LANES, width), jnp.float32)
        for j in range(neigh.shape[0]):
            found += (neigh[j : j + 1] == where).astype(jnp.float32)
        pick_ref[at : at + LANES] = found.astype(jnp.bfloat16)
    row = lax.broadcasted_iota(jnp.int32, (LANES, width), 0)
    slot = row % (2 * BORDER)
    beside = jnp.where(row < 2 * BORDER, place_ref[1], place_ref[2])
    where = (beside - here) * width + slot + jnp.where(slot < BORDER, 0, width - 2 * BORDER)
    found = jnp.zeros((LANES, width), jnp.float32)
    for j in range(neigh.shape[0]):
        found += (neigh[j : j + 1] == where).astype(jnp.float32)
    pick_ref[width:] = jnp.where(beside < 0, 0.0, found).astype(jnp.bfloat16)

    gsum = jnp.sum(gene_ref[...].astype(jnp.float32), axis=1, keepdims=True)
    part_ref[:, width:] = jnp.broadcast_to(gsum, (rank, LANES))

    def counts_at(start, size):
        copies[start // size].wait()
        values = landed[:, start : start + size].astype(jnp.float32)
        kept_ref[:, start : start + size] = values.astype(jnp.bfloat16)
        return values

    numerator(factor_columns(cells_ref[...]), gene_ref, counts_at, part_ref)


def update_kernel(part_ref, other_ref, cells_ref, tissue_ref, updated_ref, edges_ref):
    rank, width = cells_ref.shape
    flags = tissue_ref[...] > 0
    numer = part_ref[:, :width] + other_ref[:, :width]
    gsum = part_ref[:, width:] + other_ref[:, width:]
    cells = cells_ref[...]
    updated = jnp.where(flags, cells * numer / gsum[:, :1], cells)
    updated_ref[...] = updated
    masked = jnp.where(flags, updated, 0.0)
    row = jnp.broadcast_to(flags.astype(jnp.float32), (FLAG_ROWS, width))
    both = jnp.concatenate([masked, row], axis=0)
    edges_ref[:, :BORDER] = both[:, :BORDER]
    edges_ref[:, BORDER : 2 * BORDER] = both[:, width - BORDER :]
    edges_ref[:, 2 * BORDER :] = jnp.zeros_like(edges_ref[:, 2 * BORDER :])


def smoothed(updated_ref, tissue_ref, first_ref, second_ref, pick_ref):
    rank, width = updated_ref.shape
    updated = updated_ref[...]
    flags = tissue_ref[...] > 0
    masked = jnp.where(flags, updated, 0.0)
    row = jnp.broadcast_to(flags.astype(jnp.float32), (FLAG_ROWS, width))
    own = jnp.concatenate([masked, row], axis=0)
    sides = jnp.concatenate(
        [first_ref[:, : 2 * BORDER], second_ref[:, : 2 * BORDER]], axis=1
    )
    near = jnp.zeros((rank + FLAG_ROWS, width), jnp.float32)
    for values, pick in ((own, pick_ref[:width]), (sides, pick_ref[width:])):
        for part in split(values):
            near += jnp.dot(part, pick, preferred_element_type=jnp.float32)
    mean = near[:rank] / jnp.maximum(near[rank : rank + 1], 1.0)
    return jnp.where(
        flags, (1.0 - smooth_weight) * updated + smooth_weight * mean, updated
    ), flags


def next_kernel(
    updated_ref, tissue_ref, first_ref, second_ref, pick_ref, kept_ref, gene_ref,
    cells_ref, part_ref,
):
    cells, flags = smoothed(updated_ref, tissue_ref, first_ref, second_ref, pick_ref)
    cells_ref[...] = cells

    def counts_at(start, size):
        return kept_ref[:, start : start + size].astype(jnp.float32)

    numerator(factor_columns(cells), gene_ref, counts_at, part_ref)


def last_kernel(
    updated_ref, tissue_ref, first_ref, second_ref, pick_ref, kept_ref, gene_ref,
    cells_ref, hnum_ref, hden_ref,
):
    rank, genes = gene_ref.shape
    size = chunk_of(genes)
    cells, flags = smoothed(updated_ref, tissue_ref, first_ref, second_ref, pick_ref)
    cells_ref[...] = cells
    masked = jnp.where(flags, cells, 0.0)
    hden_ref[...] = jnp.broadcast_to(jnp.sum(masked, axis=1, keepdims=True), hden_ref.shape)
    columns = factor_columns(cells)
    high, low = split(masked)
    rows = jnp.concatenate([high, low], axis=0)
    for start in range(0, genes, size):
        hf = gene_ref[:, start : start + size]
        product = jnp.dot(
            columns, jnp.concatenate([hf, hf], axis=0), preferred_element_type=jnp.float32
        )
        counts = kept_ref[:, start : start + size].astype(jnp.float32)
        ratio = (counts * pl.reciprocal(product, approx=True)).astype(jnp.bfloat16)
        both = jnp.dot(rows, ratio, preferred_element_type=jnp.float32)
        hnum_ref[:, start : start + size] = both[:rank] + both[rank:]


def call(kernel, outs, scratch=(), specs=None, limit=VMEM_BYTES):
    whole = pl.BlockSpec(memory_space=pltpu.VMEM)
    return lambda *args: pl.pallas_call(
        kernel,
        out_shape=outs,
        in_specs=specs or [whole] * len(args),
        out_specs=jax.tree.map(lambda _: whole, outs),
        scratch_shapes=list(scratch),
        compiler_params=pltpu.CompilerParams(vmem_limit_bytes=limit),
    )(*args)


def beside(tiles, genes, offset):
    pairs = []
    paired = set()
    for low in range(offset, tiles - 1, 2):
        paired |= {low, low + 1}
        for gene in range(genes):
            pairs.append((low * genes + gene, (low + 1) * genes + gene))
            pairs.append(((low + 1) * genes + gene, low * genes + gene))
    for tile in range(tiles):
        if tile not in paired:
            for gene in range(genes):
                pairs.append((tile * genes + gene, tile * genes + (gene + 1) % genes))
    return pairs


def on_device(counts, cell_factor, gene_factor, tissue, neighbours):
    rank, width = cell_factor.shape
    genes = gene_factor.shape[1]
    tiles, halves = lax.axis_size("tile"), lax.axis_size("gene")
    tile = lax.axis_index("tile")
    flag_row = tissue[None]
    shape = jax.ShapeDtypeStruct

    def partner(offset):
        other = jnp.where((tile - offset) % 2 == 0, tile + 1, tile - 1)
        return jnp.where((other >= 0) & (other < tiles), other, -1)

    place = jnp.stack([tile, partner(0), partner(1)]).astype(jnp.int32)
    factor = shape((rank, width), jnp.float32)
    part_shape = shape((rank, width + LANES), jnp.float32)
    whole = pl.BlockSpec(memory_space=pltpu.VMEM)
    chunks = genes // chunk_of(genes)
    part, kept, pick = call(
        functools.partial(first_kernel, tiles),
        (
            part_shape,
            shape((counts.shape[0], genes), jnp.bfloat16),
            shape((width + LANES, width), jnp.bfloat16),
        ),
        scratch=[pltpu.VMEM(counts.shape, jnp.int32), pltpu.SemaphoreType.DMA((chunks,))],
        specs=[pl.BlockSpec(memory_space=pltpu.SMEM), pl.BlockSpec(memory_space=pl.ANY)]
        + [whole] * 3,
    )(place, counts, cell_factor, gene_factor, neighbours)
    gsum_part = part[:, width:]
    cells = cell_factor

    def update(part, cells):
        if halves == 2:
            other = lax.ppermute(part, "gene", [(0, 1), (1, 0)])
        else:
            other = lax.psum(part, "gene") - part
        updated, edges = call(
            update_kernel, (factor, shape((rank + FLAG_ROWS, LANES), jnp.float32))
        )(part, other, cells, flag_row)
        sides = [
            lax.ppermute(edges, ("tile", "gene"), beside(tiles, halves, offset))
            for offset in (0, 1)
        ]
        return updated, flag_row, *sides, pick, kept, gene_factor

    cells, numer = call(next_kernel, (factor, factor))(*update(part, cells))
    part = jnp.concatenate([numer, gsum_part], axis=1)
    cells, hnum, hden = call(
        last_kernel,
        (factor, shape((rank, genes), jnp.float32), shape((rank, LANES), jnp.float32)),
    )(*update(part, cells))

    share = genes // tiles
    sent = jnp.concatenate(
        [
            hnum.reshape(rank, tiles, share).transpose(1, 0, 2),
            jnp.broadcast_to(hden[None, :, :1], (tiles, rank, 1)),
        ],
        axis=2,
    )
    got = jnp.sum(lax.all_to_all(sent, "tile", 0, 0), axis=0)
    mine = lax.dynamic_slice_in_dim(gene_factor, tile * share, share, 1).astype(jnp.float32)
    fresh = (mine * got[:, :share] / got[:, share:]).astype(jnp.bfloat16)
    every = lax.all_to_all(jnp.broadcast_to(fresh[None], (tiles, rank, share)), "tile", 0, 0)
    return cells, every.transpose(1, 0, 2).reshape(rank, genes)


def solution(mesh):
    return jax.shard_map(
        on_device,
        mesh=mesh,
        in_specs=(
            P(("grp", "tile"), "gene"),
            P(None, ("grp", "tile")),
            P(None, ("grp", "gene")),
            P(("grp", "tile")),
            P(None, ("grp", "tile")),
        ),
        out_specs=(P(None, ("grp", "tile")), P(None, ("grp", "gene"))),
        check_vma=False,
    )
```

```python
import jax
import jax.numpy as jnp
from jax import lax
from jax.experimental import pallas as pl
from jax.experimental.pallas import tpu as pltpu
from jax.sharding import PartitionSpec as P

BORDER = 32
LANES = 128
FLAG_ROWS = 8
STAT_ROWS = 16
FULL = 32767.0
smooth_weight = 0.5
VMEM_BYTES = 24 * 1024 * 1024


def split(values):
    high = values.astype(jnp.bfloat16)
    low = (values - high.astype(jnp.float32)).astype(jnp.bfloat16)
    return high, low


def chunk_of(genes):
    for size in (512, 256, 128):
        if genes % size == 0:
            return size
    return genes


def factor_columns(cells):
    return jnp.concatenate(split(cells.T), axis=1)


def numerator(columns, gene_ref, counts_at, part_ref):
    rank, genes = gene_ref.shape
    size = chunk_of(genes)
    total = jnp.zeros((rank, columns.shape[0]), jnp.float32)
    for start in range(0, genes, size):
        hf = gene_ref[:, start : start + size]
        product = jnp.dot(
            columns, jnp.concatenate([hf, hf], axis=0), preferred_element_type=jnp.float32
        )
        ratio = counts_at(start, size) * pl.reciprocal(product, approx=True)
        total += lax.dot_general(
            hf,
            ratio.astype(jnp.bfloat16),
            (((1,), (1,)), ((), ())),
            preferred_element_type=jnp.float32,
        )
    part_ref[:, : columns.shape[0]] = total


def partner(tile, tiles, offset):
    other = jnp.where((tile + offset) % 2 == 0, tile + 1, tile - 1)
    return jnp.where((other >= 0) & (other < tiles), other, -1)


def first_kernel(
    counts_ref, cells_in, gene_in, neigh_in,
    part_ref, kept_ref, pick_ref, cells_ref, gene_ref, neigh_ref, landed, sems, small_sems,
):
    rank, genes = gene_ref.shape
    width = cells_ref.shape[1]
    size = chunk_of(genes)
    small = [
        pltpu.make_async_copy(source, target, small_sems.at[i])
        for i, (source, target) in enumerate(
            ((neigh_in, neigh_ref), (cells_in, cells_ref), (gene_in, gene_ref))
        )
    ]
    copies = [
        pltpu.make_async_copy(
            counts_ref.at[:, pl.ds(at, size)], landed.at[:, pl.ds(at, size)], sems.at[i]
        )
        for i, at in enumerate(range(0, genes, size))
    ]
    for copy in small + copies:
        copy.start()
    tiles = lax.axis_size("tile")
    here = lax.axis_index("tile")
    sides = [partner(here, tiles, offset) for offset in (0, 1)]
    small[0].wait()
    neigh = neigh_ref[...] - here * width
    for at in range(0, width, LANES):
        where = at + lax.broadcasted_iota(jnp.int32, (LANES, width), 0)
        found = jnp.zeros((LANES, width), jnp.float32)
        for j in range(neigh.shape[0]):
            found += (neigh[j : j + 1] == where).astype(jnp.float32)
        pick_ref[at : at + LANES] = found.astype(jnp.bfloat16)
    row = lax.broadcasted_iota(jnp.int32, (LANES, width), 0)
    slot = row % (2 * BORDER)
    beside = jnp.where(row < 2 * BORDER, sides[0], sides[1])
    where = (beside - here) * width + slot + jnp.where(slot < BORDER, 0, width - 2 * BORDER)
    found = jnp.zeros((LANES, width), jnp.float32)
    for j in range(neigh.shape[0]):
        found += (neigh[j : j + 1] == where).astype(jnp.float32)
    pick_ref[width:] = jnp.where(beside < 0, 0.0, found).astype(jnp.bfloat16)

    small[1].wait()
    small[2].wait()
    gsum = jnp.sum(gene_ref[...].astype(jnp.float32), axis=1, keepdims=True)
    part_ref[:, width:] = jnp.broadcast_to(gsum, (rank, LANES))

    def counts_at(start, size):
        copies[start // size].wait()
        values = landed[:, start : start + size].astype(jnp.float32)
        kept_ref[:, start : start + size] = values.astype(jnp.bfloat16)
        return values

    numerator(factor_columns(cells_ref[...]), gene_ref, counts_at, part_ref)


def update_kernel(part_ref, other_ref, cells_ref, tissue_ref, updated_ref, edges_ref):
    rank, width = cells_ref.shape
    flags = tissue_ref[...] > 0
    numer = part_ref[:, :width] + other_ref[:, :width]
    gsum = part_ref[:, width:] + other_ref[:, width:]
    cells = cells_ref[...]
    updated = jnp.where(flags, cells * numer / gsum[:, :1], cells)
    updated_ref[...] = updated
    masked = jnp.where(flags, updated, 0.0)
    row = jnp.broadcast_to(flags.astype(jnp.float32), (FLAG_ROWS, width))
    both = jnp.concatenate([masked, row], axis=0)
    edges_ref[:, :BORDER] = both[:, :BORDER]
    edges_ref[:, BORDER : 2 * BORDER] = both[:, width - BORDER :]
    edges_ref[:, 2 * BORDER :] = jnp.zeros_like(edges_ref[:, 2 * BORDER :])


def smoothed(updated_ref, tissue_ref, first_ref, second_ref, pick_ref):
    rank, width = updated_ref.shape
    updated = updated_ref[...]
    flags = tissue_ref[...] > 0
    masked = jnp.where(flags, updated, 0.0)
    row = jnp.broadcast_to(flags.astype(jnp.float32), (FLAG_ROWS, width))
    own = jnp.concatenate([masked, row], axis=0)
    sides = jnp.concatenate(
        [first_ref[:, : 2 * BORDER], second_ref[:, : 2 * BORDER]], axis=1
    )
    near = jnp.zeros((rank + FLAG_ROWS, width), jnp.float32)
    for values, pick in ((own, pick_ref[:width]), (sides, pick_ref[width:])):
        for part in split(values):
            near += jnp.dot(part, pick, preferred_element_type=jnp.float32)
    mean = near[:rank] / jnp.maximum(near[rank : rank + 1], 1.0)
    return jnp.where(
        flags, (1.0 - smooth_weight) * updated + smooth_weight * mean, updated
    ), flags


def next_kernel(
    updated_ref, tissue_ref, first_ref, second_ref, pick_ref, kept_ref, gene_ref,
    cells_ref, part_ref,
):
    cells, flags = smoothed(updated_ref, tissue_ref, first_ref, second_ref, pick_ref)
    cells_ref[...] = cells

    def counts_at(start, size):
        return kept_ref[:, start : start + size].astype(jnp.float32)

    numerator(factor_columns(cells), gene_ref, counts_at, part_ref)


def gene_totals(columns, rows, kept_ref, gene_ref, start, size):
    rank = gene_ref.shape[0]
    hf = gene_ref[:, start : start + size]
    product = jnp.dot(
        columns, jnp.concatenate([hf, hf], axis=0), preferred_element_type=jnp.float32
    )
    counts = kept_ref[:, start : start + size].astype(jnp.float32)
    ratio = (counts * pl.reciprocal(product, approx=True)).astype(jnp.bfloat16)
    both = jnp.dot(rows, ratio, preferred_element_type=jnp.float32)
    return both[:rank] + both[rank:]


def last_kernel(
    updated_ref, tissue_ref, first_ref, second_ref, pick_ref, kept_ref, gene_ref,
    cells_ref, hnum_ref, hden_ref,
):
    rank, genes = gene_ref.shape
    size = chunk_of(genes)
    cells, flags = smoothed(updated_ref, tissue_ref, first_ref, second_ref, pick_ref)
    cells_ref[...] = cells
    masked = jnp.where(flags, cells, 0.0)
    hden_ref[...] = jnp.broadcast_to(jnp.sum(masked, axis=1, keepdims=True), hden_ref.shape)
    columns = factor_columns(cells)
    rows = jnp.concatenate(split(masked), axis=0)
    for start in range(0, genes, size):
        hnum_ref[:, start : start + size] = gene_totals(
            columns, rows, kept_ref, gene_ref, start, size
        )


def exponent(values):
    return jnp.ceil(jnp.log2(jnp.maximum(values, 1e-30)))


def whole_part(values):
    return (values + 0.5).astype(jnp.int32)


def coded_kernel(
    updated_ref, tissue_ref, first_ref, second_ref, pick_ref, kept_ref, gene_ref,
    cells_ref, sent_ref,
):
    rank, genes = gene_ref.shape
    tiles = sent_ref.shape[0]
    share = genes // tiles
    runs = share // LANES
    cells, flags = smoothed(updated_ref, tissue_ref, first_ref, second_ref, pick_ref)
    cells_ref[...] = cells
    masked = jnp.where(flags, cells, 0.0)
    columns = factor_columns(cells)
    rows = jnp.concatenate(split(masked), axis=0)
    hden = jnp.sum(masked, axis=1, keepdims=True)
    power = exponent(hden)
    scaled = hden * jnp.exp2(-power) * FULL
    high = jnp.floor(scaled)
    low = jnp.floor((scaled - high) * FULL)
    lane = lax.broadcasted_iota(jnp.int32, (rank, LANES), 1)
    stats = jnp.zeros((rank, LANES), jnp.float32)
    for at, value in enumerate((power, high, low)):
        stats = jnp.where(lane == tiles + at, value, stats)
    for tile in range(tiles):
        totals = gene_totals(columns, rows, kept_ref, gene_ref, tile * share, share)
        power = exponent(jnp.max(totals, axis=1, keepdims=True))
        stats = jnp.where(lane == tile, power, stats)
        coded = whole_part(totals * (jnp.exp2(-power) * FULL)).astype(jnp.int16)
        for run in range(runs):
            sent_ref[tile, run * rank : (run + 1) * rank] = coded[
                :, run * LANES : (run + 1) * LANES
            ]
    turned = jnp.concatenate([stats, jnp.zeros((LANES - rank, LANES), jnp.float32)], axis=0).T
    turned = turned[:STAT_ROWS].astype(jnp.int32).astype(jnp.int16)
    for tile in range(tiles):
        sent_ref[tile, runs * rank :] = turned


def fresh_kernel(got_ref, gene_ref, fresh_ref):
    tiles, _, share = fresh_ref.shape
    rank = gene_ref.shape[0]
    runs = share // LANES
    here = lax.axis_index("tile")

    def number(coded):
        return coded.astype(jnp.int32).astype(jnp.float32)

    stats = [number(got_ref[tile, runs * rank :]) for tile in range(tiles)]
    lane = lax.broadcasted_iota(jnp.int32, (rank, LANES), 1)
    scales = []
    hden = jnp.zeros((rank, 1), jnp.float32)
    group = LANES // STAT_ROWS
    for first in range(0, tiles, group):
        block = stats[first : first + group]
        short = LANES - len(block) * STAT_ROWS
        if short:
            block = block + [jnp.zeros((short, LANES), jnp.float32)]
        turned = jnp.concatenate(block, axis=0).T[:rank]
        for tile in range(first, min(first + group, tiles)):
            at = (tile - first) * STAT_ROWS
            power = jnp.sum(jnp.where(lane == at + here, turned, 0.0), axis=1, keepdims=True)
            scales.append(jnp.exp2(power) / FULL)
            at += tiles
            hden += (turned[:, at + 1 : at + 2] + turned[:, at + 2 : at + 3] / FULL) * (
                jnp.exp2(turned[:, at : at + 1]) / FULL
            )
    for run in range(runs):
        total = jnp.zeros((rank, LANES), jnp.float32)
        for tile in range(tiles):
            total += number(got_ref[tile, run * rank : (run + 1) * rank]) * scales[tile]
        place = pl.multiple_of(here * share + run * LANES, LANES)
        hf = gene_ref[:, pl.ds(place, LANES)].astype(jnp.float32)
        fresh = (hf * total / hden).astype(jnp.bfloat16)
        for tile in range(tiles):
            fresh_ref[tile, :, run * LANES : (run + 1) * LANES] = fresh


def spread_kernel(every_ref, out_ref):
    tiles, _, share = every_ref.shape
    for tile in range(tiles):
        out_ref[:, tile * share : (tile + 1) * share] = every_ref[tile]


def call(kernel, outs, scratch=(), specs=None, limit=VMEM_BYTES):
    whole = pl.BlockSpec(memory_space=pltpu.VMEM)
    return lambda *args: pl.pallas_call(
        kernel,
        out_shape=outs,
        in_specs=specs or [whole] * len(args),
        out_specs=jax.tree.map(lambda _: whole, outs),
        scratch_shapes=list(scratch),
        compiler_params=pltpu.CompilerParams(vmem_limit_bytes=limit),
    )(*args)


def beside(tiles, genes, offset):
    pairs = []
    paired = set()
    for low in range(offset, tiles - 1, 2):
        paired |= {low, low + 1}
        for gene in range(genes):
            pairs.append((low * genes + gene, (low + 1) * genes + gene))
            pairs.append(((low + 1) * genes + gene, low * genes + gene))
    for tile in range(tiles):
        if tile not in paired:
            for gene in range(genes):
                pairs.append((tile * genes + gene, tile * genes + (gene + 1) % genes))
    return pairs


def on_device(counts, cell_factor, gene_factor, tissue, neighbours):
    rank, width = cell_factor.shape
    genes = gene_factor.shape[1]
    tiles, halves = lax.axis_size("tile"), lax.axis_size("gene")
    tile = lax.axis_index("tile")
    flag_row = tissue[None]
    shape = jax.ShapeDtypeStruct
    factor = shape((rank, width), jnp.float32)
    chunks = genes // chunk_of(genes)
    part, kept, pick = call(
        first_kernel,
        (
            shape((rank, width + LANES), jnp.float32),
            shape((counts.shape[0], genes), jnp.bfloat16),
            shape((width + LANES, width), jnp.bfloat16),
        ),
        scratch=[
            pltpu.VMEM(cell_factor.shape, cell_factor.dtype),
            pltpu.VMEM(gene_factor.shape, gene_factor.dtype),
            pltpu.VMEM(neighbours.shape, neighbours.dtype),
            pltpu.VMEM(counts.shape, counts.dtype),
            pltpu.SemaphoreType.DMA((chunks,)),
            pltpu.SemaphoreType.DMA((3,)),
        ],
        specs=[pl.BlockSpec(memory_space=pltpu.HBM)] * 4,
    )(counts, cell_factor, gene_factor, neighbours)
    gsum_part = part[:, width:]
    cells = cell_factor

    def update(part, cells):
        if halves == 2:
            other = lax.ppermute(part, "gene", [(0, 1), (1, 0)])
        else:
            other = lax.psum(part, "gene") - part
        updated, edges = call(
            update_kernel, (factor, shape((rank + FLAG_ROWS, LANES), jnp.float32))
        )(part, other, cells, flag_row)
        sides = [
            lax.ppermute(edges, ("tile", "gene"), beside(tiles, halves, offset))
            for offset in (0, 1)
        ]
        return updated, flag_row, *sides, pick, kept, gene_factor

    cells, numer = call(next_kernel, (factor, factor))(*update(part, cells))
    part = jnp.concatenate([numer, gsum_part], axis=1)
    share = genes // tiles
    last = update(part, cells)
    if share % LANES == 0 and tiles + 3 <= STAT_ROWS:
        cells, sent = call(
            coded_kernel,
            (factor, shape((tiles, share // LANES * rank + STAT_ROWS, LANES), jnp.int16)),
        )(*last)
        got = lax.all_to_all(sent, "tile", 0, 0)
        fresh = call(fresh_kernel, shape((tiles, rank, share), jnp.bfloat16))(got, gene_factor)
        every = lax.all_to_all(fresh, "tile", 0, 0)
        return cells, call(spread_kernel, shape((rank, genes), jnp.bfloat16))(every)

    cells, hnum, hden = call(
        last_kernel,
        (factor, shape((rank, genes), jnp.float32), shape((rank, LANES), jnp.float32)),
    )(*last)
    sent = jnp.concatenate(
        [
            hnum.reshape(rank, tiles, share).transpose(1, 0, 2),
            jnp.broadcast_to(hden[None, :, :1], (tiles, rank, 1)),
        ],
        axis=2,
    )
    got = jnp.sum(lax.all_to_all(sent, "tile", 0, 0), axis=0)
    mine = lax.dynamic_slice_in_dim(gene_factor, tile * share, share, 1).astype(jnp.float32)
    fresh = (mine * got[:, :share] / got[:, share:]).astype(jnp.bfloat16)
    every = lax.all_to_all(jnp.broadcast_to(fresh[None], (tiles, rank, share)), "tile", 0, 0)
    return cells, every.transpose(1, 0, 2).reshape(rank, genes)


def solution(mesh):
    return jax.shard_map(
        on_device,
        mesh=mesh,
        in_specs=(
            P(("grp", "tile"), "gene"),
            P(None, ("grp", "tile")),
            P(None, ("grp", "gene")),
            P(("grp", "tile")),
            P(None, ("grp", "tile")),
        ),
        out_specs=(P(None, ("grp", "tile")), P(None, ("grp", "gene"))),
        check_vma=False,
    )
```

```python
import jax
import jax.numpy as jnp
from jax import lax
from jax.experimental import pallas as pl
from jax.experimental.pallas import tpu as pltpu
from jax.sharding import PartitionSpec as P

BORDER = 32
LANES = 128
FLAG_ROWS = 8
STAT_ROWS = 16
FULL = 32767.0
smooth_weight = 0.5
VMEM_BYTES = 24 * 1024 * 1024
FIRST_VMEM_BYTES = 49 * 1024 * 1024


def split(values):
    high = values.astype(jnp.bfloat16)
    low = (values - high.astype(jnp.float32)).astype(jnp.bfloat16)
    return high, low


def chunk_of(genes):
    for size in (512, 256, 128):
        if genes % size == 0:
            return size
    return genes


def factor_columns(cells):
    return jnp.concatenate(split(cells.T), axis=1)


def numerator(columns, gene_ref, counts_at, part_ref):
    rank, genes = gene_ref.shape
    size = chunk_of(genes)
    total = jnp.zeros((rank, columns.shape[0]), jnp.float32)
    for start in range(0, genes, size):
        hf = gene_ref[:, start : start + size]
        product = jnp.dot(
            columns, jnp.concatenate([hf, hf], axis=0), preferred_element_type=jnp.float32
        )
        ratio = counts_at(start, size) * pl.reciprocal(product, approx=True)
        total += lax.dot_general(
            hf,
            ratio.astype(jnp.bfloat16),
            (((1,), (1,)), ((), ())),
            preferred_element_type=jnp.float32,
        )
    part_ref[:, : columns.shape[0]] = total


def partner(tile, tiles, offset):
    other = jnp.where((tile + offset) % 2 == 0, tile + 1, tile - 1)
    return jnp.where((other >= 0) & (other < tiles), other, -1)


def pick_kernel(neigh_ref, pick_ref):
    width = neigh_ref.shape[1]
    tiles = lax.axis_size("tile")
    here = lax.axis_index("tile")
    neigh = neigh_ref[...] - here * width

    def found(where):
        total = jnp.zeros((LANES, width), jnp.float32)
        for j in range(neigh.shape[0]):
            total += (neigh[j : j + 1] == where).astype(jnp.float32)
        return total

    row = lax.broadcasted_iota(jnp.int32, (LANES, width), 0)
    for at in range(0, width, LANES):
        pick_ref[at : at + LANES] = found(at + row).astype(jnp.bfloat16)
    slot = row % (2 * BORDER)
    beside = jnp.where(
        row < 2 * BORDER, partner(here, tiles, 0), partner(here, tiles, 1)
    )
    where = (beside - here) * width + slot + jnp.where(slot < BORDER, 0, width - 2 * BORDER)
    pick_ref[width:] = jnp.where(beside < 0, 0.0, found(where)).astype(jnp.bfloat16)


def first_kernel(counts_ref, cells_ref, gene_ref, part_ref, kept_ref, landed, sems):
    rank, genes = gene_ref.shape
    width = cells_ref.shape[1]
    size = chunk_of(genes)
    copies = [
        pltpu.make_async_copy(
            counts_ref.at[:, pl.ds(at, size)], landed.at[:, pl.ds(at, size)], sems.at[i]
        )
        for i, at in enumerate(range(0, genes, size))
    ]
    for copy in copies:
        copy.start()
    gsum = jnp.sum(gene_ref[...].astype(jnp.float32), axis=1, keepdims=True)
    part_ref[:, width:] = jnp.broadcast_to(gsum, (rank, LANES))

    def counts_at(start, size):
        copies[start // size].wait()
        values = landed[:, start : start + size].astype(jnp.float32)
        kept_ref[:, start : start + size] = values.astype(jnp.bfloat16)
        return values

    numerator(factor_columns(cells_ref[...]), gene_ref, counts_at, part_ref)


def update_kernel(part_ref, other_ref, cells_ref, tissue_ref, updated_ref, edges_ref):
    rank, width = cells_ref.shape
    flags = tissue_ref[...] > 0
    numer = part_ref[:, :width] + other_ref[:, :width]
    gsum = part_ref[:, width:] + other_ref[:, width:]
    cells = cells_ref[...]
    updated = jnp.where(flags, cells * numer / gsum[:, :1], cells)
    updated_ref[...] = updated
    masked = jnp.where(flags, updated, 0.0)
    row = jnp.broadcast_to(flags.astype(jnp.float32), (FLAG_ROWS, width))
    both = jnp.concatenate([masked, row], axis=0)
    edges_ref[:, :BORDER] = both[:, :BORDER]
    edges_ref[:, BORDER : 2 * BORDER] = both[:, width - BORDER :]
    edges_ref[:, 2 * BORDER :] = jnp.zeros_like(edges_ref[:, 2 * BORDER :])


def smoothed(updated_ref, tissue_ref, first_ref, second_ref, pick_ref):
    rank, width = updated_ref.shape
    updated = updated_ref[...]
    flags = tissue_ref[...] > 0
    masked = jnp.where(flags, updated, 0.0)
    row = jnp.broadcast_to(flags.astype(jnp.float32), (FLAG_ROWS, width))
    own = jnp.concatenate([masked, row], axis=0)
    sides = jnp.concatenate(
        [first_ref[:, : 2 * BORDER], second_ref[:, : 2 * BORDER]], axis=1
    )
    near = jnp.zeros((rank + FLAG_ROWS, width), jnp.float32)
    for values, pick in ((own, pick_ref[:width]), (sides, pick_ref[width:])):
        for part in split(values):
            near += jnp.dot(part, pick, preferred_element_type=jnp.float32)
    mean = near[:rank] / jnp.maximum(near[rank : rank + 1], 1.0)
    return jnp.where(
        flags, (1.0 - smooth_weight) * updated + smooth_weight * mean, updated
    ), flags


def next_kernel(
    updated_ref, tissue_ref, first_ref, second_ref, pick_ref, kept_ref, gene_ref,
    cells_ref, part_ref,
):
    cells, flags = smoothed(updated_ref, tissue_ref, first_ref, second_ref, pick_ref)
    cells_ref[...] = cells

    def counts_at(start, size):
        return kept_ref[:, start : start + size].astype(jnp.float32)

    numerator(factor_columns(cells), gene_ref, counts_at, part_ref)


def gene_totals(columns, rows, kept_ref, gene_ref, start, size):
    rank = gene_ref.shape[0]
    hf = gene_ref[:, start : start + size]
    product = jnp.dot(
        columns, jnp.concatenate([hf, hf], axis=0), preferred_element_type=jnp.float32
    )
    counts = kept_ref[:, start : start + size].astype(jnp.float32)
    ratio = (counts * pl.reciprocal(product, approx=True)).astype(jnp.bfloat16)
    both = jnp.dot(rows, ratio, preferred_element_type=jnp.float32)
    return both[:rank] + both[rank:]


def last_kernel(
    updated_ref, tissue_ref, first_ref, second_ref, pick_ref, kept_ref, gene_ref,
    cells_ref, hnum_ref, hden_ref,
):
    rank, genes = gene_ref.shape
    size = chunk_of(genes)
    cells, flags = smoothed(updated_ref, tissue_ref, first_ref, second_ref, pick_ref)
    cells_ref[...] = cells
    masked = jnp.where(flags, cells, 0.0)
    hden_ref[...] = jnp.broadcast_to(jnp.sum(masked, axis=1, keepdims=True), hden_ref.shape)
    columns = factor_columns(cells)
    rows = jnp.concatenate(split(masked), axis=0)
    for start in range(0, genes, size):
        hnum_ref[:, start : start + size] = gene_totals(
            columns, rows, kept_ref, gene_ref, start, size
        )


def exponent(values):
    return jnp.ceil(jnp.log2(jnp.maximum(values, 1e-30)))


def whole_part(values):
    return (values + 0.5).astype(jnp.int32)


def coded_kernel(
    updated_ref, tissue_ref, first_ref, second_ref, pick_ref, kept_ref, gene_ref,
    cells_ref, sent_ref,
):
    rank, genes = gene_ref.shape
    tiles = sent_ref.shape[0]
    share = genes // tiles
    runs = share // LANES
    cells, flags = smoothed(updated_ref, tissue_ref, first_ref, second_ref, pick_ref)
    cells_ref[...] = cells
    masked = jnp.where(flags, cells, 0.0)
    columns = factor_columns(cells)
    rows = jnp.concatenate(split(masked), axis=0)
    hden = jnp.sum(masked, axis=1, keepdims=True)
    power = exponent(hden)
    scaled = hden * jnp.exp2(-power) * FULL
    high = jnp.floor(scaled)
    low = jnp.floor((scaled - high) * FULL)
    lane = lax.broadcasted_iota(jnp.int32, (rank, LANES), 1)
    stats = jnp.zeros((rank, LANES), jnp.float32)
    for at, value in enumerate((power, high, low)):
        stats = jnp.where(lane == tiles + at, value, stats)
    for tile in range(tiles):
        totals = gene_totals(columns, rows, kept_ref, gene_ref, tile * share, share)
        power = exponent(jnp.max(totals, axis=1, keepdims=True))
        stats = jnp.where(lane == tile, power, stats)
        coded = whole_part(totals * (jnp.exp2(-power) * FULL)).astype(jnp.int16)
        for run in range(runs):
            sent_ref[tile, run * rank : (run + 1) * rank] = coded[
                :, run * LANES : (run + 1) * LANES
            ]
    turned = jnp.concatenate([stats, jnp.zeros((LANES - rank, LANES), jnp.float32)], axis=0).T
    turned = turned[:STAT_ROWS].astype(jnp.int32).astype(jnp.int16)
    for tile in range(tiles):
        sent_ref[tile, runs * rank :] = turned


def fresh_kernel(got_ref, gene_ref, fresh_ref):
    tiles, _, share = fresh_ref.shape
    rank = gene_ref.shape[0]
    runs = share // LANES
    here = lax.axis_index("tile")

    def number(coded):
        return coded.astype(jnp.int32).astype(jnp.float32)

    stats = [number(got_ref[tile, runs * rank :]) for tile in range(tiles)]
    lane = lax.broadcasted_iota(jnp.int32, (rank, LANES), 1)
    scales = []
    hden = jnp.zeros((rank, 1), jnp.float32)
    group = LANES // STAT_ROWS
    for first in range(0, tiles, group):
        block = stats[first : first + group]
        short = LANES - len(block) * STAT_ROWS
        if short:
            block = block + [jnp.zeros((short, LANES), jnp.float32)]
        turned = jnp.concatenate(block, axis=0).T[:rank]
        for tile in range(first, min(first + group, tiles)):
            at = (tile - first) * STAT_ROWS
            power = jnp.sum(jnp.where(lane == at + here, turned, 0.0), axis=1, keepdims=True)
            scales.append(jnp.exp2(power) / FULL)
            at += tiles
            hden += (turned[:, at + 1 : at + 2] + turned[:, at + 2 : at + 3] / FULL) * (
                jnp.exp2(turned[:, at : at + 1]) / FULL
            )
    for run in range(runs):
        total = jnp.zeros((rank, LANES), jnp.float32)
        for tile in range(tiles):
            total += number(got_ref[tile, run * rank : (run + 1) * rank]) * scales[tile]
        place = pl.multiple_of(here * share + run * LANES, LANES)
        hf = gene_ref[:, pl.ds(place, LANES)].astype(jnp.float32)
        fresh = (hf * total / hden).astype(jnp.bfloat16)
        for tile in range(tiles):
            fresh_ref[tile, :, run * LANES : (run + 1) * LANES] = fresh


def spread_kernel(every_ref, out_ref):
    tiles, _, share = every_ref.shape
    for tile in range(tiles):
        out_ref[:, tile * share : (tile + 1) * share] = every_ref[tile]


def call(kernel, outs, scratch=(), specs=None, limit=VMEM_BYTES):
    whole = pl.BlockSpec(memory_space=pltpu.VMEM)
    return lambda *args: pl.pallas_call(
        kernel,
        out_shape=outs,
        in_specs=specs or [whole] * len(args),
        out_specs=jax.tree.map(lambda _: whole, outs),
        scratch_shapes=list(scratch),
        compiler_params=pltpu.CompilerParams(vmem_limit_bytes=limit),
    )(*args)


def beside(tiles, genes, offset):
    pairs = []
    paired = set()
    for low in range(offset, tiles - 1, 2):
        paired |= {low, low + 1}
        for gene in range(genes):
            pairs.append((low * genes + gene, (low + 1) * genes + gene))
            pairs.append(((low + 1) * genes + gene, low * genes + gene))
    for tile in range(tiles):
        if tile not in paired:
            for gene in range(genes):
                pairs.append((tile * genes + gene, tile * genes + (gene + 1) % genes))
    return pairs


def on_device(counts, cell_factor, gene_factor, tissue, neighbours):
    rank, width = cell_factor.shape
    genes = gene_factor.shape[1]
    tiles, halves = lax.axis_size("tile"), lax.axis_size("gene")
    tile = lax.axis_index("tile")
    flag_row = tissue[None]
    shape = jax.ShapeDtypeStruct
    factor = shape((rank, width), jnp.float32)
    chunks = genes // chunk_of(genes)
    pick = call(pick_kernel, shape((width + LANES, width), jnp.bfloat16))(neighbours)
    part, kept = call(
        first_kernel,
        (
            shape((rank, width + LANES), jnp.float32),
            shape((counts.shape[0], genes), jnp.bfloat16),
        ),
        scratch=[
            pltpu.VMEM(counts.shape, counts.dtype),
            pltpu.SemaphoreType.DMA((chunks,)),
        ],
        specs=[pl.BlockSpec(memory_space=pl.ANY)]
        + [pl.BlockSpec(memory_space=pltpu.VMEM)] * 2,
        limit=FIRST_VMEM_BYTES,
    )(counts, cell_factor, gene_factor)
    gsum_part = part[:, width:]
    cells = cell_factor

    def update(part, cells):
        if halves == 2:
            other = lax.ppermute(part, "gene", [(0, 1), (1, 0)])
        else:
            other = lax.psum(part, "gene") - part
        updated, edges = call(
            update_kernel, (factor, shape((rank + FLAG_ROWS, LANES), jnp.float32))
        )(part, other, cells, flag_row)
        sides = [
            lax.ppermute(edges, ("tile", "gene"), beside(tiles, halves, offset))
            for offset in (0, 1)
        ]
        return updated, flag_row, *sides, pick, kept, gene_factor

    cells, numer = call(next_kernel, (factor, factor))(*update(part, cells))
    part = jnp.concatenate([numer, gsum_part], axis=1)
    share = genes // tiles
    last = update(part, cells)
    if share % LANES == 0 and tiles + 3 <= STAT_ROWS:
        cells, sent = call(
            coded_kernel,
            (factor, shape((tiles, share // LANES * rank + STAT_ROWS, LANES), jnp.int16)),
        )(*last)
        got = lax.all_to_all(sent, "tile", 0, 0)
        fresh = call(fresh_kernel, shape((tiles, rank, share), jnp.bfloat16))(got, gene_factor)
        every = lax.all_to_all(fresh, "tile", 0, 0)
        return cells, call(spread_kernel, shape((rank, genes), jnp.bfloat16))(every)

    cells, hnum, hden = call(
        last_kernel,
        (factor, shape((rank, genes), jnp.float32), shape((rank, LANES), jnp.float32)),
    )(*last)
    sent = jnp.concatenate(
        [
            hnum.reshape(rank, tiles, share).transpose(1, 0, 2),
            jnp.broadcast_to(hden[None, :, :1], (tiles, rank, 1)),
        ],
        axis=2,
    )
    got = jnp.sum(lax.all_to_all(sent, "tile", 0, 0), axis=0)
    mine = lax.dynamic_slice_in_dim(gene_factor, tile * share, share, 1).astype(jnp.float32)
    fresh = (mine * got[:, :share] / got[:, share:]).astype(jnp.bfloat16)
    every = lax.all_to_all(jnp.broadcast_to(fresh[None], (tiles, rank, share)), "tile", 0, 0)
    return cells, every.transpose(1, 0, 2).reshape(rank, genes)


def solution(mesh):
    return jax.shard_map(
        on_device,
        mesh=mesh,
        in_specs=(
            P(("grp", "tile"), "gene"),
            P(None, ("grp", "tile")),
            P(None, ("grp", "gene")),
            P(("grp", "tile")),
            P(None, ("grp", "tile")),
        ),
        out_specs=(P(None, ("grp", "tile")), P(None, ("grp", "gene"))),
        check_vma=False,
    )
```

```python
import jax
import jax.numpy as jnp
from jax import lax
from jax.experimental import pallas as pl
from jax.experimental.pallas import tpu as pltpu
from jax.sharding import PartitionSpec as P

BORDER = 32
LANES = 128
ROWS = 8
STAT_ROWS = 16
FULL = 32767.0
smooth_weight = 0.5
VMEM_BYTES = 24 * 1024 * 1024
HEAD_VMEM_BYTES = 53 * 1024 * 1024
FIRST_VMEM_BYTES = 50 * 1024 * 1024
COPY_COLUMNS = 512


def split(values):
    high = values.astype(jnp.bfloat16)
    low = (values - high.astype(jnp.float32)).astype(jnp.bfloat16)
    return high, low


def piece(total, wanted):
    for size in (1024, 512, 256, 128):
        if size <= wanted and total % size == 0:
            return size
    return total


def ratio_of(counts, gene_rows, factor_rows):
    product = jnp.dot(gene_rows, factor_rows, preferred_element_type=jnp.float32)
    return (counts.astype(jnp.float32) * pl.reciprocal(product, approx=True)).astype(
        jnp.bfloat16
    )


def partner(tile, tiles, offset):
    other = jnp.where((tile + offset) % 2 == 0, tile + 1, tile - 1)
    return jnp.where((other >= 0) & (other < tiles), other, -1)


def pick_kernel(neigh_ref, pick_ref):
    width = neigh_ref.shape[1]
    tiles = lax.axis_size("tile")
    here = lax.axis_index("tile")
    neigh = neigh_ref[...] - here * width

    def found(where):
        total = jnp.zeros((LANES, width), jnp.float32)
        for j in range(neigh.shape[0]):
            total += (neigh[j : j + 1] == where).astype(jnp.float32)
        return total

    row = lax.broadcasted_iota(jnp.int32, (LANES, width), 0)
    for at in range(0, width, LANES):
        pick_ref[at : at + LANES] = found(at + row).astype(jnp.bfloat16)
    slot = row % (2 * BORDER)
    beside = jnp.where(
        row < 2 * BORDER, partner(here, tiles, 0), partner(here, tiles, 1)
    )
    where = (beside - here) * width + slot + jnp.where(slot < BORDER, 0, width - 2 * BORDER)
    pick_ref[width:] = jnp.where(beside < 0, 0.0, found(where)).astype(jnp.bfloat16)


def start_copies(counts_ref, landed, sems, first):
    copies = []
    for i in range(landed.shape[1] // COPY_COLUMNS):
        at = i * COPY_COLUMNS
        copies.append(
            pltpu.make_async_copy(
                counts_ref.at[:, pl.ds(first + at, COPY_COLUMNS)],
                landed.at[:, pl.ds(at, COPY_COLUMNS)],
                sems.at[i],
            )
        )
    for copy in copies:
        copy.start()
    return copies


def turned(landed, at):
    return landed[:, at : at + COPY_COLUMNS].astype(jnp.float32).T.astype(jnp.bfloat16)


def head_kernel(counts_ref, kept_ref, landed, sems):
    for i, copy in enumerate(start_copies(counts_ref, landed, sems, 0)):
        copy.wait()
        at = i * COPY_COLUMNS
        kept_ref[at : at + COPY_COLUMNS] = turned(landed, at)


def first_kernel(
    counts_ref, head_ref, cells_ref, gene_ref, part_ref, tail_ref, rows_ref, landed, sems
):
    rank, genes = gene_ref.shape
    width = cells_ref.shape[1]
    done = head_ref.shape[0]
    copies = start_copies(counts_ref, landed, sems, done)
    factor_rows = jnp.concatenate(split(cells_ref[...]), axis=0)
    gsum = jnp.zeros((rank, 1), jnp.float32)
    total = jnp.zeros((rank, width), jnp.float32)
    for at in range(0, genes, COPY_COLUMNS):
        hf = gene_ref[:, at : at + COPY_COLUMNS]
        wide = hf.astype(jnp.float32)
        gsum += jnp.sum(wide, axis=1, keepdims=True)
        rows = jnp.concatenate([wide, wide], axis=0).T.astype(jnp.bfloat16)
        rows_ref[at : at + COPY_COLUMNS] = rows
        if at < done:
            counts = head_ref[at : at + COPY_COLUMNS]
        else:
            copies[(at - done) // COPY_COLUMNS].wait()
            counts = turned(landed, at - done)
            tail_ref[at - done : at - done + COPY_COLUMNS] = counts
        ratio = ratio_of(counts, rows, factor_rows)
        total += jnp.dot(hf, ratio, preferred_element_type=jnp.float32)
    part_ref[:, :width] = total
    part_ref[:, width:] = jnp.broadcast_to(gsum, (rank, LANES))


def masked_rows(values, flags):
    flag_rows = jnp.broadcast_to(flags.astype(jnp.float32), (ROWS, flags.shape[1]))
    return jnp.concatenate([jnp.where(flags, values, 0.0), flag_rows], axis=0)


def update_kernel(numer_ref, other_ref, gsum_ref, cells_ref, tissue_ref, updated_ref, edges_ref):
    width = cells_ref.shape[1]
    flags = tissue_ref[...] > 0
    numer = numer_ref[...] + other_ref[...]
    cells = cells_ref[...]
    updated = jnp.where(flags, cells * numer / gsum_ref[:, :1], cells)
    updated_ref[...] = updated
    both = masked_rows(updated, flags)
    edges_ref[:, :BORDER] = both[:, :BORDER]
    edges_ref[:, BORDER : 2 * BORDER] = both[:, width - BORDER :]
    edges_ref[:, 2 * BORDER :] = jnp.zeros_like(edges_ref[:, 2 * BORDER :])


def first_update_kernel(
    part_ref, other_ref, cells_ref, tissue_ref, updated_ref, edges_ref, gsum_ref
):
    width = cells_ref.shape[1]
    gsum_ref[...] = part_ref[:, width:] + other_ref[:, width:]
    update_kernel(
        part_ref.at[:, :width], other_ref.at[:, :width], gsum_ref,
        cells_ref, tissue_ref, updated_ref, edges_ref,
    )


def smoothed(updated_ref, tissue_ref, first_ref, second_ref, pick_ref):
    rank, width = updated_ref.shape
    updated = updated_ref[...]
    flags = tissue_ref[...] > 0
    own = masked_rows(updated, flags)
    sides = jnp.concatenate(
        [first_ref[:, : 2 * BORDER], second_ref[:, : 2 * BORDER]], axis=1
    )
    near = jnp.zeros(own.shape, jnp.float32)
    for values, pick in ((own, pick_ref[:width]), (sides, pick_ref[width:])):
        for part in split(values):
            near += jnp.dot(part, pick, preferred_element_type=jnp.float32)
    mean = near[:rank] / jnp.maximum(near[rank : rank + 1], 1.0)
    cells = jnp.where(
        flags, (1.0 - smooth_weight) * updated + smooth_weight * mean, updated
    )
    return cells, flags


def runs_of(head_ref, tail_ref, wanted):
    start = 0
    for ref in (head_ref, tail_ref):
        size = piece(ref.shape[0], wanted)
        for at in range(0, ref.shape[0], size):
            yield start + at, ref[at : at + size]
        start += ref.shape[0]


def next_kernel(
    updated_ref, tissue_ref, first_ref, second_ref, pick_ref, head_ref, tail_ref,
    gene_ref, rows_ref, cells_ref, numer_ref,
):
    cells, _ = smoothed(updated_ref, tissue_ref, first_ref, second_ref, pick_ref)
    cells_ref[...] = cells
    factor_rows = jnp.concatenate(split(cells), axis=0)
    total = jnp.zeros(cells.shape, jnp.float32)
    for at, counts in runs_of(head_ref, tail_ref, 1024):
        end = at + counts.shape[0]
        ratio = ratio_of(counts, rows_ref[at:end], factor_rows)
        total += jnp.dot(gene_ref[:, at:end], ratio, preferred_element_type=jnp.float32)
    numer_ref[...] = total


def exponent(values):
    return jnp.ceil(jnp.log2(jnp.maximum(values, 1e-30)))


def coded_kernel(
    updated_ref, tissue_ref, first_ref, second_ref, pick_ref, head_ref, tail_ref,
    rows_ref, cells_ref, sent_ref, totals_ref,
):
    rank, genes = totals_ref.shape
    tiles = sent_ref.shape[0]
    groups = rank // ROWS
    columns = genes * groups // tiles
    cells, flags = smoothed(updated_ref, tissue_ref, first_ref, second_ref, pick_ref)
    cells_ref[...] = cells
    masked = jnp.where(flags, cells, 0.0)
    factor_rows = jnp.concatenate(split(cells), axis=0)
    masked_parts = jnp.concatenate(split(masked), axis=0)
    hden = jnp.sum(masked, axis=1, keepdims=True)
    power = exponent(hden)
    scaled = hden * jnp.exp2(-power) * FULL
    high = jnp.floor(scaled)
    lane = lax.broadcasted_iota(jnp.int32, (rank, LANES), 1)
    stats = jnp.zeros((rank, LANES), jnp.float32)
    for at, value in enumerate((power, high, jnp.floor((scaled - high) * FULL))):
        stats = jnp.where(lane == at + 1, value, stats)
    for at, counts in runs_of(head_ref, tail_ref, 512):
        end = at + counts.shape[0]
        ratio = ratio_of(counts, rows_ref[at:end], factor_rows)
        both = lax.dot_general(
            masked_parts, ratio, (((1,), (1,)), ((), ())), preferred_element_type=jnp.float32
        )
        totals_ref[:, at:end] = both[:rank] + both[rank:]
    blank = jnp.zeros((ROWS, LANES), jnp.int32)
    for column in range(genes // columns):
        totals = totals_ref[:, column * columns : (column + 1) * columns]
        power = exponent(jnp.max(totals, axis=1, keepdims=True))
        coded = (totals * (jnp.exp2(-power) * FULL) + 0.5).astype(jnp.int32)
        marks = jnp.where(lane == 0, power, stats).astype(jnp.int32)
        for group in range(groups):
            tile = group * (genes // columns) + column
            ranks = slice(group * ROWS, (group + 1) * ROWS)
            blocks = [coded[ranks, at : at + LANES] for at in range(0, columns, LANES)]
            blocks += [blank] * (len(blocks) % 2) + [marks[ranks], blank]
            for i in range(0, len(blocks), 2):
                sent_ref[tile, i * ROWS : (i + 2) * ROWS] = jnp.concatenate(
                    blocks[i : i + 2], axis=0
                ).astype(jnp.int16)


def fresh_kernel(got_ref, gene_ref, fresh_ref):
    tiles, height, _ = got_ref.shape
    columns = fresh_ref.shape[2]
    groups = gene_ref.shape[0] // ROWS
    here = lax.axis_index("tile")
    across = tiles // groups

    def number(coded):
        return coded.astype(jnp.int32).astype(jnp.float32)

    def twice(values):
        return jnp.concatenate([values, values], axis=0)

    hden = jnp.zeros((ROWS, 1), jnp.float32)
    scales = []
    for tile in range(tiles):
        marks = number(got_ref[tile, height - STAT_ROWS :])[:ROWS]
        scales.append(twice(jnp.exp2(marks[:, :1]) / FULL))
        hden += (marks[:, 2:3] + marks[:, 3:4] / FULL) * (jnp.exp2(marks[:, 1:2]) / FULL)
    totals = []
    for at in range(0, height - STAT_ROWS, 2 * ROWS):
        total = jnp.zeros((2 * ROWS, LANES), jnp.float32)
        for tile in range(tiles):
            total += number(got_ref[tile, at : at + 2 * ROWS]) * scales[tile]
        totals += [total[:ROWS], total[ROWS:]]
    hnum = jnp.concatenate(totals[: columns // LANES], axis=1)
    place = pl.multiple_of(lax.rem(here, across) * columns, LANES)
    every = gene_ref[:, pl.ds(place, columns)].astype(jnp.float32)
    hf = every[:ROWS]
    for group in range(1, groups):
        hf = jnp.where(here // across == group, every[group * ROWS : (group + 1) * ROWS], hf)
    fresh = (hf * hnum / hden).astype(jnp.bfloat16)
    for tile in range(tiles):
        fresh_ref[tile] = fresh


def call(kernel, outs, scratch=(), specs=None, limit=VMEM_BYTES):
    whole = pl.BlockSpec(memory_space=pltpu.VMEM)
    return lambda *args: pl.pallas_call(
        kernel,
        out_shape=outs,
        in_specs=specs or [whole] * len(args),
        out_specs=jax.tree.map(lambda _: whole, outs),
        scratch_shapes=list(scratch),
        compiler_params=pltpu.CompilerParams(vmem_limit_bytes=limit),
    )(*args)


def beside(tiles, halves, offset):
    pairs = []
    paired = set()
    for low in range(offset, tiles - 1, 2):
        paired |= {low, low + 1}
        for gene in range(halves):
            pairs.append((low * halves + gene, (low + 1) * halves + gene))
            pairs.append(((low + 1) * halves + gene, low * halves + gene))
    for tile in range(tiles):
        if tile not in paired:
            for gene in range(halves):
                pairs.append((tile * halves + gene, tile * halves + (gene + 1) % halves))
    return pairs


def on_device(counts, cell_factor, gene_factor, tissue, neighbours):
    rank, width = cell_factor.shape
    genes = gene_factor.shape[1]
    tiles, halves = lax.axis_size("tile"), lax.axis_size("gene")
    flag_row = tissue[None]
    shape = jax.ShapeDtypeStruct
    factor = shape((rank, width), jnp.float32)
    edge = shape((rank + ROWS, LANES), jnp.float32)
    gene_rows = shape((genes, 2 * rank), jnp.bfloat16)
    far = pl.BlockSpec(memory_space=pl.ANY)
    near = pl.BlockSpec(memory_space=pltpu.VMEM)

    def landing(columns):
        return [
            pltpu.VMEM((width, columns), counts.dtype),
            pltpu.SemaphoreType.DMA((columns // COPY_COLUMNS,)),
        ]

    head = genes // 4
    kept_head = call(
        head_kernel, shape((head, width), jnp.bfloat16), landing(head), [far],
        HEAD_VMEM_BYTES,
    )(counts)
    part, kept_tail, rows = call(
        first_kernel,
        (
            shape((rank, width + LANES), jnp.float32),
            shape((genes - head, width), jnp.bfloat16),
            gene_rows,
        ),
        landing(genes - head),
        [far] + [near] * 3,
        FIRST_VMEM_BYTES,
    )(counts, kept_head, cell_factor, gene_factor)
    pick = call(pick_kernel, shape((width + LANES, width), jnp.bfloat16))(neighbours)

    def swapped(part):
        if halves == 2:
            return lax.ppermute(part, "gene", [(0, 1), (1, 0)])
        return lax.psum(part, "gene") - part

    def around(updated, edges):
        sides = [
            lax.ppermute(edges, ("tile", "gene"), beside(tiles, halves, offset))
            for offset in (0, 1)
        ]
        return updated, flag_row, *sides, pick, kept_head, kept_tail

    updated, edges, gsum = call(
        first_update_kernel, (factor, edge, shape((rank, LANES), jnp.float32))
    )(part, swapped(part), cell_factor, flag_row)
    cells, numer = call(next_kernel, (factor, factor))(
        *around(updated, edges), gene_factor, rows
    )
    updated, edges = call(update_kernel, (factor, edge))(
        numer, swapped(numer), gsum, cells, flag_row
    )
    across = tiles * ROWS // rank
    columns = genes // across
    blocks = columns // LANES
    height = (blocks + blocks % 2) * ROWS + STAT_ROWS
    cells, sent = call(
        coded_kernel,
        (factor, shape((tiles, height, LANES), jnp.int16)),
        [pltpu.VMEM((rank, genes), jnp.float32)],
    )(*around(updated, edges), rows)
    got = lax.all_to_all(sent, "tile", 0, 0)
    fresh = call(fresh_kernel, shape((tiles, ROWS, columns), jnp.bfloat16))(got, gene_factor)
    every = lax.all_to_all(fresh, "tile", 0, 0)
    every = every.reshape(rank // ROWS, across, ROWS, columns)
    return cells, every.transpose(0, 2, 1, 3).reshape(rank, genes)


def solution(mesh):
    return jax.shard_map(
        on_device,
        mesh=mesh,
        in_specs=(
            P(("grp", "tile"), "gene"),
            P(None, ("grp", "tile")),
            P(None, ("grp", "gene")),
            P(("grp", "tile")),
            P(None, ("grp", "tile")),
        ),
        out_specs=(P(None, ("grp", "tile")), P(None, ("grp", "gene"))),
        check_vma=False,
    )
```

```python
import jax
import jax.numpy as jnp
from jax import lax
from jax.experimental import pallas as pl
from jax.experimental.pallas import tpu as pltpu
from jax.sharding import PartitionSpec as P

BORDER = 32
LANES = 128
ROWS = 8
STAT_ROWS = 16
FULL = 32767.0
smooth_weight = 0.5
VMEM_BYTES = 24 * 1024 * 1024
COUNTS_VMEM_BYTES = 51 * 1024 * 1024
COPY_COLUMNS = 512


def split(values):
    high = values.astype(jnp.bfloat16)
    low = (values - high.astype(jnp.float32)).astype(jnp.bfloat16)
    return high, low


def piece(total, wanted):
    for size in (1024, 512, 256, 128):
        if size <= wanted and total % size == 0:
            return size
    return total


def ratio_of(counts, gene_rows, factor_rows):
    product = jnp.dot(gene_rows, factor_rows, preferred_element_type=jnp.float32)
    return (counts.astype(jnp.float32) * pl.reciprocal(product, approx=True)).astype(
        jnp.bfloat16
    )


def partner(tile, tiles, offset):
    other = jnp.where((tile + offset) % 2 == 0, tile + 1, tile - 1)
    return jnp.where((other >= 0) & (other < tiles), other, -1)


def pick_kernel(neigh_ref, pick_ref):
    width = neigh_ref.shape[1]
    tiles = lax.axis_size("tile")
    here = lax.axis_index("tile")
    neigh = neigh_ref[...] - here * width

    def found(where):
        total = jnp.zeros((LANES, width), jnp.float32)
        for j in range(neigh.shape[0]):
            total += (neigh[j : j + 1] == where).astype(jnp.float32)
        return total

    row = lax.broadcasted_iota(jnp.int32, (LANES, width), 0)
    for at in range(0, width, LANES):
        pick_ref[at : at + LANES] = found(at + row).astype(jnp.bfloat16)
    slot = row % (2 * BORDER)
    beside = jnp.where(
        row < 2 * BORDER, partner(here, tiles, 0), partner(here, tiles, 1)
    )
    where = (beside - here) * width + slot + jnp.where(slot < BORDER, 0, width - 2 * BORDER)
    pick_ref[width:] = jnp.where(beside < 0, 0.0, found(where)).astype(jnp.bfloat16)


def start_copies(counts_ref, landed, sems):
    copies = []
    for i in range(landed.shape[1] // COPY_COLUMNS):
        at = i * COPY_COLUMNS
        copies.append(
            pltpu.make_async_copy(
                counts_ref.at[:, pl.ds(at, COPY_COLUMNS)],
                landed.at[:, pl.ds(at, COPY_COLUMNS)],
                sems.at[i],
            )
        )
    for copy in copies:
        copy.start()
    return copies


def turned(landed, at):
    return landed[:, at : at + COPY_COLUMNS].astype(jnp.float32).T.astype(jnp.bfloat16)


def turn_kernel(counts_ref, kept_ref, landed, sems):
    for i, copy in enumerate(start_copies(counts_ref, landed, sems)):
        copy.wait()
        at = i * COPY_COLUMNS
        kept_ref[at : at + COPY_COLUMNS] = turned(landed, at)


def runs_of(kept_ref, wanted):
    genes = kept_ref.shape[0]
    size = piece(genes, wanted)
    for at in range(0, genes, size):
        yield at, kept_ref[at : at + size]


def first_kernel(kept_ref, cells_ref, gene_ref, part_ref, rows_ref):
    rank, genes = gene_ref.shape
    width = cells_ref.shape[1]
    factor_rows = jnp.concatenate(split(cells_ref[...]), axis=0)
    gsum = jnp.zeros((rank, 1), jnp.float32)
    total = jnp.zeros((rank, width), jnp.float32)
    for at, counts in runs_of(kept_ref, 1024):
        end = at + counts.shape[0]
        hf = gene_ref[:, at:end]
        wide = hf.astype(jnp.float32)
        gsum += jnp.sum(wide, axis=1, keepdims=True)
        rows = jnp.concatenate([wide, wide], axis=0).T.astype(jnp.bfloat16)
        rows_ref[at:end] = rows
        ratio = ratio_of(counts, rows, factor_rows)
        total += jnp.dot(hf, ratio, preferred_element_type=jnp.float32)
    part_ref[:, :width] = total
    part_ref[:, width:] = jnp.broadcast_to(gsum, (rank, LANES))


def masked_rows(values, flags):
    flag_rows = jnp.broadcast_to(flags.astype(jnp.float32), (ROWS, flags.shape[1]))
    return jnp.concatenate([jnp.where(flags, values, 0.0), flag_rows], axis=0)


def update_kernel(numer_ref, other_ref, gsum_ref, cells_ref, tissue_ref, updated_ref, edges_ref):
    width = cells_ref.shape[1]
    flags = tissue_ref[...] > 0
    numer = numer_ref[...] + other_ref[...]
    cells = cells_ref[...]
    updated = jnp.where(flags, cells * numer / gsum_ref[:, :1], cells)
    updated_ref[...] = updated
    both = masked_rows(updated, flags)
    edges_ref[:, :BORDER] = both[:, :BORDER]
    edges_ref[:, BORDER : 2 * BORDER] = both[:, width - BORDER :]
    edges_ref[:, 2 * BORDER :] = jnp.zeros_like(edges_ref[:, 2 * BORDER :])


def first_update_kernel(
    part_ref, other_ref, cells_ref, tissue_ref, updated_ref, edges_ref, gsum_ref
):
    width = cells_ref.shape[1]
    gsum_ref[...] = part_ref[:, width:] + other_ref[:, width:]
    update_kernel(
        part_ref.at[:, :width], other_ref.at[:, :width], gsum_ref,
        cells_ref, tissue_ref, updated_ref, edges_ref,
    )


def smoothed(updated_ref, tissue_ref, first_ref, second_ref, pick_ref):
    rank, width = updated_ref.shape
    updated = updated_ref[...]
    flags = tissue_ref[...] > 0
    own = masked_rows(updated, flags)
    sides = jnp.concatenate(
        [first_ref[:, : 2 * BORDER], second_ref[:, : 2 * BORDER]], axis=1
    )
    near = jnp.zeros(own.shape, jnp.float32)
    for values, pick in ((own, pick_ref[:width]), (sides, pick_ref[width:])):
        for part in split(values):
            near += jnp.dot(part, pick, preferred_element_type=jnp.float32)
    mean = near[:rank] / jnp.maximum(near[rank : rank + 1], 1.0)
    cells = jnp.where(
        flags, (1.0 - smooth_weight) * updated + smooth_weight * mean, updated
    )
    return cells, flags


def next_kernel(
    updated_ref, tissue_ref, first_ref, second_ref, pick_ref, kept_ref,
    gene_ref, rows_ref, cells_ref, numer_ref,
):
    cells, _ = smoothed(updated_ref, tissue_ref, first_ref, second_ref, pick_ref)
    cells_ref[...] = cells
    factor_rows = jnp.concatenate(split(cells), axis=0)
    total = jnp.zeros(cells.shape, jnp.float32)
    for at, counts in runs_of(kept_ref, 1024):
        end = at + counts.shape[0]
        ratio = ratio_of(counts, rows_ref[at:end], factor_rows)
        total += jnp.dot(gene_ref[:, at:end], ratio, preferred_element_type=jnp.float32)
    numer_ref[...] = total


def exponent(values):
    return jnp.ceil(jnp.log2(jnp.maximum(values, 1e-30)))


def coded_kernel(
    updated_ref, tissue_ref, first_ref, second_ref, pick_ref, kept_ref,
    rows_ref, cells_ref, sent_ref, totals_ref,
):
    rank, genes = totals_ref.shape
    tiles = sent_ref.shape[0]
    groups = rank // ROWS
    columns = genes * groups // tiles
    cells, flags = smoothed(updated_ref, tissue_ref, first_ref, second_ref, pick_ref)
    cells_ref[...] = cells
    masked = jnp.where(flags, cells, 0.0)
    factor_rows = jnp.concatenate(split(cells), axis=0)
    masked_parts = jnp.concatenate(split(masked), axis=0)
    masked_columns = masked_parts.astype(jnp.float32).T.astype(jnp.bfloat16)
    hden = jnp.sum(masked, axis=1, keepdims=True)
    power = exponent(hden)
    scaled = hden * jnp.exp2(-power) * FULL
    high = jnp.floor(scaled)
    lane = lax.broadcasted_iota(jnp.int32, (rank, LANES), 1)
    stats = jnp.zeros((rank, LANES), jnp.float32)
    for at, value in enumerate((power, high, jnp.floor((scaled - high) * FULL))):
        stats = jnp.where(lane == at + 1, value, stats)
    for at, counts in runs_of(kept_ref, 1024):
        end = at + counts.shape[0]
        ratio = ratio_of(counts, rows_ref[at:end], factor_rows)
        both = jnp.dot(ratio, masked_columns, preferred_element_type=jnp.float32).T
        totals_ref[:, at:end] = both[:rank] + both[rank:]
    blank = jnp.zeros((ROWS, LANES), jnp.int32)
    for column in range(genes // columns):
        totals = totals_ref[:, column * columns : (column + 1) * columns]
        power = exponent(jnp.max(totals, axis=1, keepdims=True))
        coded = (totals * (jnp.exp2(-power) * FULL) + 0.5).astype(jnp.int32)
        marks = jnp.where(lane == 0, power, stats).astype(jnp.int32)
        for group in range(groups):
            tile = group * (genes // columns) + column
            ranks = slice(group * ROWS, (group + 1) * ROWS)
            blocks = [coded[ranks, at : at + LANES] for at in range(0, columns, LANES)]
            blocks += [blank] * (len(blocks) % 2) + [marks[ranks], blank]
            for i in range(0, len(blocks), 2):
                sent_ref[tile, i * ROWS : (i + 2) * ROWS] = jnp.concatenate(
                    blocks[i : i + 2], axis=0
                ).astype(jnp.int16)


def fresh_kernel(got_ref, gene_ref, fresh_ref):
    tiles, height, _ = got_ref.shape
    columns = fresh_ref.shape[2]
    groups = gene_ref.shape[0] // ROWS
    here = lax.axis_index("tile")
    across = tiles // groups

    def number(coded):
        return coded.astype(jnp.int32).astype(jnp.float32)

    def twice(values):
        return jnp.concatenate([values, values], axis=0)

    hden = jnp.zeros((ROWS, 1), jnp.float32)
    scales = []
    for tile in range(tiles):
        marks = number(got_ref[tile, height - STAT_ROWS :])[:ROWS]
        scales.append(twice(jnp.exp2(marks[:, :1]) / FULL))
        hden += (marks[:, 2:3] + marks[:, 3:4] / FULL) * (jnp.exp2(marks[:, 1:2]) / FULL)
    totals = []
    for at in range(0, height - STAT_ROWS, 2 * ROWS):
        total = jnp.zeros((2 * ROWS, LANES), jnp.float32)
        for tile in range(tiles):
            total += number(got_ref[tile, at : at + 2 * ROWS]) * scales[tile]
        totals += [total[:ROWS], total[ROWS:]]
    hnum = jnp.concatenate(totals[: columns // LANES], axis=1)
    place = pl.multiple_of(lax.rem(here, across) * columns, LANES)
    every = gene_ref[:, pl.ds(place, columns)].astype(jnp.float32)
    hf = every[:ROWS]
    for group in range(1, groups):
        hf = jnp.where(here // across == group, every[group * ROWS : (group + 1) * ROWS], hf)
    fresh = (hf * hnum / hden).astype(jnp.bfloat16)
    for tile in range(tiles):
        fresh_ref[tile] = fresh


def call(kernel, outs, scratch=(), specs=None, limit=VMEM_BYTES):
    whole = pl.BlockSpec(memory_space=pltpu.VMEM)
    return lambda *args: pl.pallas_call(
        kernel,
        out_shape=outs,
        in_specs=specs or [whole] * len(args),
        out_specs=jax.tree.map(lambda _: whole, outs),
        scratch_shapes=list(scratch),
        compiler_params=pltpu.CompilerParams(vmem_limit_bytes=limit),
    )(*args)


def beside(tiles, halves, offset):
    pairs = []
    paired = set()
    for low in range(offset, tiles - 1, 2):
        paired |= {low, low + 1}
        for gene in range(halves):
            other = (gene + 1) % halves
            pairs.append((low * halves + gene, (low + 1) * halves + other))
            pairs.append(((low + 1) * halves + gene, low * halves + other))
    for tile in range(tiles):
        if tile not in paired:
            for gene in range(halves):
                pairs.append((tile * halves + gene, tile * halves + (gene + 1) % halves))
    return pairs


def on_device(counts, cell_factor, gene_factor, tissue, neighbours):
    rank, width = cell_factor.shape
    genes = gene_factor.shape[1]
    tiles, halves = lax.axis_size("tile"), lax.axis_size("gene")
    flag_row = tissue[None]
    shape = jax.ShapeDtypeStruct
    factor = shape((rank, width), jnp.float32)
    edge = shape((rank + ROWS, LANES), jnp.float32)
    gene_rows = shape((genes, 2 * rank), jnp.bfloat16)
    far = pl.BlockSpec(memory_space=pl.ANY)

    kept = call(
        turn_kernel,
        shape((genes, width), jnp.bfloat16),
        [
            pltpu.VMEM(counts.shape, counts.dtype),
            pltpu.SemaphoreType.DMA((genes // COPY_COLUMNS,)),
        ],
        [far],
        COUNTS_VMEM_BYTES,
    )(counts)
    part, rows = call(
        first_kernel, (shape((rank, width + LANES), jnp.float32), gene_rows)
    )(kept, cell_factor, gene_factor)
    pick = call(pick_kernel, shape((width + LANES, width), jnp.bfloat16))(neighbours)

    def swapped(part):
        if halves == 2:
            return lax.ppermute(part, "gene", [(0, 1), (1, 0)])
        return lax.psum(part, "gene") - part

    def around(updated, edges):
        sides = [
            lax.ppermute(edges, ("tile", "gene"), beside(tiles, halves, offset))
            for offset in (0, 1)
        ]
        return updated, flag_row, *sides, pick, kept

    updated, edges, gsum = call(
        first_update_kernel, (factor, edge, shape((rank, LANES), jnp.float32))
    )(part, swapped(part), cell_factor, flag_row)
    cells, numer = call(next_kernel, (factor, factor))(
        *around(updated, edges), gene_factor, rows
    )
    updated, edges = call(update_kernel, (factor, edge))(
        numer, swapped(numer), gsum, cells, flag_row
    )
    across = tiles * ROWS // rank
    columns = genes // across
    blocks = columns // LANES
    height = (blocks + blocks % 2) * ROWS + STAT_ROWS
    cells, sent = call(
        coded_kernel,
        (factor, shape((tiles, height, LANES), jnp.int16)),
        [pltpu.VMEM((rank, genes), jnp.float32)],
    )(*around(updated, edges), rows)
    got = lax.all_to_all(sent, "tile", 0, 0)
    fresh = call(fresh_kernel, shape((tiles, ROWS, columns), jnp.bfloat16))(got, gene_factor)
    every = lax.all_to_all(fresh, "tile", 0, 0)
    every = every.reshape(rank // ROWS, across, ROWS, columns)
    return cells, every.transpose(0, 2, 1, 3).reshape(rank, genes)


def solution(mesh):
    return jax.shard_map(
        on_device,
        mesh=mesh,
        in_specs=(
            P(("grp", "tile"), "gene"),
            P(None, ("grp", "tile")),
            P(None, ("grp", "gene")),
            P(("grp", "tile")),
            P(None, ("grp", "tile")),
        ),
        out_specs=(P(None, ("grp", "tile")), P(None, ("grp", "gene"))),
        check_vma=False,
    )
```

```python
import functools

import jax
import jax.numpy as jnp
from jax import lax
from jax.experimental import pallas as pl
from jax.experimental.pallas import tpu as pltpu
from jax.sharding import PartitionSpec as P

BORDER = 32
LANES = 128
ROWS = 8
STAT_ROWS = 16
FULL = 32767.0
smooth_weight = 0.5
VMEM_BYTES = 24 * 1024 * 1024
COUNTS_VMEM_BYTES = 51 * 1024 * 1024
COPY_COLUMNS = 512


def split(values):
    high = values.astype(jnp.bfloat16)
    low = (values - high.astype(jnp.float32)).astype(jnp.bfloat16)
    return high, low


def piece(total, wanted):
    for size in (1024, 512, 256, 128):
        if size <= wanted and total % size == 0:
            return size
    return total


def ratio_of(counts, gene_rows, factor_rows):
    product = jnp.dot(gene_rows, factor_rows, preferred_element_type=jnp.float32)
    return (counts.astype(jnp.float32) * pl.reciprocal(product, approx=True)).astype(
        jnp.bfloat16
    )


def partner(tile, tiles, offset):
    other = jnp.where((tile + offset) % 2 == 0, tile + 1, tile - 1)
    return jnp.where((other >= 0) & (other < tiles), other, -1)


def pick_kernel(neigh_ref, pick_ref):
    width = neigh_ref.shape[1]
    tiles = lax.axis_size("tile")
    here = lax.axis_index("tile")
    neigh = neigh_ref[...] - here * width

    def found(where):
        total = jnp.zeros((LANES, width), jnp.float32)
        for j in range(neigh.shape[0]):
            total += (neigh[j : j + 1] == where).astype(jnp.float32)
        return total

    row = lax.broadcasted_iota(jnp.int32, (LANES, width), 0)
    for at in range(0, width, LANES):
        pick_ref[at : at + LANES] = found(at + row).astype(jnp.bfloat16)
    slot = row % (2 * BORDER)
    beside = jnp.where(
        row < 2 * BORDER, partner(here, tiles, 0), partner(here, tiles, 1)
    )
    where = (beside - here) * width + slot + jnp.where(slot < BORDER, 0, width - 2 * BORDER)
    pick_ref[width:] = jnp.where(beside < 0, 0.0, found(where)).astype(jnp.bfloat16)


def start_copies(counts_ref, landed, sems):
    copies = []
    for i in range(landed.shape[1] // COPY_COLUMNS):
        at = i * COPY_COLUMNS
        copies.append(
            pltpu.make_async_copy(
                counts_ref.at[:, pl.ds(at, COPY_COLUMNS)],
                landed.at[:, pl.ds(at, COPY_COLUMNS)],
                sems.at[i],
            )
        )
    for copy in copies:
        copy.start()
    return copies


def turned(landed, at):
    return landed[:, at : at + COPY_COLUMNS].astype(jnp.float32).T.astype(jnp.bfloat16)


def turn_kernel(counts_ref, kept_ref, landed, sems):
    for i, copy in enumerate(start_copies(counts_ref, landed, sems)):
        copy.wait()
        at = i * COPY_COLUMNS
        kept_ref[at : at + COPY_COLUMNS] = turned(landed, at)


def runs_of(kept_ref, wanted):
    genes = kept_ref.shape[0]
    size = piece(genes, wanted)
    for at in range(0, genes, size):
        yield at, kept_ref[at : at + size]


def first_kernel(kept_ref, cells_ref, gene_ref, part_ref, rows_ref):
    rank, genes = gene_ref.shape
    width = cells_ref.shape[1]
    factor_rows = jnp.concatenate(split(cells_ref[...]), axis=0)
    gsum = jnp.zeros((rank, 1), jnp.float32)
    total = jnp.zeros((rank, width), jnp.float32)
    for at, counts in runs_of(kept_ref, 1024):
        end = at + counts.shape[0]
        hf = gene_ref[:, at:end]
        wide = hf.astype(jnp.float32)
        gsum += jnp.sum(wide, axis=1, keepdims=True)
        rows = jnp.concatenate([wide, wide], axis=0).T.astype(jnp.bfloat16)
        rows_ref[at:end] = rows
        ratio = ratio_of(counts, rows, factor_rows)
        total += jnp.dot(hf, ratio, preferred_element_type=jnp.float32)
    part_ref[:, :width] = total
    part_ref[:, width:] = jnp.broadcast_to(gsum, (rank, LANES))


def masked_rows(values, flags):
    flag_rows = jnp.broadcast_to(flags.astype(jnp.float32), (ROWS, flags.shape[1]))
    return jnp.concatenate([jnp.where(flags, values, 0.0), flag_rows], axis=0)


def update_kernel(numer_ref, other_ref, gsum_ref, cells_ref, tissue_ref, updated_ref, edges_ref):
    width = cells_ref.shape[1]
    flags = tissue_ref[...] > 0
    numer = numer_ref[...] + other_ref[...]
    cells = cells_ref[...]
    updated = jnp.where(flags, cells * numer / gsum_ref[:, :1], cells)
    updated_ref[...] = updated
    both = masked_rows(updated, flags)
    edges_ref[:, :BORDER] = both[:, :BORDER]
    edges_ref[:, BORDER : 2 * BORDER] = both[:, width - BORDER :]
    edges_ref[:, 2 * BORDER :] = jnp.zeros_like(edges_ref[:, 2 * BORDER :])


def first_update_kernel(
    part_ref, other_ref, cells_ref, tissue_ref, updated_ref, edges_ref, gsum_ref
):
    width = cells_ref.shape[1]
    gsum_ref[...] = part_ref[:, width:] + other_ref[:, width:]
    update_kernel(
        part_ref.at[:, :width], other_ref.at[:, :width], gsum_ref,
        cells_ref, tissue_ref, updated_ref, edges_ref,
    )


def smoothed(updated_ref, tissue_ref, first_ref, second_ref, pick_ref):
    rank, width = updated_ref.shape
    updated = updated_ref[...]
    flags = tissue_ref[...] > 0
    own = masked_rows(updated, flags)
    sides = jnp.concatenate(
        [first_ref[:, : 2 * BORDER], second_ref[:, : 2 * BORDER]], axis=1
    )
    near = jnp.zeros(own.shape, jnp.float32)
    for values, pick in ((own, pick_ref[:width]), (sides, pick_ref[width:])):
        for part in split(values):
            near += jnp.dot(part, pick, preferred_element_type=jnp.float32)
    mean = near[:rank] / jnp.maximum(near[rank : rank + 1], 1.0)
    cells = jnp.where(
        flags, (1.0 - smooth_weight) * updated + smooth_weight * mean, updated
    )
    return cells, flags


def next_kernel(
    updated_ref, tissue_ref, first_ref, second_ref, pick_ref, kept_ref,
    gene_ref, rows_ref, cells_ref, numer_ref,
):
    cells, _ = smoothed(updated_ref, tissue_ref, first_ref, second_ref, pick_ref)
    cells_ref[...] = cells
    factor_rows = jnp.concatenate(split(cells), axis=0)
    total = jnp.zeros(cells.shape, jnp.float32)
    for at, counts in runs_of(kept_ref, 1024):
        end = at + counts.shape[0]
        ratio = ratio_of(counts, rows_ref[at:end], factor_rows)
        total += jnp.dot(gene_ref[:, at:end], ratio, preferred_element_type=jnp.float32)
    numer_ref[...] = total


def exponent(values):
    return jnp.ceil(jnp.log2(jnp.maximum(values, 1e-30)))


def share_height(columns):
    blocks = columns // LANES
    return (blocks + blocks % 2) * ROWS + STAT_ROWS


def encode(values, hden, target):
    power = exponent(jnp.max(values, axis=1, keepdims=True))
    coded = (values * (jnp.exp2(-power) * FULL) + 0.5).astype(jnp.int32)
    hden_power = exponent(hden)
    scaled = hden * jnp.exp2(-hden_power) * FULL
    high = jnp.floor(scaled)
    low = jnp.floor((scaled - high) * FULL)
    lane = lax.broadcasted_iota(jnp.int32, (ROWS, LANES), 1)
    marks = jnp.zeros((ROWS, LANES), jnp.float32)
    for at, value in enumerate((power, hden_power, high, low)):
        marks = jnp.where(lane == at, value, marks)
    blank = jnp.zeros((ROWS, LANES), jnp.int32)
    blocks = [coded[:, at : at + LANES] for at in range(0, values.shape[1], LANES)]
    blocks += [blank] * (len(blocks) % 2) + [marks.astype(jnp.int32), blank]
    for i in range(0, len(blocks), 2):
        target[i * ROWS : (i + 2) * ROWS] = jnp.concatenate(
            blocks[i : i + 2], axis=0
        ).astype(jnp.int16)


def decode(source, columns):
    def number(start):
        return source[start : start + 2 * ROWS].astype(jnp.int32).astype(jnp.float32)

    height = source.shape[0]
    marks = number(height - STAT_ROWS)[:ROWS]
    scale = jnp.exp2(marks[:, :1]) / FULL
    hden = (marks[:, 2:3] + marks[:, 3:4] / FULL) * (jnp.exp2(marks[:, 1:2]) / FULL)
    blocks = []
    for start in range(0, height - STAT_ROWS, 2 * ROWS):
        both = number(start)
        blocks += [both[:ROWS] * scale, both[ROWS:] * scale]
    return jnp.concatenate(blocks[: columns // LANES], axis=1), hden


def last_pass(
    updated_ref, tissue_ref, first_ref, second_ref, pick_ref, kept_ref, rows_ref,
    cells_ref, totals_ref,
):
    rank, genes = totals_ref.shape[0], kept_ref.shape[0]
    cells, flags = smoothed(updated_ref, tissue_ref, first_ref, second_ref, pick_ref)
    cells_ref[...] = cells
    masked = jnp.where(flags, cells, 0.0)
    factor_rows = jnp.concatenate(split(cells), axis=0)
    masked_rows = jnp.concatenate(split(masked), axis=0)
    masked_columns = masked_rows.astype(jnp.float32).T.astype(jnp.bfloat16)
    hden = jnp.sum(masked, axis=1, keepdims=True)
    totals_ref[:, genes:] = jnp.broadcast_to(hden, (rank, LANES))
    for at, counts in runs_of(kept_ref, 1024):
        end = at + counts.shape[0]
        ratio = ratio_of(counts, rows_ref[at:end], factor_rows)
        both = jnp.dot(ratio, masked_columns, preferred_element_type=jnp.float32).T
        totals_ref[:, at:end] = both[:rank] + both[rank:]


def shares_kernel(*refs):
    *passed, sent_ref, totals_ref = refs
    last_pass(*passed, totals_ref)
    rank = totals_ref.shape[0]
    genes = totals_ref.shape[1] - LANES
    across = sent_ref.shape[0] * ROWS // rank
    columns = genes // across
    for tile in range(sent_ref.shape[0]):
        ranks = pl.ds(tile // across * ROWS, ROWS)
        start = tile % across * columns
        encode(
            totals_ref[ranks, start : start + columns],
            totals_ref[ranks, genes : genes + 1],
            sent_ref.at[tile],
        )


def distance_kernel(*refs):
    passed, (*sent_refs, own_ref, totals_ref, coded_ref) = refs[:8], refs[8:]
    last_pass(*passed, totals_ref)
    tiles, height, _ = coded_ref.shape
    genes = totals_ref.shape[1] - LANES
    columns = genes // 2
    for tile in range(tiles):
        ranks = slice(tile // 2 * ROWS, (tile // 2 + 1) * ROWS)
        start = tile % 2 * columns
        encode(
            totals_ref[ranks, start : start + columns],
            totals_ref[ranks, genes : genes + 1],
            coded_ref.at[tile],
        )
    tile = lax.axis_index("tile")
    for distance in range(tiles // 2):
        there = tile ^ (2 * distance)
        own_ref[distance * height : (distance + 1) * height] = coded_ref[there]
        place = sent_refs[(distance or tiles // 2 - 1) - 1]
        start = 0 if distance else height
        place[start : start + height] = coded_ref[there ^ 1]


def column_kernel(distance, columns, got_ref, own_ref, sent_ref):
    height = sent_ref.shape[0]
    start = 0 if distance else height
    values, hden = decode(got_ref.at[start : start + height], columns)
    start = height * distance
    more, more_hden = decode(own_ref.at[start : start + height], columns)
    encode(values + more, hden + more_hden, sent_ref)


def fresh_of(hnum, hden, gene_ref, across):
    columns = hnum.shape[1]
    here = lax.axis_index("tile")
    place = pl.multiple_of(lax.rem(here, across) * columns, LANES)
    every = gene_ref[:, pl.ds(place, columns)].astype(jnp.float32)
    hf = every[:ROWS]
    for group in range(1, gene_ref.shape[0] // ROWS):
        hf = jnp.where(here // across == group, every[group * ROWS : (group + 1) * ROWS], hf)
    return (hf * hnum / hden).astype(jnp.bfloat16)


def all_shares_kernel(got_ref, gene_ref, fresh_ref):
    tiles, _, columns = fresh_ref.shape
    hnum, hden = decode(got_ref.at[0], columns)
    for tile in range(1, tiles):
        more, more_hden = decode(got_ref.at[tile], columns)
        hnum += more
        hden += more_hden
    fresh = fresh_of(hnum, hden, gene_ref, tiles * ROWS // gene_ref.shape[0])
    for tile in range(tiles):
        fresh_ref[tile] = fresh


def fresh_kernel(*refs):
    *got_refs, gene_ref, fresh_ref = refs
    hnum, hden = 0.0, 0.0
    for ref in got_refs:
        more, more_hden = decode(ref, fresh_ref.shape[1])
        hnum += more
        hden += more_hden
    fresh_ref[...] = fresh_of(hnum, hden, gene_ref, 2)


def spread_kernel(*refs):
    *share_refs, out_ref = refs
    groups = len(share_refs) // 2
    columns = share_refs[0].shape[1]
    tile = lax.axis_index("tile")
    here, side = tile // 2, lax.rem(tile, 2)
    shares = [ref[...].astype(jnp.float32) for ref in share_refs]
    for column in range(2):
        own = side == column
        picked = []
        for group in range(groups):
            distance = here ^ group
            share = jnp.where(own, shares[0], shares[groups])
            for at in range(1, groups):
                either = jnp.where(own, shares[at], shares[groups + at])
                share = jnp.where(distance == at, either, share)
            picked.append(share)
        for group in range(0, groups, 2):
            out_ref[
                group * ROWS : (group + 2) * ROWS, column * columns : (column + 1) * columns
            ] = jnp.concatenate(picked[group : group + 2], axis=0).astype(jnp.bfloat16)


def call(kernel, outs, scratch=(), specs=None, limit=VMEM_BYTES):
    whole = pl.BlockSpec(memory_space=pltpu.VMEM)
    return lambda *args: pl.pallas_call(
        kernel,
        out_shape=outs,
        in_specs=specs or [whole] * len(args),
        out_specs=jax.tree.map(lambda _: whole, outs),
        scratch_shapes=list(scratch),
        compiler_params=pltpu.CompilerParams(vmem_limit_bytes=limit),
    )(*args)


def beside(tiles, halves, offset):
    pairs = []
    paired = set()
    for low in range(offset, tiles - 1, 2):
        paired |= {low, low + 1}
        for gene in range(halves):
            other = (gene + 1) % halves
            pairs.append((low * halves + gene, (low + 1) * halves + other))
            pairs.append(((low + 1) * halves + gene, low * halves + other))
    for tile in range(tiles):
        if tile not in paired:
            for gene in range(halves):
                pairs.append((tile * halves + gene, tile * halves + (gene + 1) % halves))
    return pairs


def on_device(counts, cell_factor, gene_factor, tissue, neighbours):
    rank, width = cell_factor.shape
    genes = gene_factor.shape[1]
    tiles, halves = lax.axis_size("tile"), lax.axis_size("gene")
    flag_row = tissue[None]
    shape = jax.ShapeDtypeStruct
    factor = shape((rank, width), jnp.float32)
    edge = shape((rank + ROWS, LANES), jnp.float32)
    gene_rows = shape((genes, 2 * rank), jnp.bfloat16)
    far = pl.BlockSpec(memory_space=pl.ANY)

    kept = call(
        turn_kernel,
        shape((genes, width), jnp.bfloat16),
        [
            pltpu.VMEM(counts.shape, counts.dtype),
            pltpu.SemaphoreType.DMA((genes // COPY_COLUMNS,)),
        ],
        [far],
        COUNTS_VMEM_BYTES,
    )(counts)
    part, rows = call(
        first_kernel, (shape((rank, width + LANES), jnp.float32), gene_rows)
    )(kept, cell_factor, gene_factor)
    pick = call(pick_kernel, shape((width + LANES, width), jnp.bfloat16))(neighbours)

    def swapped(part):
        if halves == 2:
            return lax.ppermute(part, "gene", [(0, 1), (1, 0)])
        return lax.psum(part, "gene") - part

    def around(updated, edges):
        sides = [
            lax.ppermute(edges, ("tile", "gene"), beside(tiles, halves, offset))
            for offset in (0, 1)
        ]
        return updated, flag_row, *sides, pick, kept

    updated, edges, gsum = call(
        first_update_kernel, (factor, edge, shape((rank, LANES), jnp.float32))
    )(part, swapped(part), cell_factor, flag_row)
    cells, numer = call(next_kernel, (factor, factor))(
        *around(updated, edges), gene_factor, rows
    )
    updated, edges = call(update_kernel, (factor, edge))(
        numer, swapped(numer), gsum, cells, flag_row
    )
    across = tiles * ROWS // rank
    groups = rank // ROWS
    columns = genes // across
    height = share_height(columns)
    last = (*around(updated, edges), rows)
    totals = [pltpu.VMEM((rank, genes + LANES), jnp.float32)]
    if across != 2 or groups != 4 or halves != 2:
        cells, sent = call(
            shares_kernel, (factor, shape((tiles, height, LANES), jnp.int16)), totals
        )(*last)
        got = lax.all_to_all(sent, "tile", 0, 0)
        fresh = call(all_shares_kernel, shape((tiles, ROWS, columns), jnp.bfloat16))(
            got, gene_factor
        )
        every = lax.all_to_all(fresh, "tile", 0, 0).reshape(groups, across, ROWS, columns)
        return cells, every.transpose(0, 2, 1, 3).reshape(rank, genes)

    def moved(array, step, cross):
        pairs = [
            (tile * halves + gene, (tile ^ step) * halves + (gene ^ cross))
            for tile in range(tiles)
            for gene in range(halves)
        ]
        return lax.ppermute(array, ("tile", "gene"), pairs)

    one = shape((height, LANES), jnp.int16)
    cells, *sent, own = call(
        distance_kernel,
        (
            factor,
            *[one] * (groups - 2),
            shape((2 * height, LANES), jnp.int16),
            shape((groups * height, LANES), jnp.int16),
        ),
        totals + [pltpu.VMEM((tiles, height, LANES), jnp.int16)],
    )(*last)
    distances = range(groups - 1, 0, -1)
    own = moved(own, 0, 1)
    got = {distance: moved(sent[distance - 1], 1, 1) for distance in distances}
    got[0] = got[groups - 1]
    summed = []
    for distance in (*distances, 0):
        both = call(functools.partial(column_kernel, distance, columns), one)(
            got[distance], own
        )
        summed.append(moved(both, 2 * distance, 1))
    fresh = call(fresh_kernel, shape((ROWS, columns), jnp.bfloat16))(*summed, gene_factor)
    shares, others = [fresh], [moved(fresh, 1, 0)]
    passing = {distance: moved(fresh, 2 * distance, 1) for distance in distances}
    for distance in range(1, groups):
        shares.append(moved(passing[distance], 0, 1))
        others.append(moved(passing[distance], 1, 1))
    return cells, call(spread_kernel, shape((rank, genes), jnp.bfloat16))(*shares, *others)


def solution(mesh):
    return jax.shard_map(
        on_device,
        mesh=mesh,
        in_specs=(
            P(("grp", "tile"), "gene"),
            P(None, ("grp", "tile")),
            P(None, ("grp", "gene")),
            P(("grp", "tile")),
            P(None, ("grp", "tile")),
        ),
        out_specs=(P(None, ("grp", "tile")), P(None, ("grp", "gene"))),
        check_vma=False,
    )
```

```python
import functools

import jax
import jax.numpy as jnp
from jax import lax
from jax.experimental import pallas as pl
from jax.experimental.pallas import tpu as pltpu
from jax.sharding import PartitionSpec as P

BORDER = 32
LANES = 128
ROWS = 8
STAT_ROWS = 16
FULL = 32767.0
smooth_weight = 0.5
VMEM_BYTES = 24 * 1024 * 1024
COUNTS_VMEM_BYTES = 51 * 1024 * 1024
COPY_COLUMNS = 512


def split(values):
    high = values.astype(jnp.bfloat16)
    low = (values - high.astype(jnp.float32)).astype(jnp.bfloat16)
    return high, low


def piece(total, wanted):
    for size in (4096, 2048, 1024, 512, 256, 128):
        if size <= wanted and total % size == 0:
            return size
    return total


def quarter(width):
    return width // 4


def outer_of(values):
    side = quarter(values.shape[1])
    return jnp.concatenate([values[:, :side], values[:, -side:]], axis=1)


def inner_of(values):
    side = quarter(values.shape[1])
    return values[:, side:-side]


def whole_of(outer, inner):
    side = quarter(2 * outer.shape[1])
    return jnp.concatenate([outer[:, :side], inner, outer[:, side:]], axis=1)


def ratio_of(kept_ref, run, gene_rows, cells):
    factor_rows = jnp.concatenate(split(cells), axis=0)
    product = jnp.dot(gene_rows, factor_rows, preferred_element_type=jnp.float32)
    counts = kept_ref[run].astype(jnp.float32)
    return (counts * pl.reciprocal(product, approx=True)).astype(jnp.bfloat16)


def runs_of(genes, wanted=1024):
    size = piece(genes, wanted)
    return [slice(at, at + size) for at in range(0, genes, size)]


def numerator(gene_ref, run, ratio):
    return jnp.dot(gene_ref[:, run], ratio, preferred_element_type=jnp.float32)


def partner(tile, tiles, offset):
    other = jnp.where((tile + offset) % 2 == 0, tile + 1, tile - 1)
    return jnp.where((other >= 0) & (other < tiles), other, -1)


def pick_kernel(neigh_ref, pick_ref):
    width = neigh_ref.shape[1]
    tiles = lax.axis_size("tile")
    here = lax.axis_index("tile")
    neigh = neigh_ref[...] - here * width
    neigh = jnp.concatenate([outer_of(neigh), inner_of(neigh)], axis=1)

    def found(where):
        total = jnp.zeros((LANES, width), jnp.float32)
        for j in range(neigh.shape[0]):
            total += (neigh[j : j + 1] == where).astype(jnp.float32)
        return total

    row = lax.broadcasted_iota(jnp.int32, (LANES, width), 0)
    for at in range(0, width, LANES):
        pick_ref[at : at + LANES] = found(at + row).astype(jnp.bfloat16)
    slot = row % (2 * BORDER)
    beside = jnp.where(
        row < 2 * BORDER, partner(here, tiles, 0), partner(here, tiles, 1)
    )
    where = (beside - here) * width + slot + jnp.where(slot < BORDER, 0, width - 2 * BORDER)
    pick_ref[width:] = jnp.where(beside < 0, 0.0, found(where)).astype(jnp.bfloat16)


def turn_kernel(counts_ref, outer_ref, inner_ref, landed, sems):
    width, genes = landed.shape
    side = quarter(width)
    copies = []
    for i in range(genes // COPY_COLUMNS):
        columns = pl.ds(i * COPY_COLUMNS, COPY_COLUMNS)
        copies.append(
            pltpu.make_async_copy(
                counts_ref.at[:, columns], landed.at[:, columns], sems.at[i]
            )
        )
    for copy in copies:
        copy.start()
    for i, copy in enumerate(copies):
        copy.wait()
        run = slice(i * COPY_COLUMNS, (i + 1) * COPY_COLUMNS)
        ends = jnp.concatenate([landed[:side, run], landed[width - side :, run]], axis=0)
        outer_ref[run] = ends.astype(jnp.float32).T.astype(jnp.bfloat16)
        middle = landed[side : width - side, run]
        inner_ref[run] = middle.astype(jnp.float32).T.astype(jnp.bfloat16)


def first_kernel(outer_ref, inner_ref, cells_ref, gene_ref, part_ref, rows_ref):
    rank, genes = gene_ref.shape
    width = cells_ref.shape[1]
    cells = cells_ref[...]
    cells = jnp.concatenate([outer_of(cells), inner_of(cells)], axis=1)
    factor_rows = jnp.concatenate(split(cells), axis=0)
    gsum = jnp.zeros((rank, 1), jnp.float32)
    total = jnp.zeros((rank, width), jnp.float32)
    for run in runs_of(genes):
        wide = gene_ref[:, run].astype(jnp.float32)
        gsum += jnp.sum(wide, axis=1, keepdims=True)
        rows = jnp.concatenate([wide, wide], axis=0).T.astype(jnp.bfloat16)
        rows_ref[run] = rows
        product = jnp.dot(rows, factor_rows, preferred_element_type=jnp.float32)
        counts = jnp.concatenate([outer_ref[run], inner_ref[run]], axis=1)
        ratio = counts.astype(jnp.float32) * pl.reciprocal(product, approx=True)
        total += numerator(gene_ref, run, ratio.astype(jnp.bfloat16))
    part_ref[:, :width] = whole_of(total[:, : width // 2], total[:, width // 2 :])
    part_ref[:, width:] = jnp.broadcast_to(gsum, (rank, LANES))


def masked_rows(values, flags):
    flag_rows = jnp.broadcast_to(flags.astype(jnp.float32), (ROWS, flags.shape[1]))
    return jnp.concatenate([jnp.where(flags, values, 0.0), flag_rows], axis=0)


def update_kernel(numer_ref, other_ref, gsum_ref, cells_ref, tissue_ref, updated_ref, edges_ref):
    width = cells_ref.shape[1]
    flags = tissue_ref[...] > 0
    numer = numer_ref[...] + other_ref[...]
    cells = cells_ref[...]
    updated = jnp.where(flags, cells * numer / gsum_ref[:, :1], cells)
    updated_ref[...] = updated
    both = masked_rows(updated, flags)
    edges_ref[:, :BORDER] = both[:, :BORDER]
    edges_ref[:, BORDER : 2 * BORDER] = both[:, width - BORDER :]
    edges_ref[:, 2 * BORDER :] = jnp.zeros_like(edges_ref[:, 2 * BORDER :])


def first_update_kernel(
    part_ref, other_ref, cells_ref, tissue_ref, updated_ref, edges_ref, gsum_ref
):
    width = cells_ref.shape[1]
    gsum_ref[...] = part_ref[:, width:] + other_ref[:, width:]
    update_kernel(
        part_ref.at[:, :width], other_ref.at[:, :width], gsum_ref,
        cells_ref, tissue_ref, updated_ref, edges_ref,
    )


def mixed(updated, flags, near):
    rank = updated.shape[0]
    mean = near[:rank] / jnp.maximum(near[rank : rank + 1], 1.0)
    return jnp.where(
        flags, (1.0 - smooth_weight) * updated + smooth_weight * mean, updated
    )


def picked(values, pick):
    return sum(
        jnp.dot(part, pick, preferred_element_type=jnp.float32) for part in split(values)
    )


def smoothed_inner(updated_ref, tissue_ref, pick_ref):
    updated, tissue = updated_ref[...], tissue_ref[...]
    width = updated.shape[1]
    near = picked(masked_rows(updated, tissue > 0), pick_ref[:width, width // 2 :])
    flags = inner_of(tissue) > 0
    return mixed(inner_of(updated), flags, near), flags


def smoothed_outer(updated_ref, tissue_ref, pick_ref, first_ref, second_ref):
    updated, tissue = updated_ref[...], tissue_ref[...]
    width = updated.shape[1]
    sides = jnp.concatenate(
        [first_ref[:, : 2 * BORDER], second_ref[:, : 2 * BORDER]], axis=1
    )
    near = picked(masked_rows(updated, tissue > 0), pick_ref[:width, : width // 2])
    near += picked(sides, pick_ref[width:, : width // 2])
    flags = outer_of(tissue) > 0
    return mixed(outer_of(updated), flags, near), flags


def inner_kernel(
    updated_ref, tissue_ref, pick_ref, kept_ref, rows_ref, gene_ref, cells_ref, numer_ref
):
    cells, _ = smoothed_inner(updated_ref, tissue_ref, pick_ref)
    cells_ref[...] = cells
    numer_ref[...] = sum(
        numerator(gene_ref, run, ratio_of(kept_ref, run, rows_ref[run], cells))
        for run in runs_of(gene_ref.shape[1], 2048)
    )


def outer_kernel(
    updated_ref, tissue_ref, pick_ref, first_ref, second_ref, kept_ref, rows_ref,
    gene_ref, inner_cells_ref, inner_numer_ref, cells_ref, numer_ref,
):
    cells, _ = smoothed_outer(updated_ref, tissue_ref, pick_ref, first_ref, second_ref)
    cells_ref[...] = whole_of(cells, inner_cells_ref[...])
    numer = sum(
        numerator(gene_ref, run, ratio_of(kept_ref, run, rows_ref[run], cells))
        for run in runs_of(gene_ref.shape[1], 2048)
    )
    numer_ref[...] = whole_of(numer, inner_numer_ref[...])


def exponent(values):
    return jnp.ceil(jnp.log2(jnp.maximum(values, 1e-30)))


def share_height(columns):
    blocks = columns // LANES
    return (blocks + blocks % 2) * ROWS + STAT_ROWS


def encode(values, hden, targets):
    power = exponent(jnp.max(values, axis=1, keepdims=True))
    coded = (values * (jnp.exp2(-power) * FULL) + 0.5).astype(jnp.int32)
    hden_power = exponent(hden)
    scaled = hden * jnp.exp2(-hden_power) * FULL
    high = jnp.floor(scaled)
    low = jnp.floor((scaled - high) * FULL)
    lane = lax.broadcasted_iota(jnp.int32, (values.shape[0], LANES), 1)
    marks = jnp.zeros((values.shape[0], LANES), jnp.float32)
    for at, value in enumerate((power, hden_power, high, low)):
        marks = jnp.where(lane == at, value, marks)
    marks = marks.astype(jnp.int32)
    blank = jnp.zeros((ROWS, LANES), jnp.int32)
    for group, target in enumerate(targets):
        ranks = slice(group * ROWS, (group + 1) * ROWS)
        blocks = [coded[ranks, at : at + LANES] for at in range(0, values.shape[1], LANES)]
        blocks += [blank] * (len(blocks) % 2) + [marks[ranks], blank]
        for i in range(0, len(blocks), 2):
            target[i * ROWS : (i + 2) * ROWS] = jnp.concatenate(
                blocks[i : i + 2], axis=0
            ).astype(jnp.int16)


def decode(source, columns):
    def number(start):
        return source[start : start + 2 * ROWS].astype(jnp.int32).astype(jnp.float32)

    height = source.shape[0]
    marks = number(height - STAT_ROWS)[:ROWS]
    scale = jnp.exp2(marks[:, :1]) / FULL
    hden = (marks[:, 2:3] + marks[:, 3:4] / FULL) * (jnp.exp2(marks[:, 1:2]) / FULL)
    blocks = []
    for start in range(0, height - STAT_ROWS, 2 * ROWS):
        both = number(start)
        blocks += [both[:ROWS] * scale, both[ROWS:] * scale]
    return jnp.concatenate(blocks[: columns // LANES], axis=1), hden


def gene_totals(cells, flags, kept_ref, rows_ref, totals_ref):
    rank = cells.shape[0]
    genes = totals_ref.shape[1] - LANES
    masked = jnp.where(flags, cells, 0.0)
    parts = jnp.concatenate(split(masked), axis=0)
    columns = parts.astype(jnp.float32).T.astype(jnp.bfloat16)
    hden = jnp.sum(masked, axis=1, keepdims=True)
    totals_ref[:, genes:] = jnp.broadcast_to(hden, (rank, LANES))
    for run in runs_of(genes, 1024):
        ratio = ratio_of(kept_ref, run, rows_ref[run], cells)
        total = jnp.dot(ratio, columns, preferred_element_type=jnp.float32).T
        totals_ref[:, run] = total[:rank] + total[rank:]


def inner_totals_kernel(
    updated_ref, tissue_ref, pick_ref, kept_ref, rows_ref, cells_ref, totals_ref
):
    cells, flags = smoothed_inner(updated_ref, tissue_ref, pick_ref)
    cells_ref[...] = cells
    gene_totals(cells, flags, kept_ref, rows_ref, totals_ref)


def last_pass(
    updated_ref, tissue_ref, pick_ref, first_ref, second_ref, kept_ref, rows_ref,
    inner_cells_ref, inner_totals_ref, cells_ref, totals_ref,
):
    cells, flags = smoothed_outer(updated_ref, tissue_ref, pick_ref, first_ref, second_ref)
    cells_ref[...] = whole_of(cells, inner_cells_ref[...])
    gene_totals(cells, flags, kept_ref, rows_ref, totals_ref)
    totals_ref[...] += inner_totals_ref[...]


def encode_tiles(totals_ref, sent_ref):
    rank, genes = totals_ref.shape[0], totals_ref.shape[1] - LANES
    tiles = sent_ref.shape[0]
    across = tiles * ROWS // rank
    columns = genes // across
    for column in range(across):
        encode(
            totals_ref[:, column * columns : (column + 1) * columns],
            totals_ref[:, genes : genes + 1],
            [sent_ref.at[tile] for tile in range(column, tiles, across)],
        )


def shares_kernel(*refs):
    *passed, sent_ref, totals_ref = refs
    last_pass(*passed, totals_ref)
    encode_tiles(totals_ref, sent_ref)


def distance_kernel(*refs):
    passed, (*sent_refs, own_ref, totals_ref, coded_ref) = refs[:10], refs[10:]
    last_pass(*passed, totals_ref)
    tiles, height, _ = coded_ref.shape
    encode_tiles(totals_ref, coded_ref)
    tile = lax.axis_index("tile")
    for distance in range(tiles // 2):
        there = tile ^ (2 * distance)
        own_ref[distance * height : (distance + 1) * height] = coded_ref[there]
        place = sent_refs[(distance or tiles // 2 - 1) - 1]
        start = 0 if distance else height
        place[start : start + height] = coded_ref[there ^ 1]


def column_kernel(distance, columns, got_ref, own_ref, sent_ref):
    height = sent_ref.shape[0]
    start = 0 if distance else height
    values, hden = decode(got_ref.at[start : start + height], columns)
    start = height * distance
    more, more_hden = decode(own_ref.at[start : start + height], columns)
    encode(values + more, hden + more_hden, [sent_ref])


def fresh_of(hnum, hden, gene_ref, across):
    columns = hnum.shape[1]
    here = lax.axis_index("tile")
    place = pl.multiple_of(lax.rem(here, across) * columns, LANES)
    every = gene_ref[:, pl.ds(place, columns)].astype(jnp.float32)
    hf = every[:ROWS]
    for group in range(1, gene_ref.shape[0] // ROWS):
        hf = jnp.where(here // across == group, every[group * ROWS : (group + 1) * ROWS], hf)
    return (hf * hnum / hden).astype(jnp.bfloat16)


def all_shares_kernel(got_ref, gene_ref, fresh_ref):
    tiles, _, columns = fresh_ref.shape
    hnum, hden = decode(got_ref.at[0], columns)
    for tile in range(1, tiles):
        more, more_hden = decode(got_ref.at[tile], columns)
        hnum += more
        hden += more_hden
    fresh = fresh_of(hnum, hden, gene_ref, tiles * ROWS // gene_ref.shape[0])
    for tile in range(tiles):
        fresh_ref[tile] = fresh


def fresh_kernel(*refs):
    *got_refs, gene_ref, fresh_ref = refs
    hnum, hden = 0.0, 0.0
    for ref in got_refs:
        more, more_hden = decode(ref, fresh_ref.shape[1])
        hnum += more
        hden += more_hden
    fresh_ref[...] = fresh_of(hnum, hden, gene_ref, 2)


def spread_kernel(*refs):
    *share_refs, out_ref = refs
    groups = len(share_refs) // 2
    columns = share_refs[0].shape[1]
    tile = lax.axis_index("tile")
    here, side = tile // 2, lax.rem(tile, 2)
    shares = [ref[...].astype(jnp.float32) for ref in share_refs]
    for column in range(2):
        own = side == column
        picked = []
        for group in range(groups):
            distance = here ^ group
            share = jnp.where(own, shares[0], shares[groups])
            for at in range(1, groups):
                either = jnp.where(own, shares[at], shares[groups + at])
                share = jnp.where(distance == at, either, share)
            picked.append(share)
        for group in range(0, groups, 2):
            out_ref[
                group * ROWS : (group + 2) * ROWS, column * columns : (column + 1) * columns
            ] = jnp.concatenate(picked[group : group + 2], axis=0).astype(jnp.bfloat16)


def call(kernel, outs, scratch=(), specs=None, limit=VMEM_BYTES):
    whole = pl.BlockSpec(memory_space=pltpu.VMEM)
    return lambda *args: pl.pallas_call(
        kernel,
        out_shape=outs,
        in_specs=specs or [whole] * len(args),
        out_specs=jax.tree.map(lambda _: whole, outs),
        scratch_shapes=list(scratch),
        compiler_params=pltpu.CompilerParams(vmem_limit_bytes=limit),
    )(*args)


def beside(tiles, halves, offset):
    pairs = []
    paired = set()
    for low in range(offset, tiles - 1, 2):
        paired |= {low, low + 1}
        for gene in range(halves):
            other = (gene + 1) % halves
            pairs.append((low * halves + gene, (low + 1) * halves + other))
            pairs.append(((low + 1) * halves + gene, low * halves + other))
    for tile in range(tiles):
        if tile not in paired:
            for gene in range(halves):
                pairs.append((tile * halves + gene, tile * halves + (gene + 1) % halves))
    return pairs


def on_device(counts, cell_factor, gene_factor, tissue, neighbours):
    rank, width = cell_factor.shape
    genes = gene_factor.shape[1]
    tiles, halves = lax.axis_size("tile"), lax.axis_size("gene")
    flag_row = tissue[None]
    shape = jax.ShapeDtypeStruct
    factor = shape((rank, width), jnp.float32)
    edge = shape((rank + ROWS, LANES), jnp.float32)
    half = shape((rank, width // 2), jnp.float32)
    half_kept = shape((genes, width // 2), jnp.bfloat16)
    gene_rows = shape((genes, 2 * rank), jnp.bfloat16)
    far = pl.BlockSpec(memory_space=pl.ANY)

    outer, inner = call(
        turn_kernel,
        (half_kept, half_kept),
        [
            pltpu.VMEM(counts.shape, counts.dtype),
            pltpu.SemaphoreType.DMA((genes // COPY_COLUMNS,)),
        ],
        [far],
        COUNTS_VMEM_BYTES,
    )(counts)
    part, rows = call(
        first_kernel, (shape((rank, width + LANES), jnp.float32), gene_rows)
    )(outer, inner, cell_factor, gene_factor)
    pick = call(pick_kernel, shape((width + LANES, width), jnp.bfloat16))(neighbours)

    def swapped(part):
        if halves == 2:
            return lax.ppermute(part, "gene", [(0, 1), (1, 0)])
        return lax.psum(part, "gene") - part

    def around(edges):
        return [
            lax.ppermute(edges, ("tile", "gene"), beside(tiles, halves, offset))
            for offset in (0, 1)
        ]

    updated, edges, gsum = call(
        first_update_kernel, (factor, edge, shape((rank, LANES), jnp.float32))
    )(part, swapped(part), cell_factor, flag_row)
    inner_of_both = call(inner_kernel, (half, half))(
        updated, flag_row, pick, inner, rows, gene_factor
    )
    cells, numer = call(outer_kernel, (factor, factor))(
        updated, flag_row, pick, *around(edges), outer, rows, gene_factor, *inner_of_both
    )
    updated, edges = call(update_kernel, (factor, edge))(
        numer, swapped(numer), gsum, cells, flag_row
    )
    across = tiles * ROWS // rank
    groups = rank // ROWS
    columns = genes // across
    height = share_height(columns)
    inner_of_both = call(
        inner_totals_kernel, (half, shape((rank, genes + LANES), jnp.float32))
    )(updated, flag_row, pick, inner, rows)
    last = (updated, flag_row, pick, *around(edges), outer, rows, *inner_of_both)
    totals = [pltpu.VMEM((rank, genes + LANES), jnp.float32)]
    if across != 2 or groups != 4 or halves != 2:
        cells, sent = call(
            shares_kernel, (factor, shape((tiles, height, LANES), jnp.int16)), totals
        )(*last)
        got = lax.all_to_all(sent, "tile", 0, 0)
        fresh = call(all_shares_kernel, shape((tiles, ROWS, columns), jnp.bfloat16))(
            got, gene_factor
        )
        every = lax.all_to_all(fresh, "tile", 0, 0).reshape(groups, across, ROWS, columns)
        return cells, every.transpose(0, 2, 1, 3).reshape(rank, genes)

    def moved(array, step, cross):
        pairs = [
            (tile * halves + gene, (tile ^ step) * halves + (gene ^ cross))
            for tile in range(tiles)
            for gene in range(halves)
        ]
        return lax.ppermute(array, ("tile", "gene"), pairs)

    one = shape((height, LANES), jnp.int16)
    cells, *sent, own = call(
        distance_kernel,
        (
            factor,
            *[one] * (groups - 2),
            shape((2 * height, LANES), jnp.int16),
            shape((groups * height, LANES), jnp.int16),
        ),
        totals + [pltpu.VMEM((tiles, height, LANES), jnp.int16)],
    )(*last)
    distances = range(groups - 1, 0, -1)
    own = moved(own, 0, 1)
    got = {distance: moved(sent[distance - 1], 1, 1) for distance in distances}
    got[0] = got[groups - 1]
    summed = []
    for distance in (*distances, 0):
        both = call(functools.partial(column_kernel, distance, columns), one)(
            got[distance], own
        )
        summed.append(moved(both, 2 * distance, 1))
    fresh = call(fresh_kernel, shape((ROWS, columns), jnp.bfloat16))(*summed, gene_factor)
    shares, others = [fresh], [moved(fresh, 1, 0)]
    passing = {distance: moved(fresh, 2 * distance, 1) for distance in distances}
    for distance in range(1, groups):
        shares.append(moved(passing[distance], 0, 1))
        others.append(moved(passing[distance], 1, 1))
    return cells, call(spread_kernel, shape((rank, genes), jnp.bfloat16))(*shares, *others)


def solution(mesh):
    return jax.shard_map(
        on_device,
        mesh=mesh,
        in_specs=(
            P(("grp", "tile"), "gene"),
            P(None, ("grp", "tile")),
            P(None, ("grp", "gene")),
            P(("grp", "tile")),
            P(None, ("grp", "tile")),
        ),
        out_specs=(P(None, ("grp", "tile")), P(None, ("grp", "gene"))),
        check_vma=False,
    )
```

```python
import functools

import jax
import jax.numpy as jnp
from jax import lax
from jax.experimental import pallas as pl
from jax.experimental.pallas import tpu as pltpu
from jax.sharding import PartitionSpec as P

BORDER = 32
LANES = 128
ROWS = 8
STAT_ROWS = 16
FULL = 32767.0
smooth_weight = 0.5
VMEM_BYTES = 24 * 1024 * 1024
COUNTS_VMEM_BYTES = 51 * 1024 * 1024
COPY_COLUMNS = 512


def split(values):
    high = values.astype(jnp.bfloat16)
    low = (values - high.astype(jnp.float32)).astype(jnp.bfloat16)
    return high, low


def piece(total, wanted):
    for size in (4096, 2048, 1024, 512, 256, 128):
        if size <= wanted and total % size == 0:
            return size
    return total


def quarter(width):
    return width // 4


def outer_of(values):
    side = quarter(values.shape[1])
    return jnp.concatenate([values[:, :side], values[:, -side:]], axis=1)


def inner_of(values):
    side = quarter(values.shape[1])
    return values[:, side:-side]


def whole_of(outer, inner):
    side = quarter(2 * outer.shape[1])
    return jnp.concatenate([outer[:, :side], inner, outer[:, side:]], axis=1)


def ratio_of(kept_ref, run, gene_rows, cells):
    factor_rows = jnp.concatenate(split(cells), axis=0)
    product = jnp.dot(gene_rows, factor_rows, preferred_element_type=jnp.float32)
    counts = kept_ref[run].astype(jnp.float32)
    return (counts * pl.reciprocal(product, approx=True)).astype(jnp.bfloat16)


def runs_of(genes, wanted=1024):
    size = piece(genes, wanted)
    return [slice(at, at + size) for at in range(0, genes, size)]


def numerator(gene_ref, run, ratio):
    return jnp.dot(gene_ref[:, run], ratio, preferred_element_type=jnp.float32)


def partner(tile, tiles, offset):
    other = jnp.where((tile + offset) % 2 == 0, tile + 1, tile - 1)
    return jnp.where((other >= 0) & (other < tiles), other, -1)


def pick_kernel(neigh_ref, pick_ref):
    width = neigh_ref.shape[1]
    tiles = lax.axis_size("tile")
    here = lax.axis_index("tile")
    neigh = neigh_ref[...] - here * width
    neigh = jnp.concatenate([outer_of(neigh), inner_of(neigh)], axis=1)

    def found(where):
        total = jnp.zeros((LANES, width), jnp.float32)
        for j in range(neigh.shape[0]):
            total += (neigh[j : j + 1] == where).astype(jnp.float32)
        return total

    row = lax.broadcasted_iota(jnp.int32, (LANES, width), 0)
    for at in range(0, width, LANES):
        pick_ref[at : at + LANES] = found(at + row).astype(jnp.bfloat16)
    slot = row % (2 * BORDER)
    beside = jnp.where(
        row < 2 * BORDER, partner(here, tiles, 0), partner(here, tiles, 1)
    )
    where = (beside - here) * width + slot + jnp.where(slot < BORDER, 0, width - 2 * BORDER)
    pick_ref[width:] = jnp.where(beside < 0, 0.0, found(where)).astype(jnp.bfloat16)


def turn_kernel(counts_ref, outer_ref, inner_ref, landed, sems):
    width, genes = landed.shape
    side = quarter(width)
    copies = []
    for i in range(genes // COPY_COLUMNS):
        columns = pl.ds(i * COPY_COLUMNS, COPY_COLUMNS)
        copies.append(
            pltpu.make_async_copy(
                counts_ref.at[:, columns], landed.at[:, columns], sems.at[i]
            )
        )
    for copy in copies:
        copy.start()
    for i, copy in enumerate(copies):
        copy.wait()
        run = slice(i * COPY_COLUMNS, (i + 1) * COPY_COLUMNS)
        ends = jnp.concatenate([landed[:side, run], landed[width - side :, run]], axis=0)
        outer_ref[run] = ends.astype(jnp.float32).T.astype(jnp.bfloat16)
        middle = landed[side : width - side, run]
        inner_ref[run] = middle.astype(jnp.float32).T.astype(jnp.bfloat16)


def first_kernel(outer_ref, inner_ref, cells_ref, gene_ref, part_ref, rows_ref):
    rank, genes = gene_ref.shape
    width = cells_ref.shape[1]
    cells = cells_ref[...]
    cells = jnp.concatenate([outer_of(cells), inner_of(cells)], axis=1)
    factor_rows = jnp.concatenate(split(cells), axis=0)
    gsum = jnp.zeros((rank, 1), jnp.float32)
    total = jnp.zeros((rank, width), jnp.float32)
    for run in runs_of(genes):
        wide = gene_ref[:, run].astype(jnp.float32)
        gsum += jnp.sum(wide, axis=1, keepdims=True)
        rows = jnp.concatenate([wide, wide], axis=0).T.astype(jnp.bfloat16)
        rows_ref[run] = rows
        product = jnp.dot(rows, factor_rows, preferred_element_type=jnp.float32)
        counts = jnp.concatenate([outer_ref[run], inner_ref[run]], axis=1)
        ratio = counts.astype(jnp.float32) * pl.reciprocal(product, approx=True)
        total += numerator(gene_ref, run, ratio.astype(jnp.bfloat16))
    part_ref[:, :width] = whole_of(total[:, : width // 2], total[:, width // 2 :])
    part_ref[:, width:] = jnp.broadcast_to(gsum, (rank, LANES))


def masked_rows(values, flags):
    flag_rows = jnp.broadcast_to(flags.astype(jnp.float32), (ROWS, flags.shape[1]))
    return jnp.concatenate([jnp.where(flags, values, 0.0), flag_rows], axis=0)


def update_kernel(numer_ref, other_ref, gsum_ref, cells_ref, tissue_ref, updated_ref, edges_ref):
    width = cells_ref.shape[1]
    flags = tissue_ref[...] > 0
    numer = numer_ref[...] + other_ref[...]
    cells = cells_ref[...]
    updated = jnp.where(flags, cells * numer / gsum_ref[:, :1], cells)
    updated_ref[...] = updated
    both = masked_rows(updated, flags)
    edges_ref[:, :BORDER] = both[:, :BORDER]
    edges_ref[:, BORDER : 2 * BORDER] = both[:, width - BORDER :]
    edges_ref[:, 2 * BORDER :] = jnp.zeros_like(edges_ref[:, 2 * BORDER :])


def first_update_kernel(
    part_ref, other_ref, cells_ref, tissue_ref, _, updated_ref, edges_ref, gsum_ref
):
    width = cells_ref.shape[1]
    gsum_ref[...] = part_ref[:, width:] + other_ref[:, width:]
    update_kernel(
        part_ref.at[:, :width], other_ref.at[:, :width], gsum_ref,
        cells_ref, tissue_ref, updated_ref, edges_ref,
    )


def mixed(updated, flags, near):
    rank = updated.shape[0]
    mean = near[:rank] / jnp.maximum(near[rank : rank + 1], 1.0)
    return jnp.where(
        flags, (1.0 - smooth_weight) * updated + smooth_weight * mean, updated
    )


def picked(values, pick):
    return sum(
        jnp.dot(part, pick, preferred_element_type=jnp.float32) for part in split(values)
    )


def smoothed_inner(updated_ref, tissue_ref, pick_ref):
    updated, tissue = updated_ref[...], tissue_ref[...]
    width = updated.shape[1]
    near = picked(masked_rows(updated, tissue > 0), pick_ref[:width, width // 2 :])
    flags = inner_of(tissue) > 0
    return mixed(inner_of(updated), flags, near), flags


def smoothed_outer(updated_ref, tissue_ref, pick_ref, first_ref, second_ref):
    updated, tissue = updated_ref[...], tissue_ref[...]
    width = updated.shape[1]
    sides = jnp.concatenate(
        [first_ref[:, : 2 * BORDER], second_ref[:, : 2 * BORDER]], axis=1
    )
    near = picked(masked_rows(updated, tissue > 0), pick_ref[:width, : width // 2])
    near += picked(sides, pick_ref[width:, : width // 2])
    flags = outer_of(tissue) > 0
    return mixed(outer_of(updated), flags, near), flags


def inner_kernel(
    updated_ref, tissue_ref, pick_ref, kept_ref, rows_ref, gene_ref, cells_ref, numer_ref
):
    cells, _ = smoothed_inner(updated_ref, tissue_ref, pick_ref)
    cells_ref[...] = cells
    numer_ref[...] = sum(
        numerator(gene_ref, run, ratio_of(kept_ref, run, rows_ref[run], cells))
        for run in runs_of(gene_ref.shape[1], 2048)
    )


def outer_kernel(
    updated_ref, tissue_ref, pick_ref, first_ref, second_ref, kept_ref, rows_ref,
    gene_ref, inner_cells_ref, inner_numer_ref, cells_ref, numer_ref,
):
    cells, _ = smoothed_outer(updated_ref, tissue_ref, pick_ref, first_ref, second_ref)
    cells_ref[...] = whole_of(cells, inner_cells_ref[...])
    numer = sum(
        numerator(gene_ref, run, ratio_of(kept_ref, run, rows_ref[run], cells))
        for run in runs_of(gene_ref.shape[1], 2048)
    )
    numer_ref[...] = whole_of(numer, inner_numer_ref[...])


def exponent(values):
    return jnp.ceil(jnp.log2(jnp.maximum(values, 1e-30)))


def share_height(columns):
    blocks = columns // LANES
    return (blocks + blocks % 2) * ROWS + STAT_ROWS


def encode(values, hden, targets):
    power = exponent(jnp.max(values, axis=1, keepdims=True))
    coded = (values * (jnp.exp2(-power) * FULL) + 0.5).astype(jnp.int32)
    hden_power = exponent(hden)
    scaled = hden * jnp.exp2(-hden_power) * FULL
    high = jnp.floor(scaled)
    low = jnp.floor((scaled - high) * FULL)
    lane = lax.broadcasted_iota(jnp.int32, (values.shape[0], LANES), 1)
    marks = jnp.zeros((values.shape[0], LANES), jnp.float32)
    for at, value in enumerate((power, hden_power, high, low)):
        marks = jnp.where(lane == at, value, marks)
    marks = marks.astype(jnp.int32)
    blank = jnp.zeros((ROWS, LANES), jnp.int32)
    for group, target in enumerate(targets):
        ranks = slice(group * ROWS, (group + 1) * ROWS)
        blocks = [coded[ranks, at : at + LANES] for at in range(0, values.shape[1], LANES)]
        blocks += [blank] * (len(blocks) % 2) + [marks[ranks], blank]
        for i in range(0, len(blocks), 2):
            target[i * ROWS : (i + 2) * ROWS] = jnp.concatenate(
                blocks[i : i + 2], axis=0
            ).astype(jnp.int16)


def decode(source, columns):
    def number(start):
        return source[start : start + 2 * ROWS].astype(jnp.int32).astype(jnp.float32)

    height = source.shape[0]
    marks = number(height - STAT_ROWS)[:ROWS]
    scale = jnp.exp2(marks[:, :1]) / FULL
    hden = (marks[:, 2:3] + marks[:, 3:4] / FULL) * (jnp.exp2(marks[:, 1:2]) / FULL)
    blocks = []
    for start in range(0, height - STAT_ROWS, 2 * ROWS):
        both = number(start)
        blocks += [both[:ROWS] * scale, both[ROWS:] * scale]
    return jnp.concatenate(blocks[: columns // LANES], axis=1), hden


def gene_totals(cells, flags, kept_ref, rows_ref, totals_ref, others_ref=None):
    def put(columns, values):
        if others_ref is not None:
            values += others_ref[:, columns]
        totals_ref[:, columns] = values

    rank = cells.shape[0]
    genes = totals_ref.shape[1] - LANES
    masked = jnp.where(flags, cells, 0.0)
    parts = jnp.concatenate(split(masked), axis=0)
    columns = parts.astype(jnp.float32).T.astype(jnp.bfloat16)
    hden = jnp.sum(masked, axis=1, keepdims=True)
    put(slice(genes, genes + LANES), jnp.broadcast_to(hden, (rank, LANES)))
    for run in runs_of(genes, 1024):
        ratio = ratio_of(kept_ref, run, rows_ref[run], cells)
        total = jnp.dot(ratio, columns, preferred_element_type=jnp.float32).T
        put(run, total[:rank] + total[rank:])


def inner_totals_kernel(
    updated_ref, tissue_ref, pick_ref, kept_ref, rows_ref, cells_ref, totals_ref
):
    cells, flags = smoothed_inner(updated_ref, tissue_ref, pick_ref)
    cells_ref[...] = cells
    gene_totals(cells, flags, kept_ref, rows_ref, totals_ref)


def last_pass(
    updated_ref, tissue_ref, pick_ref, first_ref, second_ref, kept_ref, rows_ref,
    inner_cells_ref, inner_totals_ref, cells_ref, totals_ref,
):
    cells, flags = smoothed_outer(updated_ref, tissue_ref, pick_ref, first_ref, second_ref)
    cells_ref[...] = whole_of(cells, inner_cells_ref[...])
    gene_totals(cells, flags, kept_ref, rows_ref, totals_ref, inner_totals_ref)


def encode_tiles(totals_ref, sent_ref):
    rank, genes = totals_ref.shape[0], totals_ref.shape[1] - LANES
    tiles = sent_ref.shape[0]
    across = tiles * ROWS // rank
    columns = genes // across
    for column in range(across):
        encode(
            totals_ref[:, column * columns : (column + 1) * columns],
            totals_ref[:, genes : genes + 1],
            [sent_ref.at[tile] for tile in range(column, tiles, across)],
        )


def shares_kernel(*refs):
    *passed, sent_ref, totals_ref = refs
    last_pass(*passed, totals_ref)
    encode_tiles(totals_ref, sent_ref)


def distance_kernel(*refs):
    passed, (*sent_refs, own_ref, totals_ref, coded_ref) = refs[:10], refs[10:]
    last_pass(*passed, totals_ref)
    tiles, height, _ = coded_ref.shape
    encode_tiles(totals_ref, coded_ref)
    tile = lax.axis_index("tile")
    for distance in range(tiles // 2):
        there = tile ^ (2 * distance)
        own_ref[distance * height : (distance + 1) * height] = coded_ref[there]
        place = sent_refs[(distance or tiles // 2 - 1) - 1]
        start = 0 if distance else height
        place[start : start + height] = coded_ref[there ^ 1]


def column_kernel(distance, columns, got_ref, own_ref, *refs):
    sent_ref = refs[-1]
    height = sent_ref.shape[0]
    start = 0 if distance else height
    values, hden = decode(got_ref.at[start : start + height], columns)
    start = height * distance
    more, more_hden = decode(own_ref.at[start : start + height], columns)
    encode(values + more, hden + more_hden, [sent_ref])


def fresh_of(hnum, hden, gene_ref, across):
    columns = hnum.shape[1]
    here = lax.axis_index("tile")
    place = pl.multiple_of(lax.rem(here, across) * columns, LANES)
    every = gene_ref[:, pl.ds(place, columns)].astype(jnp.float32)
    hf = every[:ROWS]
    for group in range(1, gene_ref.shape[0] // ROWS):
        hf = jnp.where(here // across == group, every[group * ROWS : (group + 1) * ROWS], hf)
    return (hf * hnum / hden).astype(jnp.bfloat16)


def all_shares_kernel(got_ref, gene_ref, fresh_ref):
    tiles, _, columns = fresh_ref.shape
    hnum, hden = decode(got_ref.at[0], columns)
    for tile in range(1, tiles):
        more, more_hden = decode(got_ref.at[tile], columns)
        hnum += more
        hden += more_hden
    fresh = fresh_of(hnum, hden, gene_ref, tiles * ROWS // gene_ref.shape[0])
    for tile in range(tiles):
        fresh_ref[tile] = fresh


def fresh_kernel(*refs):
    *got_refs, gene_ref, fresh_ref = refs
    hnum, hden = 0.0, 0.0
    for ref in got_refs:
        more, more_hden = decode(ref, fresh_ref.shape[1])
        hnum += more
        hden += more_hden
    fresh_ref[...] = fresh_of(hnum, hden, gene_ref, 2)


def spread_kernel(*refs):
    *share_refs, out_ref = refs
    groups = len(share_refs) // 2
    columns = share_refs[0].shape[1]
    tile = lax.axis_index("tile")
    here, side = tile // 2, lax.rem(tile, 2)
    shares = [ref[...].astype(jnp.float32) for ref in share_refs]
    for column in range(2):
        own = side == column
        picked = []
        for group in range(groups):
            distance = here ^ group
            share = jnp.where(own, shares[0], shares[groups])
            for at in range(1, groups):
                either = jnp.where(own, shares[at], shares[groups + at])
                share = jnp.where(distance == at, either, share)
            picked.append(share)
        for group in range(0, groups, 2):
            out_ref[
                group * ROWS : (group + 2) * ROWS, column * columns : (column + 1) * columns
            ] = jnp.concatenate(picked[group : group + 2], axis=0).astype(jnp.bfloat16)


def call(kernel, outs, scratch=(), specs=None, limit=VMEM_BYTES):
    whole = pl.BlockSpec(memory_space=pltpu.VMEM)
    return lambda *args: pl.pallas_call(
        kernel,
        out_shape=outs,
        in_specs=specs or [whole] * len(args),
        out_specs=jax.tree.map(lambda _: whole, outs),
        scratch_shapes=list(scratch),
        compiler_params=pltpu.CompilerParams(vmem_limit_bytes=limit),
    )(*args)


def beside(tiles, halves, offset):
    pairs = []
    paired = set()
    for low in range(offset, tiles - 1, 2):
        paired |= {low, low + 1}
        for gene in range(halves):
            other = (gene + 1) % halves
            pairs.append((low * halves + gene, (low + 1) * halves + other))
            pairs.append(((low + 1) * halves + gene, low * halves + other))
    for tile in range(tiles):
        if tile not in paired:
            for gene in range(halves):
                pairs.append((tile * halves + gene, tile * halves + (gene + 1) % halves))
    return pairs


def on_device(counts, cell_factor, gene_factor, tissue, neighbours):
    rank, width = cell_factor.shape
    genes = gene_factor.shape[1]
    tiles, halves = lax.axis_size("tile"), lax.axis_size("gene")
    flag_row = tissue[None]
    shape = jax.ShapeDtypeStruct
    factor = shape((rank, width), jnp.float32)
    edge = shape((rank + ROWS, LANES), jnp.float32)
    half = shape((rank, width // 2), jnp.float32)
    half_kept = shape((genes, width // 2), jnp.bfloat16)
    gene_rows = shape((genes, 2 * rank), jnp.bfloat16)
    far = pl.BlockSpec(memory_space=pl.ANY)
    near = pl.BlockSpec(memory_space=pltpu.VMEM)

    outer, inner = call(
        turn_kernel,
        (half_kept, half_kept),
        [
            pltpu.VMEM(counts.shape, counts.dtype),
            pltpu.SemaphoreType.DMA((genes // COPY_COLUMNS,)),
        ],
        [far],
        COUNTS_VMEM_BYTES,
    )(counts)
    part, rows = call(
        first_kernel, (shape((rank, width + LANES), jnp.float32), gene_rows)
    )(outer, inner, cell_factor, gene_factor)
    pick = call(pick_kernel, shape((width + LANES, width), jnp.bfloat16))(neighbours)

    def swapped(part):
        if halves == 2:
            return lax.ppermute(part, "gene", [(0, 1), (1, 0)])
        return lax.psum(part, "gene") - part

    def around(edges):
        return [
            lax.ppermute(edges, ("tile", "gene"), beside(tiles, halves, offset))
            for offset in (0, 1)
        ]

    updated, edges, gsum = call(
        first_update_kernel,
        (factor, edge, shape((rank, LANES), jnp.float32)),
        specs=[near] * 4 + [far],
    )(part, swapped(part), cell_factor, flag_row, pick)
    inner_of_both = call(inner_kernel, (half, half))(
        updated, flag_row, pick, inner, rows, gene_factor
    )
    cells, numer = call(outer_kernel, (factor, factor))(
        updated, flag_row, pick, *around(edges), outer, rows, gene_factor, *inner_of_both
    )
    updated, edges = call(update_kernel, (factor, edge))(
        numer, swapped(numer), gsum, cells, flag_row
    )
    across = tiles * ROWS // rank
    groups = rank // ROWS
    columns = genes // across
    height = share_height(columns)
    inner_of_both = call(
        inner_totals_kernel, (half, shape((rank, genes + LANES), jnp.float32))
    )(updated, flag_row, pick, inner, rows)
    last = (updated, flag_row, pick, *around(edges), outer, rows, *inner_of_both)
    totals = [pltpu.VMEM((rank, genes + LANES), jnp.float32)]
    if across != 2 or groups != 4 or halves != 2:
        cells, sent = call(
            shares_kernel, (factor, shape((tiles, height, LANES), jnp.int16)), totals
        )(*last)
        got = lax.all_to_all(sent, "tile", 0, 0)
        fresh = call(all_shares_kernel, shape((tiles, ROWS, columns), jnp.bfloat16))(
            got, gene_factor
        )
        every = lax.all_to_all(fresh, "tile", 0, 0).reshape(groups, across, ROWS, columns)
        return cells, every.transpose(0, 2, 1, 3).reshape(rank, genes)

    def moved(array, step, cross):
        pairs = [
            (tile * halves + gene, (tile ^ step) * halves + (gene ^ cross))
            for tile in range(tiles)
            for gene in range(halves)
        ]
        return lax.ppermute(array, ("tile", "gene"), pairs)

    one = shape((height, LANES), jnp.int16)
    cells, *sent, own = call(
        distance_kernel,
        (
            factor,
            *[one] * (groups - 2),
            shape((2 * height, LANES), jnp.int16),
            shape((groups * height, LANES), jnp.int16),
        ),
        totals + [pltpu.VMEM((tiles, height, LANES), jnp.int16)],
    )(*last)
    distances = range(groups - 1, 0, -1)
    own = moved(own, 0, 1)
    got = {distance: moved(sent[distance - 1], 1, 1) for distance in distances}
    got[0] = got[groups - 1]
    summed = []
    for distance in (*distances, 0):
        after = () if distance else summed[:1]
        both = call(
            functools.partial(column_kernel, distance, columns), one,
            specs=[near] * 2 + [far] * len(after),
        )(got[distance], own, *after)
        summed.append(moved(both, 2 * distance, 1))
    fresh = call(fresh_kernel, shape((ROWS, columns), jnp.bfloat16))(*summed, gene_factor)
    shares, others = [fresh], [moved(fresh, 1, 0)]
    passing = {distance: moved(fresh, 2 * distance, 1) for distance in distances}
    for distance in range(1, groups):
        shares.append(moved(passing[distance], 0, 1))
        others.append(moved(passing[distance], 1, 1))
    return cells, call(spread_kernel, shape((rank, genes), jnp.bfloat16))(*shares, *others)


def solution(mesh):
    return jax.shard_map(
        on_device,
        mesh=mesh,
        in_specs=(
            P(("grp", "tile"), "gene"),
            P(None, ("grp", "tile")),
            P(None, ("grp", "gene")),
            P(("grp", "tile")),
            P(None, ("grp", "tile")),
        ),
        out_specs=(P(None, ("grp", "tile")), P(None, ("grp", "gene"))),
        check_vma=False,
    )
```

```python
import functools

import jax
import jax.numpy as jnp
from jax import lax
from jax.experimental import pallas as pl
from jax.experimental.pallas import tpu as pltpu
from jax.sharding import PartitionSpec as P

BORDER = 32
LANES = 128
ROWS = 8
STAT_ROWS = 16
FULL = 32767.0
smooth_weight = 0.5
VMEM_BYTES = 24 * 1024 * 1024
COUNTS_VMEM_BYTES = 51 * 1024 * 1024
COPY_COLUMNS = 512


def split(values):
    high = values.astype(jnp.bfloat16)
    low = (values - high.astype(jnp.float32)).astype(jnp.bfloat16)
    return high, low


def piece(total, wanted):
    for size in (4096, 2048, 1024, 512, 256, 128):
        if size <= wanted and total % size == 0:
            return size
    return total


def quarter(width):
    return width // 4


def outer_of(values):
    side = quarter(values.shape[1])
    return jnp.concatenate([values[:, :side], values[:, -side:]], axis=1)


def inner_of(values):
    side = quarter(values.shape[1])
    return values[:, side:-side]


def whole_of(outer, inner):
    side = quarter(2 * outer.shape[1])
    return jnp.concatenate([outer[:, :side], inner, outer[:, side:]], axis=1)


def ratio_of(kept_ref, run, gene_rows, cells):
    factor_rows = jnp.concatenate(split(cells), axis=0)
    product = jnp.dot(gene_rows, factor_rows, preferred_element_type=jnp.float32)
    counts = kept_ref[run].astype(jnp.float32)
    return (counts * pl.reciprocal(product, approx=True)).astype(jnp.bfloat16)


def runs_of(genes, wanted=1024):
    size = piece(genes, wanted)
    return [slice(at, at + size) for at in range(0, genes, size)]


def numerator(gene_ref, run, ratio):
    return jnp.dot(gene_ref[:, run], ratio, preferred_element_type=jnp.float32)


def partner(tile, tiles, offset):
    other = jnp.where((tile + offset) % 2 == 0, tile + 1, tile - 1)
    return jnp.where((other >= 0) & (other < tiles), other, -1)


def pick_kernel(neigh_ref, pick_ref):
    width = neigh_ref.shape[1]
    tiles = lax.axis_size("tile")
    here = lax.axis_index("tile")
    neigh = neigh_ref[...] - here * width
    neigh = jnp.concatenate([outer_of(neigh), inner_of(neigh)], axis=1)

    def found(where):
        total = jnp.zeros((LANES, width), jnp.float32)
        for j in range(neigh.shape[0]):
            total += (neigh[j : j + 1] == where).astype(jnp.float32)
        return total

    row = lax.broadcasted_iota(jnp.int32, (LANES, width), 0)
    for at in range(0, width, LANES):
        pick_ref[at : at + LANES] = found(at + row).astype(jnp.bfloat16)
    slot = row % (2 * BORDER)
    beside = jnp.where(
        row < 2 * BORDER, partner(here, tiles, 0), partner(here, tiles, 1)
    )
    where = (beside - here) * width + slot + jnp.where(slot < BORDER, 0, width - 2 * BORDER)
    pick_ref[width:] = jnp.where(beside < 0, 0.0, found(where)).astype(jnp.bfloat16)


def turn_kernel(counts_ref, outer_ref, inner_ref, landed, sems):
    width, genes = landed.shape
    side = quarter(width)
    copies = []
    for i in range(genes // COPY_COLUMNS):
        columns = pl.ds(i * COPY_COLUMNS, COPY_COLUMNS)
        copies.append(
            pltpu.make_async_copy(
                counts_ref.at[:, columns], landed.at[:, columns], sems.at[i]
            )
        )
    for copy in copies:
        copy.start()
    for i, copy in enumerate(copies):
        copy.wait()
        run = slice(i * COPY_COLUMNS, (i + 1) * COPY_COLUMNS)
        ends = jnp.concatenate([landed[:side, run], landed[width - side :, run]], axis=0)
        outer_ref[run] = ends.astype(jnp.float32).T.astype(jnp.bfloat16)
        middle = landed[side : width - side, run]
        inner_ref[run] = middle.astype(jnp.float32).T.astype(jnp.bfloat16)


def first_kernel(outer_ref, inner_ref, cells_ref, gene_ref, part_ref, rows_ref):
    rank, genes = gene_ref.shape
    width = cells_ref.shape[1]
    cells = cells_ref[...]
    cells = jnp.concatenate([outer_of(cells), inner_of(cells)], axis=1)
    factor_rows = jnp.concatenate(split(cells), axis=0)
    gsum = jnp.zeros((rank, 1), jnp.float32)
    total = jnp.zeros((rank, width), jnp.float32)
    for run in runs_of(genes):
        wide = gene_ref[:, run].astype(jnp.float32)
        gsum += jnp.sum(wide, axis=1, keepdims=True)
        rows = jnp.concatenate([wide, wide], axis=0).T.astype(jnp.bfloat16)
        rows_ref[run] = rows
        product = jnp.dot(rows, factor_rows, preferred_element_type=jnp.float32)
        counts = jnp.concatenate([outer_ref[run], inner_ref[run]], axis=1)
        ratio = counts.astype(jnp.float32) * pl.reciprocal(product, approx=True)
        total += numerator(gene_ref, run, ratio.astype(jnp.bfloat16))
    part_ref[:, :width] = whole_of(total[:, : width // 2], total[:, width // 2 :])
    part_ref[:, width:] = jnp.broadcast_to(gsum, (rank, LANES))


def masked_rows(values, flags):
    flag_rows = jnp.broadcast_to(flags.astype(jnp.float32), (ROWS, flags.shape[1]))
    return jnp.concatenate([jnp.where(flags, values, 0.0), flag_rows], axis=0)


def update_kernel(numer_ref, other_ref, gsum_ref, cells_ref, tissue_ref, updated_ref, edges_ref):
    width = cells_ref.shape[1]
    flags = tissue_ref[...] > 0
    numer = numer_ref[...] + other_ref[...]
    cells = cells_ref[...]
    updated = jnp.where(flags, cells * numer / gsum_ref[:, :1], cells)
    updated_ref[...] = updated
    both = masked_rows(updated, flags)
    edges_ref[:, :BORDER] = both[:, :BORDER]
    edges_ref[:, BORDER : 2 * BORDER] = both[:, width - BORDER :]
    edges_ref[:, 2 * BORDER :] = jnp.zeros_like(edges_ref[:, 2 * BORDER :])


def first_update_kernel(
    part_ref, other_ref, cells_ref, tissue_ref, _, updated_ref, edges_ref, gsum_ref
):
    width = cells_ref.shape[1]
    gsum_ref[...] = part_ref[:, width:] + other_ref[:, width:]
    update_kernel(
        part_ref.at[:, :width], other_ref.at[:, :width], gsum_ref,
        cells_ref, tissue_ref, updated_ref, edges_ref,
    )


def mixed(updated, flags, near):
    rank = updated.shape[0]
    mean = near[:rank] / jnp.maximum(near[rank : rank + 1], 1.0)
    return jnp.where(
        flags, (1.0 - smooth_weight) * updated + smooth_weight * mean, updated
    )


def picked(values, pick):
    return sum(
        jnp.dot(part, pick, preferred_element_type=jnp.float32) for part in split(values)
    )


def smoothed_inner(updated_ref, tissue_ref, pick_ref):
    updated, tissue = updated_ref[...], tissue_ref[...]
    width = updated.shape[1]
    near = picked(masked_rows(updated, tissue > 0), pick_ref[:width, width // 2 :])
    flags = inner_of(tissue) > 0
    return mixed(inner_of(updated), flags, near), flags


def smoothed_outer(updated_ref, tissue_ref, pick_ref, first_ref, second_ref):
    updated, tissue = updated_ref[...], tissue_ref[...]
    width = updated.shape[1]
    sides = jnp.concatenate(
        [first_ref[:, : 2 * BORDER], second_ref[:, : 2 * BORDER]], axis=1
    )
    near = picked(masked_rows(updated, tissue > 0), pick_ref[:width, : width // 2])
    near += picked(sides, pick_ref[width:, : width // 2])
    flags = outer_of(tissue) > 0
    return mixed(outer_of(updated), flags, near), flags


def inner_kernel(
    updated_ref, tissue_ref, pick_ref, kept_ref, rows_ref, gene_ref, cells_ref, numer_ref
):
    cells, _ = smoothed_inner(updated_ref, tissue_ref, pick_ref)
    cells_ref[...] = cells
    numer_ref[...] = sum(
        numerator(gene_ref, run, ratio_of(kept_ref, run, rows_ref[run], cells))
        for run in runs_of(gene_ref.shape[1], 2048)
    )


def outer_kernel(
    updated_ref, tissue_ref, pick_ref, first_ref, second_ref, kept_ref, rows_ref,
    gene_ref, inner_cells_ref, inner_numer_ref, cells_ref, numer_ref,
):
    cells, _ = smoothed_outer(updated_ref, tissue_ref, pick_ref, first_ref, second_ref)
    cells_ref[...] = whole_of(cells, inner_cells_ref[...])
    numer = sum(
        numerator(gene_ref, run, ratio_of(kept_ref, run, rows_ref[run], cells))
        for run in runs_of(gene_ref.shape[1], 2048)
    )
    numer_ref[...] = whole_of(numer, inner_numer_ref[...])


def exponent(values):
    return jnp.ceil(jnp.log2(jnp.maximum(values, 1e-30)))


def share_height(columns):
    blocks = columns // LANES
    return (blocks + blocks % 2) * ROWS + STAT_ROWS


def encode(values, hden, targets):
    power = exponent(jnp.max(values, axis=1, keepdims=True))
    coded = (values * (jnp.exp2(-power) * FULL) + 0.5).astype(jnp.int32)
    hden_power = exponent(hden)
    scaled = hden * jnp.exp2(-hden_power) * FULL
    high = jnp.floor(scaled)
    low = jnp.floor((scaled - high) * FULL)
    lane = lax.broadcasted_iota(jnp.int32, (values.shape[0], LANES), 1)
    marks = jnp.zeros((values.shape[0], LANES), jnp.float32)
    for at, value in enumerate((power, hden_power, high, low)):
        marks = jnp.where(lane == at, value, marks)
    marks = marks.astype(jnp.int32)
    blank = jnp.zeros((ROWS, LANES), jnp.int32)
    for group, target in enumerate(targets):
        ranks = slice(group * ROWS, (group + 1) * ROWS)
        blocks = [coded[ranks, at : at + LANES] for at in range(0, values.shape[1], LANES)]
        blocks += [blank] * (len(blocks) % 2) + [marks[ranks], blank]
        for i in range(0, len(blocks), 2):
            target[i * ROWS : (i + 2) * ROWS] = jnp.concatenate(
                blocks[i : i + 2], axis=0
            ).astype(jnp.int16)


def decode(source, columns):
    def number(start):
        return source[start : start + 2 * ROWS].astype(jnp.int32).astype(jnp.float32)

    height = source.shape[0]
    marks = number(height - STAT_ROWS)[:ROWS]
    scale = jnp.exp2(marks[:, :1]) / FULL
    hden = (marks[:, 2:3] + marks[:, 3:4] / FULL) * (jnp.exp2(marks[:, 1:2]) / FULL)
    blocks = []
    for start in range(0, height - STAT_ROWS, 2 * ROWS):
        both = number(start)
        blocks += [both[:ROWS] * scale, both[ROWS:] * scale]
    return jnp.concatenate(blocks[: columns // LANES], axis=1), hden


def gene_totals(cells, flags, kept_ref, rows_ref, totals_ref, others_ref=None):
    def put(columns, values):
        if others_ref is not None:
            values += others_ref[:, columns]
        totals_ref[:, columns] = values

    rank = cells.shape[0]
    genes = totals_ref.shape[1] - LANES
    masked = jnp.where(flags, cells, 0.0)
    parts = jnp.concatenate(split(masked), axis=0)
    columns = parts.astype(jnp.float32).T.astype(jnp.bfloat16)
    hden = jnp.sum(masked, axis=1, keepdims=True)
    put(slice(genes, genes + LANES), jnp.broadcast_to(hden, (rank, LANES)))
    for run in runs_of(genes, 1024):
        ratio = ratio_of(kept_ref, run, rows_ref[run], cells)
        total = jnp.dot(ratio, columns, preferred_element_type=jnp.float32).T
        put(run, total[:rank] + total[rank:])


def inner_totals_kernel(
    updated_ref, tissue_ref, pick_ref, kept_ref, rows_ref, cells_ref, totals_ref
):
    cells, flags = smoothed_inner(updated_ref, tissue_ref, pick_ref)
    cells_ref[...] = cells
    gene_totals(cells, flags, kept_ref, rows_ref, totals_ref)


def last_pass(
    updated_ref, tissue_ref, pick_ref, first_ref, second_ref, kept_ref, rows_ref,
    inner_cells_ref, inner_totals_ref, cells_ref, totals_ref,
):
    cells, flags = smoothed_outer(updated_ref, tissue_ref, pick_ref, first_ref, second_ref)
    cells_ref[...] = whole_of(cells, inner_cells_ref[...])
    gene_totals(cells, flags, kept_ref, rows_ref, totals_ref, inner_totals_ref)


def encode_tiles(totals_ref, sent_ref):
    rank, genes = totals_ref.shape[0], totals_ref.shape[1] - LANES
    tiles = sent_ref.shape[0]
    across = tiles * ROWS // rank
    columns = genes // across
    for column in range(across):
        encode(
            totals_ref[:, column * columns : (column + 1) * columns],
            totals_ref[:, genes : genes + 1],
            [sent_ref.at[tile] for tile in range(column, tiles, across)],
        )


def shares_kernel(*refs):
    *passed, sent_ref, totals_ref = refs
    last_pass(*passed, totals_ref)
    encode_tiles(totals_ref, sent_ref)


def distance_kernel(*refs):
    passed, (*sent_refs, own_ref, totals_ref, coded_ref) = refs[:10], refs[10:]
    last_pass(*passed, totals_ref)
    tiles, height, _ = coded_ref.shape
    encode_tiles(totals_ref, coded_ref)
    tile = lax.axis_index("tile")
    for distance in range(tiles // 2):
        there = tile ^ (2 * distance)
        own_ref[distance * height : (distance + 1) * height] = coded_ref[there]
        sent_refs[distance][...] = coded_ref[there ^ 1]


def column_kernel(distance, columns, got_ref, own_ref, *refs):
    sent_ref = refs[-1]
    height = sent_ref.shape[0]
    values, hden = decode(got_ref, columns)
    start = height * distance
    more, more_hden = decode(own_ref.at[start : start + height], columns)
    encode(values + more, hden + more_hden, [sent_ref])


def fresh_of(hnum, hden, gene_ref, across):
    columns = hnum.shape[1]
    here = lax.axis_index("tile")
    place = pl.multiple_of(lax.rem(here, across) * columns, LANES)
    every = gene_ref[:, pl.ds(place, columns)].astype(jnp.float32)
    hf = every[:ROWS]
    for group in range(1, gene_ref.shape[0] // ROWS):
        hf = jnp.where(here // across == group, every[group * ROWS : (group + 1) * ROWS], hf)
    return (hf * hnum / hden).astype(jnp.bfloat16)


def all_shares_kernel(got_ref, gene_ref, fresh_ref):
    tiles, _, columns = fresh_ref.shape
    hnum, hden = decode(got_ref.at[0], columns)
    for tile in range(1, tiles):
        more, more_hden = decode(got_ref.at[tile], columns)
        hnum += more
        hden += more_hden
    fresh = fresh_of(hnum, hden, gene_ref, tiles * ROWS // gene_ref.shape[0])
    for tile in range(tiles):
        fresh_ref[tile] = fresh


def fresh_kernel(*refs):
    *got_refs, gene_ref, fresh_ref = refs
    hnum, hden = 0.0, 0.0
    for ref in got_refs:
        more, more_hden = decode(ref, fresh_ref.shape[1])
        hnum += more
        hden += more_hden
    fresh_ref[...] = fresh_of(hnum, hden, gene_ref, 2)


def spread_kernel(*refs):
    *share_refs, out_ref = refs
    groups = len(share_refs) // 2
    columns = share_refs[0].shape[1]
    tile = lax.axis_index("tile")
    here, side = tile // 2, lax.rem(tile, 2)
    shares = [ref[...].astype(jnp.float32) for ref in share_refs]
    for column in range(2):
        own = side == column
        picked = []
        for group in range(groups):
            distance = here ^ group
            share = jnp.where(own, shares[0], shares[groups])
            for at in range(1, groups):
                either = jnp.where(own, shares[at], shares[groups + at])
                share = jnp.where(distance == at, either, share)
            picked.append(share)
        for group in range(0, groups, 2):
            out_ref[
                group * ROWS : (group + 2) * ROWS, column * columns : (column + 1) * columns
            ] = jnp.concatenate(picked[group : group + 2], axis=0).astype(jnp.bfloat16)


def call(kernel, outs, scratch=(), specs=None, limit=VMEM_BYTES):
    whole = pl.BlockSpec(memory_space=pltpu.VMEM)
    return lambda *args: pl.pallas_call(
        kernel,
        out_shape=outs,
        in_specs=specs or [whole] * len(args),
        out_specs=jax.tree.map(lambda _: whole, outs),
        scratch_shapes=list(scratch),
        compiler_params=pltpu.CompilerParams(vmem_limit_bytes=limit),
    )(*args)


def beside(tiles, halves, offset):
    pairs = []
    paired = set()
    for low in range(offset, tiles - 1, 2):
        paired |= {low, low + 1}
        for gene in range(halves):
            other = (gene + 1) % halves
            pairs.append((low * halves + gene, (low + 1) * halves + other))
            pairs.append(((low + 1) * halves + gene, low * halves + other))
    for tile in range(tiles):
        if tile not in paired:
            for gene in range(halves):
                pairs.append((tile * halves + gene, tile * halves + (gene + 1) % halves))
    return pairs


def on_device(counts, cell_factor, gene_factor, tissue, neighbours):
    rank, width = cell_factor.shape
    genes = gene_factor.shape[1]
    tiles, halves = lax.axis_size("tile"), lax.axis_size("gene")
    flag_row = tissue[None]
    shape = jax.ShapeDtypeStruct
    factor = shape((rank, width), jnp.float32)
    edge = shape((rank + ROWS, LANES), jnp.float32)
    half = shape((rank, width // 2), jnp.float32)
    half_kept = shape((genes, width // 2), jnp.bfloat16)
    gene_rows = shape((genes, 2 * rank), jnp.bfloat16)
    far = pl.BlockSpec(memory_space=pl.ANY)
    near = pl.BlockSpec(memory_space=pltpu.VMEM)

    outer, inner = call(
        turn_kernel,
        (half_kept, half_kept),
        [
            pltpu.VMEM(counts.shape, counts.dtype),
            pltpu.SemaphoreType.DMA((genes // COPY_COLUMNS,)),
        ],
        [far],
        COUNTS_VMEM_BYTES,
    )(counts)
    part, rows = call(
        first_kernel, (shape((rank, width + LANES), jnp.float32), gene_rows)
    )(outer, inner, cell_factor, gene_factor)
    pick = call(pick_kernel, shape((width + LANES, width), jnp.bfloat16))(neighbours)

    def swapped(part):
        if halves == 2:
            return lax.ppermute(part, "gene", [(0, 1), (1, 0)])
        return lax.psum(part, "gene") - part

    def around(edges):
        return [
            lax.ppermute(edges, ("tile", "gene"), beside(tiles, halves, offset))
            for offset in (0, 1)
        ]

    updated, edges, gsum = call(
        first_update_kernel,
        (factor, edge, shape((rank, LANES), jnp.float32)),
        specs=[near] * 4 + [far],
    )(part, swapped(part), cell_factor, flag_row, pick)
    inner_of_both = call(inner_kernel, (half, half))(
        updated, flag_row, pick, inner, rows, gene_factor
    )
    cells, numer = call(outer_kernel, (factor, factor))(
        updated, flag_row, pick, *around(edges), outer, rows, gene_factor, *inner_of_both
    )
    updated, edges = call(update_kernel, (factor, edge))(
        numer, swapped(numer), gsum, cells, flag_row
    )
    across = tiles * ROWS // rank
    groups = rank // ROWS
    columns = genes // across
    height = share_height(columns)
    inner_of_both = call(
        inner_totals_kernel, (half, shape((rank, genes + LANES), jnp.float32))
    )(updated, flag_row, pick, inner, rows)
    last = (updated, flag_row, pick, *around(edges), outer, rows, *inner_of_both)
    totals = [pltpu.VMEM((rank, genes + LANES), jnp.float32)]
    if across != 2 or groups != 4 or halves != 2:
        cells, sent = call(
            shares_kernel, (factor, shape((tiles, height, LANES), jnp.int16)), totals
        )(*last)
        got = lax.all_to_all(sent, "tile", 0, 0)
        fresh = call(all_shares_kernel, shape((tiles, ROWS, columns), jnp.bfloat16))(
            got, gene_factor
        )
        every = lax.all_to_all(fresh, "tile", 0, 0).reshape(groups, across, ROWS, columns)
        return cells, every.transpose(0, 2, 1, 3).reshape(rank, genes)

    def moved(array, step, cross):
        pairs = [
            (tile * halves + gene, (tile ^ step) * halves + (gene ^ cross))
            for tile in range(tiles)
            for gene in range(halves)
        ]
        return lax.ppermute(array, ("tile", "gene"), pairs)

    one = shape((height, LANES), jnp.int16)
    cells, *sent, own = call(
        distance_kernel,
        (
            factor,
            *[one] * groups,
            shape((groups * height, LANES), jnp.int16),
        ),
        totals + [pltpu.VMEM((tiles, height, LANES), jnp.int16)],
    )(*last)
    distances = range(groups - 1, 0, -1)
    own = moved(own, 0, 1)
    got = [moved(share, 1, 1) for share in sent]
    summed = []
    for distance in (*distances, 0):
        after = () if distance else summed[:1]
        both = call(
            functools.partial(column_kernel, distance, columns), one,
            specs=[near] * 2 + [far] * len(after),
        )(got[distance], own, *after)
        summed.append(moved(both, 2 * distance, 1))
    fresh = call(fresh_kernel, shape((ROWS, columns), jnp.bfloat16))(*summed, gene_factor)
    shares, others = [fresh], [moved(fresh, 1, 0)]
    passing = {distance: moved(fresh, 2 * distance, 1) for distance in distances}
    for distance in range(1, groups):
        shares.append(moved(passing[distance], 0, 1))
        others.append(moved(passing[distance], 1, 1))
    return cells, call(spread_kernel, shape((rank, genes), jnp.bfloat16))(*shares, *others)


def solution(mesh):
    return jax.shard_map(
        on_device,
        mesh=mesh,
        in_specs=(
            P(("grp", "tile"), "gene"),
            P(None, ("grp", "tile")),
            P(None, ("grp", "gene")),
            P(("grp", "tile")),
            P(None, ("grp", "tile")),
        ),
        out_specs=(P(None, ("grp", "tile")), P(None, ("grp", "gene"))),
        check_vma=False,
    )
```

```python
import functools

import jax
import jax.numpy as jnp
from jax import lax
from jax.experimental import pallas as pl
from jax.experimental.pallas import tpu as pltpu
from jax.sharding import PartitionSpec as P

BORDER = 32
LANES = 128
ROWS = 8
STAT_ROWS = 16
FULL = 32767.0
smooth_weight = 0.5
VMEM_BYTES = 24 * 1024 * 1024
COUNTS_VMEM_BYTES = 51 * 1024 * 1024
COPY_COLUMNS = 512


def split(values):
    high = values.astype(jnp.bfloat16)
    low = (values - high.astype(jnp.float32)).astype(jnp.bfloat16)
    return high, low


def piece(total, wanted):
    for size in (4096, 2048, 1024, 512, 256, 128):
        if size <= wanted and total % size == 0:
            return size
    return total


def quarter(width):
    return width // 4


def outer_of(values):
    side = quarter(values.shape[1])
    return jnp.concatenate([values[:, :side], values[:, -side:]], axis=1)


def inner_of(values):
    side = quarter(values.shape[1])
    return values[:, side:-side]


def whole_of(outer, inner):
    side = quarter(2 * outer.shape[1])
    return jnp.concatenate([outer[:, :side], inner, outer[:, side:]], axis=1)


def ratio_of(kept_ref, run, gene_rows, cells):
    factor_rows = jnp.concatenate(split(cells), axis=0)
    product = jnp.dot(gene_rows, factor_rows, preferred_element_type=jnp.float32)
    counts = kept_ref[run].astype(jnp.float32)
    return (counts * pl.reciprocal(product, approx=True)).astype(jnp.bfloat16)


def runs_of(genes, wanted=1024):
    size = piece(genes, wanted)
    return [slice(at, at + size) for at in range(0, genes, size)]


def numerator(gene_ref, run, ratio):
    return jnp.dot(gene_ref[:, run], ratio, preferred_element_type=jnp.float32)


def partner(tile, tiles, offset):
    other = jnp.where((tile + offset) % 2 == 0, tile + 1, tile - 1)
    return jnp.where((other >= 0) & (other < tiles), other, -1)


def pick_kernel(neigh_ref, pick_ref):
    width = neigh_ref.shape[1]
    tiles = lax.axis_size("tile")
    here = lax.axis_index("tile")
    neigh = neigh_ref[...] - here * width
    neigh = jnp.concatenate([outer_of(neigh), inner_of(neigh)], axis=1)

    def found(where):
        total = jnp.zeros((LANES, width), jnp.float32)
        for j in range(neigh.shape[0]):
            total += (neigh[j : j + 1] == where).astype(jnp.float32)
        return total

    row = lax.broadcasted_iota(jnp.int32, (LANES, width), 0)
    for at in range(0, width, LANES):
        pick_ref[at : at + LANES] = found(at + row).astype(jnp.bfloat16)
    slot = row % (2 * BORDER)
    beside = jnp.where(
        row < 2 * BORDER, partner(here, tiles, 0), partner(here, tiles, 1)
    )
    where = (beside - here) * width + slot + jnp.where(slot < BORDER, 0, width - 2 * BORDER)
    pick_ref[width:] = jnp.where(beside < 0, 0.0, found(where)).astype(jnp.bfloat16)


def turn_kernel(counts_ref, outer_ref, inner_ref, landed, sems):
    width, genes = landed.shape
    side = quarter(width)
    copies = []
    for i in range(genes // COPY_COLUMNS):
        columns = pl.ds(i * COPY_COLUMNS, COPY_COLUMNS)
        copies.append(
            pltpu.make_async_copy(
                counts_ref.at[:, columns], landed.at[:, columns], sems.at[i]
            )
        )
    for copy in copies:
        copy.start()
    for i, copy in enumerate(copies):
        copy.wait()
        run = slice(i * COPY_COLUMNS, (i + 1) * COPY_COLUMNS)
        ends = jnp.concatenate([landed[:side, run], landed[width - side :, run]], axis=0)
        outer_ref[run] = ends.astype(jnp.float32).T.astype(jnp.bfloat16)
        middle = landed[side : width - side, run]
        inner_ref[run] = middle.astype(jnp.float32).T.astype(jnp.bfloat16)


def first_kernel(outer_ref, inner_ref, cells_ref, gene_ref, part_ref, rows_ref):
    rank, genes = gene_ref.shape
    width = cells_ref.shape[1]
    cells = cells_ref[...]
    cells = jnp.concatenate([outer_of(cells), inner_of(cells)], axis=1)
    factor_rows = jnp.concatenate(split(cells), axis=0)
    gsum = jnp.zeros((rank, 1), jnp.float32)
    total = jnp.zeros((rank, width), jnp.float32)
    for run in runs_of(genes):
        wide = gene_ref[:, run].astype(jnp.float32)
        gsum += jnp.sum(wide, axis=1, keepdims=True)
        rows = jnp.concatenate([wide, wide], axis=0).T.astype(jnp.bfloat16)
        rows_ref[run] = rows
        product = jnp.dot(rows, factor_rows, preferred_element_type=jnp.float32)
        counts = jnp.concatenate([outer_ref[run], inner_ref[run]], axis=1)
        ratio = counts.astype(jnp.float32) * pl.reciprocal(product, approx=True)
        total += numerator(gene_ref, run, ratio.astype(jnp.bfloat16))
    part_ref[:, :width] = whole_of(total[:, : width // 2], total[:, width // 2 :])
    part_ref[:, width:] = jnp.broadcast_to(gsum, (rank, LANES))


def masked_rows(values, flags):
    flag_rows = jnp.broadcast_to(flags.astype(jnp.float32), (ROWS, flags.shape[1]))
    return jnp.concatenate([jnp.where(flags, values, 0.0), flag_rows], axis=0)


def update_kernel(numer_ref, other_ref, gsum_ref, cells_ref, tissue_ref, updated_ref, edges_ref):
    width = cells_ref.shape[1]
    flags = tissue_ref[...] > 0
    numer = numer_ref[...] + other_ref[...]
    cells = cells_ref[...]
    updated = jnp.where(flags, cells * numer / gsum_ref[:, :1], cells)
    updated_ref[...] = updated
    both = masked_rows(updated, flags)
    edges_ref[:, :BORDER] = both[:, :BORDER]
    edges_ref[:, BORDER : 2 * BORDER] = both[:, width - BORDER :]
    edges_ref[:, 2 * BORDER :] = jnp.zeros_like(edges_ref[:, 2 * BORDER :])


def first_update_kernel(
    part_ref, other_ref, cells_ref, tissue_ref, _, updated_ref, edges_ref, gsum_ref
):
    width = cells_ref.shape[1]
    gsum_ref[...] = part_ref[:, width:] + other_ref[:, width:]
    update_kernel(
        part_ref.at[:, :width], other_ref.at[:, :width], gsum_ref,
        cells_ref, tissue_ref, updated_ref, edges_ref,
    )


def mixed(updated, flags, near):
    rank = updated.shape[0]
    mean = near[:rank] / jnp.maximum(near[rank : rank + 1], 1.0)
    return jnp.where(
        flags, (1.0 - smooth_weight) * updated + smooth_weight * mean, updated
    )


def picked(values, pick):
    return sum(
        jnp.dot(part, pick, preferred_element_type=jnp.float32) for part in split(values)
    )


def smoothed_inner(updated_ref, tissue_ref, pick_ref):
    updated, tissue = updated_ref[...], tissue_ref[...]
    width = updated.shape[1]
    near = picked(masked_rows(updated, tissue > 0), pick_ref[:width, width // 2 :])
    flags = inner_of(tissue) > 0
    return mixed(inner_of(updated), flags, near), flags


def smoothed_outer(updated_ref, tissue_ref, pick_ref, first_ref, second_ref):
    updated, tissue = updated_ref[...], tissue_ref[...]
    width = updated.shape[1]
    sides = jnp.concatenate(
        [first_ref[:, : 2 * BORDER], second_ref[:, : 2 * BORDER]], axis=1
    )
    near = picked(masked_rows(updated, tissue > 0), pick_ref[:width, : width // 2])
    near += picked(sides, pick_ref[width:, : width // 2])
    flags = outer_of(tissue) > 0
    return mixed(outer_of(updated), flags, near), flags


def inner_kernel(
    updated_ref, tissue_ref, pick_ref, kept_ref, rows_ref, gene_ref, cells_ref, numer_ref
):
    cells, _ = smoothed_inner(updated_ref, tissue_ref, pick_ref)
    cells_ref[...] = cells
    numer_ref[...] = sum(
        numerator(gene_ref, run, ratio_of(kept_ref, run, rows_ref[run], cells))
        for run in runs_of(gene_ref.shape[1], 2048)
    )


def outer_kernel(
    updated_ref, tissue_ref, pick_ref, first_ref, second_ref, kept_ref, rows_ref,
    gene_ref, inner_cells_ref, inner_numer_ref, cells_ref, numer_ref,
):
    cells, _ = smoothed_outer(updated_ref, tissue_ref, pick_ref, first_ref, second_ref)
    cells_ref[...] = whole_of(cells, inner_cells_ref[...])
    numer = sum(
        numerator(gene_ref, run, ratio_of(kept_ref, run, rows_ref[run], cells))
        for run in runs_of(gene_ref.shape[1], 2048)
    )
    numer_ref[...] = whole_of(numer, inner_numer_ref[...])


def exponent(values):
    return jnp.ceil(jnp.log2(jnp.maximum(values, 1e-30)))


def share_height(columns):
    blocks = columns // LANES
    return (blocks + blocks % 2) * ROWS + STAT_ROWS


def encode(values, hden, targets):
    power = exponent(jnp.max(values, axis=1, keepdims=True))
    coded = (values * (jnp.exp2(-power) * FULL) + 0.5).astype(jnp.int32)
    hden_power = exponent(hden)
    scaled = hden * jnp.exp2(-hden_power) * FULL
    high = jnp.floor(scaled)
    low = jnp.floor((scaled - high) * FULL)
    lane = lax.broadcasted_iota(jnp.int32, (values.shape[0], LANES), 1)
    marks = jnp.zeros((values.shape[0], LANES), jnp.float32)
    for at, value in enumerate((power, hden_power, high, low)):
        marks = jnp.where(lane == at, value, marks)
    marks = marks.astype(jnp.int32)
    blank = jnp.zeros((ROWS, LANES), jnp.int32)
    for group, target in enumerate(targets):
        ranks = slice(group * ROWS, (group + 1) * ROWS)
        blocks = [coded[ranks, at : at + LANES] for at in range(0, values.shape[1], LANES)]
        blocks += [blank] * (len(blocks) % 2) + [marks[ranks], blank]
        for i in range(0, len(blocks), 2):
            target[i * ROWS : (i + 2) * ROWS] = jnp.concatenate(
                blocks[i : i + 2], axis=0
            ).astype(jnp.int16)


def decode(source, columns):
    def number(start):
        return source[start : start + 2 * ROWS].astype(jnp.int32).astype(jnp.float32)

    height = source.shape[0]
    marks = number(height - STAT_ROWS)[:ROWS]
    scale = jnp.exp2(marks[:, :1]) / FULL
    hden = (marks[:, 2:3] + marks[:, 3:4] / FULL) * (jnp.exp2(marks[:, 1:2]) / FULL)
    blocks = []
    for start in range(0, height - STAT_ROWS, 2 * ROWS):
        both = number(start)
        blocks += [both[:ROWS] * scale, both[ROWS:] * scale]
    return jnp.concatenate(blocks[: columns // LANES], axis=1), hden


def gene_totals(cells, flags, kept_ref, rows_ref, totals_ref, others_ref=None):
    def put(columns, values):
        if others_ref is not None:
            values += others_ref[:, columns]
        totals_ref[:, columns] = values

    rank = cells.shape[0]
    genes = totals_ref.shape[1] - LANES
    masked = jnp.where(flags, cells, 0.0)
    parts = jnp.concatenate(split(masked), axis=0)
    columns = parts.astype(jnp.float32).T.astype(jnp.bfloat16)
    hden = jnp.sum(masked, axis=1, keepdims=True)
    put(slice(genes, genes + LANES), jnp.broadcast_to(hden, (rank, LANES)))
    for run in runs_of(genes, 1024):
        ratio = ratio_of(kept_ref, run, rows_ref[run], cells)
        total = jnp.dot(ratio, columns, preferred_element_type=jnp.float32).T
        put(run, total[:rank] + total[rank:])


def inner_totals_kernel(
    updated_ref, tissue_ref, pick_ref, kept_ref, rows_ref, cells_ref, totals_ref
):
    cells, flags = smoothed_inner(updated_ref, tissue_ref, pick_ref)
    cells_ref[...] = cells
    gene_totals(cells, flags, kept_ref, rows_ref, totals_ref)


def last_pass(
    updated_ref, tissue_ref, pick_ref, first_ref, second_ref, kept_ref, rows_ref,
    inner_cells_ref, inner_totals_ref, cells_ref, totals_ref,
):
    cells, flags = smoothed_outer(updated_ref, tissue_ref, pick_ref, first_ref, second_ref)
    cells_ref[...] = whole_of(cells, inner_cells_ref[...])
    gene_totals(cells, flags, kept_ref, rows_ref, totals_ref, inner_totals_ref)


def encode_tiles(totals_ref, sent_ref):
    rank, genes = totals_ref.shape[0], totals_ref.shape[1] - LANES
    tiles = sent_ref.shape[0]
    across = tiles * ROWS // rank
    columns = genes // across
    for column in range(across):
        encode(
            totals_ref[:, column * columns : (column + 1) * columns],
            totals_ref[:, genes : genes + 1],
            [sent_ref.at[tile] for tile in range(column, tiles, across)],
        )


def shares_kernel(*refs):
    *passed, sent_ref, totals_ref = refs
    last_pass(*passed, totals_ref)
    encode_tiles(totals_ref, sent_ref)


def distance_kernel(*refs):
    passed, (*sent_refs, own_ref, totals_ref, coded_ref) = refs[:10], refs[10:]
    last_pass(*passed, totals_ref)
    tiles, height, _ = coded_ref.shape
    encode_tiles(totals_ref, coded_ref)
    tile = lax.axis_index("tile")
    for distance in range(tiles // 2):
        there = tile ^ (2 * distance)
        own_ref[distance * height : (distance + 1) * height] = coded_ref[there]
        sent_refs[distance][...] = coded_ref[there ^ 1]


def column_kernel(distance, columns, got_ref, own_ref, *refs):
    sent_ref = refs[-1]
    height = sent_ref.shape[0]
    values, hden = decode(got_ref, columns)
    start = height * distance
    more, more_hden = decode(own_ref.at[start : start + height], columns)
    encode(values + more, hden + more_hden, [sent_ref])


def fresh_of(hnum, hden, gene_ref, across):
    columns = hnum.shape[1]
    here = lax.axis_index("tile")
    place = pl.multiple_of(lax.rem(here, across) * columns, LANES)
    every = gene_ref[:, pl.ds(place, columns)].astype(jnp.float32)
    hf = every[:ROWS]
    for group in range(1, gene_ref.shape[0] // ROWS):
        hf = jnp.where(here // across == group, every[group * ROWS : (group + 1) * ROWS], hf)
    return (hf * hnum / hden).astype(jnp.bfloat16)


def all_shares_kernel(got_ref, gene_ref, fresh_ref):
    tiles, _, columns = fresh_ref.shape
    hnum, hden = decode(got_ref.at[0], columns)
    for tile in range(1, tiles):
        more, more_hden = decode(got_ref.at[tile], columns)
        hnum += more
        hden += more_hden
    fresh = fresh_of(hnum, hden, gene_ref, tiles * ROWS // gene_ref.shape[0])
    for tile in range(tiles):
        fresh_ref[tile] = fresh


def fresh_kernel(*refs):
    *got_refs, gene_ref, fresh_ref = refs
    hnum, hden = 0.0, 0.0
    for ref in got_refs:
        more, more_hden = decode(ref, fresh_ref.shape[1])
        hnum += more
        hden += more_hden
    fresh_ref[...] = fresh_of(hnum, hden, gene_ref, 2)


def spread_kernel(*refs):
    *share_refs, cells_ref, new_cells_ref, out_ref = refs
    new_cells_ref[...] = cells_ref[...]
    groups = len(share_refs) // 2
    columns = share_refs[0].shape[1]
    tile = lax.axis_index("tile")
    here, side = tile // 2, lax.rem(tile, 2)
    shares = [ref[...].astype(jnp.float32) for ref in share_refs]
    for column in range(2):
        own = side == column
        picked = []
        for group in range(groups):
            distance = here ^ group
            share = jnp.where(own, shares[0], shares[groups])
            for at in range(1, groups):
                either = jnp.where(own, shares[at], shares[groups + at])
                share = jnp.where(distance == at, either, share)
            picked.append(share)
        for group in range(0, groups, 2):
            out_ref[
                group * ROWS : (group + 2) * ROWS, column * columns : (column + 1) * columns
            ] = jnp.concatenate(picked[group : group + 2], axis=0).astype(jnp.bfloat16)


def call(kernel, outs, scratch=(), specs=None, limit=VMEM_BYTES):
    whole = pl.BlockSpec(memory_space=pltpu.VMEM)
    return lambda *args: pl.pallas_call(
        kernel,
        out_shape=outs,
        in_specs=specs or [whole] * len(args),
        out_specs=jax.tree.map(lambda _: whole, outs),
        scratch_shapes=list(scratch),
        compiler_params=pltpu.CompilerParams(vmem_limit_bytes=limit),
    )(*args)


def beside(tiles, halves, offset):
    pairs = []
    paired = set()
    for low in range(offset, tiles - 1, 2):
        paired |= {low, low + 1}
        for gene in range(halves):
            other = (gene + 1) % halves
            pairs.append((low * halves + gene, (low + 1) * halves + other))
            pairs.append(((low + 1) * halves + gene, low * halves + other))
    for tile in range(tiles):
        if tile not in paired:
            for gene in range(halves):
                pairs.append((tile * halves + gene, tile * halves + (gene + 1) % halves))
    return pairs


def on_device(counts, cell_factor, gene_factor, tissue, neighbours):
    rank, width = cell_factor.shape
    genes = gene_factor.shape[1]
    tiles, halves = lax.axis_size("tile"), lax.axis_size("gene")
    flag_row = tissue[None]
    shape = jax.ShapeDtypeStruct
    factor = shape((rank, width), jnp.float32)
    edge = shape((rank + ROWS, LANES), jnp.float32)
    half = shape((rank, width // 2), jnp.float32)
    half_kept = shape((genes, width // 2), jnp.bfloat16)
    gene_rows = shape((genes, 2 * rank), jnp.bfloat16)
    far = pl.BlockSpec(memory_space=pl.ANY)
    near = pl.BlockSpec(memory_space=pltpu.VMEM)

    outer, inner = call(
        turn_kernel,
        (half_kept, half_kept),
        [
            pltpu.VMEM(counts.shape, counts.dtype),
            pltpu.SemaphoreType.DMA((genes // COPY_COLUMNS,)),
        ],
        [far],
        COUNTS_VMEM_BYTES,
    )(counts)
    part, rows = call(
        first_kernel, (shape((rank, width + LANES), jnp.float32), gene_rows)
    )(outer, inner, cell_factor, gene_factor)
    pick = call(pick_kernel, shape((width + LANES, width), jnp.bfloat16))(neighbours)

    def swapped(part):
        if halves == 2:
            return lax.ppermute(part, "gene", [(0, 1), (1, 0)])
        return lax.psum(part, "gene") - part

    def around(edges):
        return [
            lax.ppermute(edges, ("tile", "gene"), beside(tiles, halves, offset))
            for offset in (0, 1)
        ]

    updated, edges, gsum = call(
        first_update_kernel,
        (factor, edge, shape((rank, LANES), jnp.float32)),
        specs=[near] * 4 + [far],
    )(part, swapped(part), cell_factor, flag_row, pick)
    inner_of_both = call(inner_kernel, (half, half))(
        updated, flag_row, pick, inner, rows, gene_factor
    )
    cells, numer = call(outer_kernel, (factor, factor))(
        updated, flag_row, pick, *around(edges), outer, rows, gene_factor, *inner_of_both
    )
    updated, edges = call(update_kernel, (factor, edge))(
        numer, swapped(numer), gsum, cells, flag_row
    )
    across = tiles * ROWS // rank
    groups = rank // ROWS
    columns = genes // across
    height = share_height(columns)
    inner_of_both = call(
        inner_totals_kernel, (half, shape((rank, genes + LANES), jnp.float32))
    )(updated, flag_row, pick, inner, rows)
    last = (updated, flag_row, pick, *around(edges), outer, rows, *inner_of_both)
    totals = [pltpu.VMEM((rank, genes + LANES), jnp.float32)]
    if across != 2 or groups != 4 or halves != 2:
        cells, sent = call(
            shares_kernel, (factor, shape((tiles, height, LANES), jnp.int16)), totals
        )(*last)
        got = lax.all_to_all(sent, "tile", 0, 0)
        fresh = call(all_shares_kernel, shape((tiles, ROWS, columns), jnp.bfloat16))(
            got, gene_factor
        )
        every = lax.all_to_all(fresh, "tile", 0, 0).reshape(groups, across, ROWS, columns)
        return cells, every.transpose(0, 2, 1, 3).reshape(rank, genes)

    def moved(array, step, cross):
        pairs = [
            (tile * halves + gene, (tile ^ step) * halves + (gene ^ cross))
            for tile in range(tiles)
            for gene in range(halves)
        ]
        return lax.ppermute(array, ("tile", "gene"), pairs)

    one = shape((height, LANES), jnp.int16)
    cells, *sent, own = call(
        distance_kernel,
        (
            factor,
            *[one] * groups,
            shape((groups * height, LANES), jnp.int16),
        ),
        totals + [pltpu.VMEM((tiles, height, LANES), jnp.int16)],
    )(*last)
    distances = range(groups - 1, 0, -1)
    own = moved(own, 0, 1)
    got = [moved(share, 1, 1) for share in sent]
    summed = []
    for distance in (*distances, 0):
        after = () if distance else summed[:1]
        both = call(
            functools.partial(column_kernel, distance, columns), one,
            specs=[near] * 2 + [far] * len(after),
        )(got[distance], own, *after)
        summed.append(moved(both, 2 * distance, 1))
    fresh = call(fresh_kernel, shape((ROWS, columns), jnp.bfloat16))(*summed, gene_factor)
    shares, others = [fresh], [moved(fresh, 1, 0)]
    passing = {distance: moved(fresh, 2 * distance, 1) for distance in distances}
    for distance in range(1, groups):
        shares.append(moved(passing[distance], 0, 1))
        others.append(moved(passing[distance], 1, 1))
    return call(spread_kernel, (factor, shape((rank, genes), jnp.bfloat16)))(
        *shares, *others, cells
    )


def solution(mesh):
    return jax.shard_map(
        on_device,
        mesh=mesh,
        in_specs=(
            P(("grp", "tile"), "gene"),
            P(None, ("grp", "tile")),
            P(None, ("grp", "gene")),
            P(("grp", "tile")),
            P(None, ("grp", "tile")),
        ),
        out_specs=(P(None, ("grp", "tile")), P(None, ("grp", "gene"))),
        check_vma=False,
    )
```

```python
import functools

import jax
import jax.numpy as jnp
from jax import lax
from jax.experimental import pallas as pl
from jax.experimental.pallas import tpu as pltpu
from jax.sharding import PartitionSpec as P

BORDER = 32
LANES = 128
ROWS = 8
STAT_ROWS = 16
FULL = 32767.0
smooth_weight = 0.5
VMEM_BYTES = 24 * 1024 * 1024
COUNTS_VMEM_BYTES = 51 * 1024 * 1024
COPY_COLUMNS = 512


def split(values):
    high = values.astype(jnp.bfloat16)
    low = (values - high.astype(jnp.float32)).astype(jnp.bfloat16)
    return high, low


def piece(total, wanted):
    for size in (4096, 2048, 1024, 512, 256, 128):
        if size <= wanted and total % size == 0:
            return size
    return total


def quarter(width):
    return width // 4


def outer_of(values):
    side = quarter(values.shape[1])
    return jnp.concatenate([values[:, :side], values[:, -side:]], axis=1)


def inner_of(values):
    side = quarter(values.shape[1])
    return values[:, side:-side]


def whole_of(outer, inner):
    side = quarter(2 * outer.shape[1])
    return jnp.concatenate([outer[:, :side], inner, outer[:, side:]], axis=1)


def ratio_of(kept_ref, run, gene_rows, cells):
    factor_rows = jnp.concatenate(split(cells), axis=0)
    product = jnp.dot(gene_rows, factor_rows, preferred_element_type=jnp.float32)
    counts = kept_ref[run].astype(jnp.float32)
    return (counts * pl.reciprocal(product, approx=True)).astype(jnp.bfloat16)


def runs_of(genes, wanted=1024):
    size = piece(genes, wanted)
    return [slice(at, at + size) for at in range(0, genes, size)]


def numerator(gene_ref, run, ratio):
    return jnp.dot(gene_ref[:, run], ratio, preferred_element_type=jnp.float32)


def partner(tile, tiles, offset):
    other = jnp.where((tile + offset) % 2 == 0, tile + 1, tile - 1)
    return jnp.where((other >= 0) & (other < tiles), other, -1)


def pick_kernel(neigh_ref, pick_ref):
    width = neigh_ref.shape[1]
    tiles = lax.axis_size("tile")
    here = lax.axis_index("tile")
    neigh = neigh_ref[...] - here * width
    neigh = jnp.concatenate([outer_of(neigh), inner_of(neigh)], axis=1)

    def found(where):
        total = jnp.zeros((LANES, width), jnp.float32)
        for j in range(neigh.shape[0]):
            total += (neigh[j : j + 1] == where).astype(jnp.float32)
        return total

    row = lax.broadcasted_iota(jnp.int32, (LANES, width), 0)
    for at in range(0, width, LANES):
        pick_ref[at : at + LANES] = found(at + row).astype(jnp.bfloat16)
    slot = row % (2 * BORDER)
    beside = jnp.where(
        row < 2 * BORDER, partner(here, tiles, 0), partner(here, tiles, 1)
    )
    where = (beside - here) * width + slot + jnp.where(slot < BORDER, 0, width - 2 * BORDER)
    pick_ref[width:] = jnp.where(beside < 0, 0.0, found(where)).astype(jnp.bfloat16)


def turn_kernel(counts_ref, outer_ref, inner_ref, landed, sems):
    width, genes = landed.shape
    side = quarter(width)
    copies = []
    for i in range(genes // COPY_COLUMNS):
        columns = pl.ds(i * COPY_COLUMNS, COPY_COLUMNS)
        copies.append(
            pltpu.make_async_copy(
                counts_ref.at[:, columns], landed.at[:, columns], sems.at[i]
            )
        )
    for copy in copies:
        copy.start()
    for i, copy in enumerate(copies):
        copy.wait()
        run = slice(i * COPY_COLUMNS, (i + 1) * COPY_COLUMNS)
        ends = jnp.concatenate([landed[:side, run], landed[width - side :, run]], axis=0)
        outer_ref[run] = ends.astype(jnp.float32).T.astype(jnp.bfloat16)
        middle = landed[side : width - side, run]
        inner_ref[run] = middle.astype(jnp.float32).T.astype(jnp.bfloat16)


def first_kernel(outer_ref, inner_ref, cells_ref, gene_ref, part_ref, rows_ref):
    rank, genes = gene_ref.shape
    width = cells_ref.shape[1]
    cells = cells_ref[...]
    cells = jnp.concatenate([outer_of(cells), inner_of(cells)], axis=1)
    factor_rows = jnp.concatenate(split(cells), axis=0)
    gsum = jnp.zeros((rank, 1), jnp.float32)
    total = jnp.zeros((rank, width), jnp.float32)
    for run in runs_of(genes):
        wide = gene_ref[:, run].astype(jnp.float32)
        gsum += jnp.sum(wide, axis=1, keepdims=True)
        rows = jnp.concatenate([wide, wide], axis=0).T.astype(jnp.bfloat16)
        rows_ref[run] = rows
        product = jnp.dot(rows, factor_rows, preferred_element_type=jnp.float32)
        counts = jnp.concatenate([outer_ref[run], inner_ref[run]], axis=1)
        ratio = counts.astype(jnp.float32) * pl.reciprocal(product, approx=True)
        total += numerator(gene_ref, run, ratio.astype(jnp.bfloat16))
    part_ref[:, :width] = whole_of(total[:, : width // 2], total[:, width // 2 :])
    part_ref[:, width:] = jnp.broadcast_to(gsum, (rank, LANES))


def masked_rows(values, flags):
    flag_rows = jnp.broadcast_to(flags.astype(jnp.float32), (ROWS, flags.shape[1]))
    return jnp.concatenate([jnp.where(flags, values, 0.0), flag_rows], axis=0)


def update_kernel(numer_ref, other_ref, gsum_ref, cells_ref, tissue_ref, updated_ref, edges_ref):
    width = cells_ref.shape[1]
    flags = tissue_ref[...] > 0
    numer = numer_ref[...] + other_ref[...]
    cells = cells_ref[...]
    updated = jnp.where(flags, cells * numer / gsum_ref[:, :1], cells)
    updated_ref[...] = updated
    both = masked_rows(updated, flags)
    edges_ref[:, :BORDER] = both[:, :BORDER]
    edges_ref[:, BORDER : 2 * BORDER] = both[:, width - BORDER :]
    edges_ref[:, 2 * BORDER :] = jnp.zeros_like(edges_ref[:, 2 * BORDER :])


def first_update_kernel(
    part_ref, other_ref, cells_ref, tissue_ref, _, updated_ref, edges_ref, gsum_ref
):
    width = cells_ref.shape[1]
    gsum_ref[...] = part_ref[:, width:] + other_ref[:, width:]
    update_kernel(
        part_ref.at[:, :width], other_ref.at[:, :width], gsum_ref,
        cells_ref, tissue_ref, updated_ref, edges_ref,
    )


def mixed(updated, flags, near):
    rank = updated.shape[0]
    mean = near[:rank] / jnp.maximum(near[rank : rank + 1], 1.0)
    return jnp.where(
        flags, (1.0 - smooth_weight) * updated + smooth_weight * mean, updated
    )


def picked(values, pick):
    return sum(
        jnp.dot(part, pick, preferred_element_type=jnp.float32) for part in split(values)
    )


def smoothed_inner(updated_ref, tissue_ref, pick_ref):
    updated, tissue = updated_ref[...], tissue_ref[...]
    width = updated.shape[1]
    near = picked(masked_rows(updated, tissue > 0), pick_ref[:width, width // 2 :])
    flags = inner_of(tissue) > 0
    return mixed(inner_of(updated), flags, near), flags


def smoothed_outer(updated_ref, tissue_ref, pick_ref, first_ref, second_ref):
    updated, tissue = updated_ref[...], tissue_ref[...]
    width = updated.shape[1]
    sides = jnp.concatenate(
        [first_ref[:, : 2 * BORDER], second_ref[:, : 2 * BORDER]], axis=1
    )
    near = picked(masked_rows(updated, tissue > 0), pick_ref[:width, : width // 2])
    near += picked(sides, pick_ref[width:, : width // 2])
    flags = outer_of(tissue) > 0
    return mixed(outer_of(updated), flags, near), flags


def inner_kernel(
    updated_ref, tissue_ref, pick_ref, kept_ref, rows_ref, gene_ref, cells_ref, numer_ref
):
    cells, _ = smoothed_inner(updated_ref, tissue_ref, pick_ref)
    cells_ref[...] = cells
    numer_ref[...] = sum(
        numerator(gene_ref, run, ratio_of(kept_ref, run, rows_ref[run], cells))
        for run in runs_of(gene_ref.shape[1], 2048)
    )


def outer_kernel(
    updated_ref, tissue_ref, pick_ref, first_ref, second_ref, kept_ref, rows_ref,
    gene_ref, inner_cells_ref, inner_numer_ref, cells_ref, numer_ref,
):
    cells, _ = smoothed_outer(updated_ref, tissue_ref, pick_ref, first_ref, second_ref)
    cells_ref[...] = whole_of(cells, inner_cells_ref[...])
    numer = sum(
        numerator(gene_ref, run, ratio_of(kept_ref, run, rows_ref[run], cells))
        for run in runs_of(gene_ref.shape[1], 2048)
    )
    numer_ref[...] = whole_of(numer, inner_numer_ref[...])


def exponent(values):
    return jnp.ceil(jnp.log2(jnp.maximum(values, 1e-30)))


def share_height(columns):
    blocks = columns // LANES
    return (blocks + blocks % 2) * ROWS + STAT_ROWS


def encode(values, hden, targets):
    power = exponent(jnp.max(values, axis=1, keepdims=True))
    coded = (values * (jnp.exp2(-power) * FULL) + 0.5).astype(jnp.int32)
    hden_power = exponent(hden)
    scaled = hden * jnp.exp2(-hden_power) * FULL
    high = jnp.floor(scaled)
    low = jnp.floor((scaled - high) * FULL)
    lane = lax.broadcasted_iota(jnp.int32, (values.shape[0], LANES), 1)
    marks = jnp.zeros((values.shape[0], LANES), jnp.float32)
    for at, value in enumerate((power, hden_power, high, low)):
        marks = jnp.where(lane == at, value, marks)
    marks = marks.astype(jnp.int32)
    blank = jnp.zeros((ROWS, LANES), jnp.int32)
    for group, target in enumerate(targets):
        ranks = slice(group * ROWS, (group + 1) * ROWS)
        blocks = [coded[ranks, at : at + LANES] for at in range(0, values.shape[1], LANES)]
        blocks += [blank] * (len(blocks) % 2) + [marks[ranks], blank]
        for i in range(0, len(blocks), 2):
            target[i * ROWS : (i + 2) * ROWS] = jnp.concatenate(
                blocks[i : i + 2], axis=0
            ).astype(jnp.int16)


def decode(source, columns):
    def number(start):
        return source[start : start + 2 * ROWS].astype(jnp.int32).astype(jnp.float32)

    height = source.shape[0]
    marks = number(height - STAT_ROWS)[:ROWS]
    scale = jnp.exp2(marks[:, :1]) / FULL
    hden = (marks[:, 2:3] + marks[:, 3:4] / FULL) * (jnp.exp2(marks[:, 1:2]) / FULL)
    blocks = []
    for start in range(0, height - STAT_ROWS, 2 * ROWS):
        both = number(start)
        blocks += [both[:ROWS] * scale, both[ROWS:] * scale]
    return jnp.concatenate(blocks[: columns // LANES], axis=1), hden


def gene_totals(cells, flags, kept_ref, rows_ref, totals_ref, others_ref=None):
    def put(columns, values):
        if others_ref is not None:
            values += others_ref[:, columns]
        totals_ref[:, columns] = values

    rank = cells.shape[0]
    genes = totals_ref.shape[1] - LANES
    masked = jnp.where(flags, cells, 0.0)
    parts = jnp.concatenate(split(masked), axis=0)
    columns = parts.astype(jnp.float32).T.astype(jnp.bfloat16)
    hden = jnp.sum(masked, axis=1, keepdims=True)
    put(slice(genes, genes + LANES), jnp.broadcast_to(hden, (rank, LANES)))
    for run in runs_of(genes, 1024):
        ratio = ratio_of(kept_ref, run, rows_ref[run], cells)
        total = jnp.dot(ratio, columns, preferred_element_type=jnp.float32).T
        put(run, total[:rank] + total[rank:])


def inner_totals_kernel(
    updated_ref, tissue_ref, pick_ref, kept_ref, rows_ref, cells_ref, totals_ref
):
    cells, flags = smoothed_inner(updated_ref, tissue_ref, pick_ref)
    cells_ref[...] = cells
    gene_totals(cells, flags, kept_ref, rows_ref, totals_ref)


def last_pass(
    updated_ref, tissue_ref, pick_ref, first_ref, second_ref, kept_ref, rows_ref,
    inner_cells_ref, inner_totals_ref, cells_ref, totals_ref,
):
    cells, flags = smoothed_outer(updated_ref, tissue_ref, pick_ref, first_ref, second_ref)
    cells_ref[...] = whole_of(cells, inner_cells_ref[...])
    gene_totals(cells, flags, kept_ref, rows_ref, totals_ref, inner_totals_ref)


def encode_tiles(totals_ref, sent_ref):
    rank, genes = totals_ref.shape[0], totals_ref.shape[1] - LANES
    tiles = sent_ref.shape[0]
    across = tiles * ROWS // rank
    columns = genes // across
    for column in range(across):
        encode(
            totals_ref[:, column * columns : (column + 1) * columns],
            totals_ref[:, genes : genes + 1],
            [sent_ref.at[tile] for tile in range(column, tiles, across)],
        )


def shares_kernel(*refs):
    *passed, sent_ref, totals_ref = refs
    last_pass(*passed, totals_ref)
    encode_tiles(totals_ref, sent_ref)


def distance_kernel(*refs):
    passed, (*sent_refs, own_ref, totals_ref, coded_ref) = refs[:10], refs[10:]
    last_pass(*passed, totals_ref)
    tiles, height, _ = coded_ref.shape
    encode_tiles(totals_ref, coded_ref)
    tile = lax.axis_index("tile")
    for distance in range(tiles // 2):
        there = tile ^ (2 * distance)
        own_ref[distance * height : (distance + 1) * height] = coded_ref[there]
        sent_refs[distance][...] = coded_ref[there ^ 1]


def column_kernel(distance, columns, got_ref, own_ref, *refs):
    sent_ref = refs[-1]
    height = sent_ref.shape[0]
    values, hden = decode(got_ref, columns)
    start = height * distance
    more, more_hden = decode(own_ref.at[start : start + height], columns)
    encode(values + more, hden + more_hden, [sent_ref])


def fresh_of(hnum, hden, gene_ref, across):
    columns = hnum.shape[1]
    here = lax.axis_index("tile")
    place = pl.multiple_of(lax.rem(here, across) * columns, LANES)
    every = gene_ref[:, pl.ds(place, columns)].astype(jnp.float32)
    hf = every[:ROWS]
    for group in range(1, gene_ref.shape[0] // ROWS):
        hf = jnp.where(here // across == group, every[group * ROWS : (group + 1) * ROWS], hf)
    return (hf * hnum / hden).astype(jnp.bfloat16)


def all_shares_kernel(got_ref, gene_ref, fresh_ref):
    tiles, _, columns = fresh_ref.shape
    hnum, hden = decode(got_ref.at[0], columns)
    for tile in range(1, tiles):
        more, more_hden = decode(got_ref.at[tile], columns)
        hnum += more
        hden += more_hden
    fresh = fresh_of(hnum, hden, gene_ref, tiles * ROWS // gene_ref.shape[0])
    for tile in range(tiles):
        fresh_ref[tile] = fresh


def fresh_kernel(*refs):
    *got_refs, gene_ref, fresh_ref = refs
    hnum, hden = 0.0, 0.0
    for ref in got_refs:
        more, more_hden = decode(ref, fresh_ref.shape[1])
        hnum += more
        hden += more_hden
    fresh_ref[...] = fresh_of(hnum, hden, gene_ref, 2)


def spread_kernel(*refs):
    *share_refs, cells_ref, new_cells_ref, out_ref = refs
    new_cells_ref[...] = cells_ref[...]
    groups = len(share_refs) // 2
    columns = share_refs[0].shape[1]
    tile = lax.axis_index("tile")
    here, side = tile // 2, lax.rem(tile, 2)
    shares = [ref[...].astype(jnp.float32) for ref in share_refs]
    for some, column in ((shares[:groups], side), (shares[groups:], 1 - side)):
        picked = []
        for group in range(groups):
            share = some[0]
            for at in range(1, groups):
                share = jnp.where(here ^ group == at, some[at], share)
            picked.append(share)
        place = pl.ds(pl.multiple_of(column * columns, LANES), columns)
        for group in range(0, groups, 2):
            out_ref[group * ROWS : (group + 2) * ROWS, place] = jnp.concatenate(
                picked[group : group + 2], axis=0
            ).astype(jnp.bfloat16)


def call(kernel, outs, scratch=(), specs=None, limit=VMEM_BYTES):
    whole = pl.BlockSpec(memory_space=pltpu.VMEM)
    return lambda *args: pl.pallas_call(
        kernel,
        out_shape=outs,
        in_specs=specs or [whole] * len(args),
        out_specs=jax.tree.map(lambda _: whole, outs),
        scratch_shapes=list(scratch),
        compiler_params=pltpu.CompilerParams(vmem_limit_bytes=limit),
    )(*args)


def beside(tiles, halves, offset):
    pairs = []
    paired = set()
    for low in range(offset, tiles - 1, 2):
        paired |= {low, low + 1}
        for gene in range(halves):
            other = (gene + 1) % halves
            pairs.append((low * halves + gene, (low + 1) * halves + other))
            pairs.append(((low + 1) * halves + gene, low * halves + other))
    for tile in range(tiles):
        if tile not in paired:
            for gene in range(halves):
                pairs.append((tile * halves + gene, tile * halves + (gene + 1) % halves))
    return pairs


def on_device(counts, cell_factor, gene_factor, tissue, neighbours):
    rank, width = cell_factor.shape
    genes = gene_factor.shape[1]
    tiles, halves = lax.axis_size("tile"), lax.axis_size("gene")
    flag_row = tissue[None]
    shape = jax.ShapeDtypeStruct
    factor = shape((rank, width), jnp.float32)
    edge = shape((rank + ROWS, LANES), jnp.float32)
    half = shape((rank, width // 2), jnp.float32)
    half_kept = shape((genes, width // 2), jnp.bfloat16)
    gene_rows = shape((genes, 2 * rank), jnp.bfloat16)
    far = pl.BlockSpec(memory_space=pl.ANY)
    near = pl.BlockSpec(memory_space=pltpu.VMEM)

    outer, inner = call(
        turn_kernel,
        (half_kept, half_kept),
        [
            pltpu.VMEM(counts.shape, counts.dtype),
            pltpu.SemaphoreType.DMA((genes // COPY_COLUMNS,)),
        ],
        [far],
        COUNTS_VMEM_BYTES,
    )(counts)
    part, rows = call(
        first_kernel, (shape((rank, width + LANES), jnp.float32), gene_rows)
    )(outer, inner, cell_factor, gene_factor)
    pick = call(pick_kernel, shape((width + LANES, width), jnp.bfloat16))(neighbours)

    def swapped(part):
        if halves == 2:
            return lax.ppermute(part, "gene", [(0, 1), (1, 0)])
        return lax.psum(part, "gene") - part

    def around(edges):
        return [
            lax.ppermute(edges, ("tile", "gene"), beside(tiles, halves, offset))
            for offset in (0, 1)
        ]

    updated, edges, gsum = call(
        first_update_kernel,
        (factor, edge, shape((rank, LANES), jnp.float32)),
        specs=[near] * 4 + [far],
    )(part, swapped(part), cell_factor, flag_row, pick)
    inner_of_both = call(inner_kernel, (half, half))(
        updated, flag_row, pick, inner, rows, gene_factor
    )
    cells, numer = call(outer_kernel, (factor, factor))(
        updated, flag_row, pick, *around(edges), outer, rows, gene_factor, *inner_of_both
    )
    updated, edges = call(update_kernel, (factor, edge))(
        numer, swapped(numer), gsum, cells, flag_row
    )
    across = tiles * ROWS // rank
    groups = rank // ROWS
    columns = genes // across
    height = share_height(columns)
    inner_of_both = call(
        inner_totals_kernel, (half, shape((rank, genes + LANES), jnp.float32))
    )(updated, flag_row, pick, inner, rows)
    last = (updated, flag_row, pick, *around(edges), outer, rows, *inner_of_both)
    totals = [pltpu.VMEM((rank, genes + LANES), jnp.float32)]
    if across != 2 or groups != 4 or halves != 2:
        cells, sent = call(
            shares_kernel, (factor, shape((tiles, height, LANES), jnp.int16)), totals
        )(*last)
        got = lax.all_to_all(sent, "tile", 0, 0)
        fresh = call(all_shares_kernel, shape((tiles, ROWS, columns), jnp.bfloat16))(
            got, gene_factor
        )
        every = lax.all_to_all(fresh, "tile", 0, 0).reshape(groups, across, ROWS, columns)
        return cells, every.transpose(0, 2, 1, 3).reshape(rank, genes)

    def moved(array, step, cross):
        pairs = [
            (tile * halves + gene, (tile ^ step) * halves + (gene ^ cross))
            for tile in range(tiles)
            for gene in range(halves)
        ]
        return lax.ppermute(array, ("tile", "gene"), pairs)

    one = shape((height, LANES), jnp.int16)
    cells, *sent, own = call(
        distance_kernel,
        (
            factor,
            *[one] * groups,
            shape((groups * height, LANES), jnp.int16),
        ),
        totals + [pltpu.VMEM((tiles, height, LANES), jnp.int16)],
    )(*last)
    distances = range(groups - 1, 0, -1)
    own = moved(own, 0, 1)
    got = [moved(share, 1, 1) for share in sent]
    summed = []
    for distance in (*distances, 0):
        after = () if distance else summed[:1]
        both = call(
            functools.partial(column_kernel, distance, columns), one,
            specs=[near] * 2 + [far] * len(after),
        )(got[distance], own, *after)
        summed.append(moved(both, 2 * distance, 1))
    fresh = call(fresh_kernel, shape((ROWS, columns), jnp.bfloat16))(*summed, gene_factor)
    shares, others = [fresh], [moved(fresh, 1, 0)]
    passing = {distance: moved(fresh, 2 * distance, 1) for distance in distances}
    for distance in range(1, groups):
        shares.append(moved(passing[distance], 0, 1))
        others.append(moved(passing[distance], 1, 1))
    return call(spread_kernel, (factor, shape((rank, genes), jnp.bfloat16)))(
        *shares, *others, cells
    )


def solution(mesh):
    return jax.shard_map(
        on_device,
        mesh=mesh,
        in_specs=(
            P(("grp", "tile"), "gene"),
            P(None, ("grp", "tile")),
            P(None, ("grp", "gene")),
            P(("grp", "tile")),
            P(None, ("grp", "tile")),
        ),
        out_specs=(P(None, ("grp", "tile")), P(None, ("grp", "gene"))),
        check_vma=False,
    )
```
